32 devices in a mesh: gx: 4 (over x, core), gy: 4 (over z), gz: 2 (over y).
Axes of the slice: x: 2, y: 2, z: 4, core: 2. Of those that a mesh axis runs over, the one named last changes fastest.
Arguments:
- layer_input: bfloat16 [1024, 6144], P(('gx', 'gy'), 'gz'), may hold values from -70 to 70
- out_cotangent: bfloat16 [1024, 6144], P(('gx', 'gy'), 'gz'), may hold values from -6 to 6
- w_query: bfloat16 [6144, 6144], P(('gz', 'gx'), 'gy'), may hold values from -0.078125 to 0.078125
- w_key: bfloat16 [6144, 6144], P(('gz', 'gx'), 'gy'), may hold values from -0.078125 to 0.078125
- w_value: bfloat16 [6144, 6144], P(('gz', 'gx'), 'gy'), may hold values from -0.078125 to 0.078125
- w_mlp_in: bfloat16 [6144, 24576], P(('gz', 'gx'), 'gy'), may hold values from -0.078125 to 0.078125
- w_attn_out: bfloat16 [6144, 6144], P(('gy', 'gx'), 'gz'), may hold values from -0.078125 to 0.078125
- w_mlp_out: bfloat16 [24576, 6144], P(('gy', 'gx'), 'gz'), may hold values from -0.0390625 to 0.0390625
Outputs:
- layer_out: bfloat16 [1024, 6144], P(('gx', 'gy'), 'gz')
- input_grad: bfloat16 [1024, 6144], P(('gx', 'gy'), 'gz')
The draws below stay inside these ranges and needn't reach their ends.
All inputs are finite; a program needn't handle non-finite values.
Results may differ from the reference program's by a relative error of at most 0.01.
Values may be sent and summed in bfloat16 or wider, within the bound.
No kernel may reach another device: no remote copies, remote signals or barrier semaphores. Data moves between devices by JAX's collectives and lax.ppermute only.
A program may use at most 320 MiB of HBM per device.

```python
import math
import jax
import jax.numpy as jnp
from jax import lax

D = 6144
FF = 24576
HEADS = 48
HEAD_DIM = 128
IMG_TOK = 256
TOKENS = 1024
N_GZ = 2


def draw_layer_input(key, part):
    key = jax.random.fold_in(key, 11)
    first_key, second_key, third_key = jax.random.split(key, 3)
    position = jnp.arange(D, dtype=jnp.float32) / D
    column_jitter = jnp.power(10.0, jax.random.uniform(third_key, (1, D), jnp.float32, -0.5, 0.5))
    base = jax.random.truncated_normal(first_key, -4.0, 4.0, (TOKENS, D), jnp.float32)
    row_scale = jnp.exp(jax.random.uniform(second_key, (TOKENS, 1), jnp.float32, math.log(0.3), math.log(3.0)))
    column_scale = column_jitter * jnp.power(3.0, position - 0.5)[None, :]
    result = base * row_scale * column_scale
    return result.astype(jnp.bfloat16)


def levels(stream_key, shape, cuts, low, high):
    factor_of = 1.0
    for dim, parts in cuts:
        draws = jax.random.uniform(jax.random.fold_in(jax.random.fold_in(stream_key, 6), dim), (parts,), jnp.float32, low / len(cuts), high / len(cuts))
        factor_of = factor_of * jnp.repeat(jnp.exp(draws), shape[dim] // parts).reshape((-1,) + (1,) * (len(shape) - 1 - dim))
    return factor_of


def bell_draw(own_key, shape, scale, most, shards=(), kind=jnp.bfloat16):
    values = jax.random.normal(own_key, shape, jnp.float32) * scale
    if len(shards) > 0:
        values = levels(own_key, shape, shards, -0.22, 0.18) * values
    return jnp.clip(values, min=-most, max=most).astype(kind)


def setup_inputs(seed: int = 0) -> dict:
    streams_of = jax.random.split(jax.random.key(seed), 9)
    return {
        "layer_input": draw_layer_input(jax.random.fold_in(streams_of[8], 71), 0),
        "out_cotangent": bell_draw(streams_of[1], (TOKENS, D), 1.0, 6.0, ((0, 16), (1, 2))),
        "w_query": bell_draw(streams_of[2], (D, D), D ** -0.5, 0.078125, ((0, 8), (1, 4))),
        "w_key": bell_draw(streams_of[3], (D, D), D ** -0.5, 0.078125, ((0, 8), (1, 4))),
        "w_value": bell_draw(streams_of[4], (D, D), D ** -0.5, 0.078125, ((0, 8), (1, 4))),
        "w_mlp_in": bell_draw(streams_of[5], (D, FF), D ** -0.5, 0.078125, ((0, 8), (1, 4))),
        "w_attn_out": bell_draw(streams_of[6], (D, D), D ** -0.5, 0.078125, ((0, 16), (1, 2))),
        "w_mlp_out": bell_draw(streams_of[7], (FF, D), FF ** -0.5, 0.0390625, ((0, 16), (1, 2))),
    }


EPSILON = 1e-06
ROOT_HALF = 0.7071067811865476
ROOT_TWO_PI_INV = 0.3989422804014327

def round_half(values):
    return lax.optimization_barrier(values.astype(jnp.bfloat16)).astype(jnp.float32)

def head_norm(values):
    center = values - lax.optimization_barrier(jnp.mean(values, axis=-1, keepdims=True))
    spread = lax.optimization_barrier(jnp.mean(center * center, axis=-1, keepdims=True))
    return center * lax.rsqrt(spread + EPSILON)

def attend(query, keys, values):
    q_norm = round_half(head_norm(query))
    k_norm = round_half(head_norm(keys))
    v_half = round_half(values)
    scale = 1.0 / math.sqrt(query.shape[-1])
    scores = jnp.einsum('bqhd,bkhd->bhqk', q_norm, k_norm) * scale
    weights = jnp.exp(scores)
    probs = weights / lax.optimization_barrier(jnp.sum(weights, axis=-1, keepdims=True))
    probs_half = round_half(probs)
    mixed = jnp.einsum('bhqk,bkhd->bqhd', probs_half, v_half)
    return mixed.astype(jnp.bfloat16)

def gelu(pre):
    return pre * 0.5 * (1.0 + lax.erf(pre * ROOT_HALF))

def gelu_back(pre, grad_half):
    cdf = 0.5 * (1.0 + lax.erf(pre * ROOT_HALF))
    pdf = jnp.exp(-0.5 * pre * pre) * ROOT_TWO_PI_INV
    return (grad_half.astype(jnp.float32) * (cdf + pre * pdf)).astype(jnp.bfloat16)

def depth_sum(left, right):
    width = left.shape[1] // N_GZ
    total = jnp.zeros((left.shape[0], right.shape[1]), jnp.float32)
    for index in range(N_GZ):
        part = jnp.dot(left[:, index * width:(index + 1) * width], right[index * width:(index + 1) * width], preferred_element_type=jnp.float32)
        total = total + round_half(part)
    return total

def reference(layer_input, out_cotangent, w_query, w_key, w_value, w_mlp_in, w_attn_out, w_mlp_out):
    wide = layer_input.astype(jnp.float32)
    center = lax.optimization_barrier(jnp.sum(wide, axis=1)) / D
    spread = lax.optimization_barrier(jnp.sum(wide * wide, axis=1)) / D - center * center
    inverse = lax.rsqrt(spread + EPSILON)
    normed = (wide - center[:, None]) * inverse[:, None]
    normed_half = normed.astype(jnp.bfloat16)
    query = depth_sum(normed_half, w_query)
    keys = depth_sum(normed_half, w_key)
    values = depth_sum(normed_half, w_value)
    hidden_pre = depth_sum(normed_half, w_mlp_in)
    images = TOKENS // IMG_TOK

    def split_heads(block):
        return block.reshape(images, IMG_TOK, HEADS, HEAD_DIM)
    mixed, attend_back = jax.vjp(attend, split_heads(query), split_heads(keys), split_heads(values))
    mixed_rows = mixed.reshape(TOKENS, D)
    activated = gelu(hidden_pre).astype(jnp.bfloat16)
    summed = jnp.dot(mixed_rows, w_attn_out, preferred_element_type=jnp.float32) + jnp.dot(activated, w_mlp_out, preferred_element_type=jnp.float32)
    layer_out = (wide + summed).astype(jnp.bfloat16)
    mixed_grad = depth_sum(out_cotangent, w_attn_out.T).astype(jnp.bfloat16)
    act_grad = depth_sum(out_cotangent, w_mlp_out.T).astype(jnp.bfloat16)
    query_grad, key_grad, value_grad = attend_back(split_heads(mixed_grad))
    query_half = query_grad.reshape(TOKENS, D).astype(jnp.bfloat16)
    key_half = key_grad.reshape(TOKENS, D).astype(jnp.bfloat16)
    value_half = value_grad.reshape(TOKENS, D).astype(jnp.bfloat16)
    hidden_grad = gelu_back(hidden_pre, act_grad)
    normed_grad = jnp.dot(query_half, w_query.T, preferred_element_type=jnp.float32)
    normed_grad = normed_grad + jnp.dot(key_half, w_key.T, preferred_element_type=jnp.float32)
    normed_grad = normed_grad + jnp.dot(value_half, w_value.T, preferred_element_type=jnp.float32)
    normed_grad = normed_grad + jnp.dot(hidden_grad, w_mlp_in.T, preferred_element_type=jnp.float32)
    first = lax.optimization_barrier(jnp.sum(normed_grad, axis=1)) / D
    second = lax.optimization_barrier(jnp.sum(normed_grad * normed, axis=1)) / D
    grad_full = out_cotangent.astype(jnp.float32) + inverse[:, None] * (normed_grad - first[:, None] - normed * second[:, None])
    return (layer_out, grad_full.astype(jnp.bfloat16))
```

```python
import math

import jax
import jax.numpy as jnp
from jax import lax
from jax.sharding import PartitionSpec as P

D = 6144
HEAD_DIM = 128
IMG_TOK = 256


EPSILON = 1e-06
ROOT_HALF = 0.7071067811865476
ROOT_TWO_PI_INV = 0.3989422804014327


def head_norm(values):
    center = values - jnp.mean(values, axis=-1, keepdims=True)
    spread = jnp.mean(center * center, axis=-1, keepdims=True)
    return center * lax.rsqrt(spread + EPSILON)


def attend(query, keys, values):
    q_norm = head_norm(query).astype(jnp.bfloat16)
    k_norm = head_norm(keys).astype(jnp.bfloat16)
    v_half = values.astype(jnp.bfloat16)
    scale = 1.0 / math.sqrt(query.shape[-1])
    scores = (
        jnp.einsum("bqhd,bkhd->bhqk", q_norm, k_norm, preferred_element_type=jnp.float32) * scale
    )
    weights = jnp.exp(scores)
    probs = weights / jnp.sum(weights, axis=-1, keepdims=True)
    probs_half = probs.astype(jnp.bfloat16)
    mixed = jnp.einsum("bhqk,bkhd->bqhd", probs_half, v_half, preferred_element_type=jnp.float32)
    return mixed.astype(jnp.bfloat16)


def gelu(pre):
    return pre * 0.5 * (1.0 + lax.erf(pre * ROOT_HALF))


def gelu_back(pre, grad_half):
    cdf = 0.5 * (1.0 + lax.erf(pre * ROOT_HALF))
    pdf = jnp.exp(-0.5 * pre * pre) * ROOT_TWO_PI_INV
    return (grad_half.astype(jnp.float32) * (cdf + pre * pdf)).astype(jnp.bfloat16)


def dot(left, right):
    return jnp.dot(left, right, preferred_element_type=jnp.float32)


def back_dot(left, right):
    return lax.dot_general(
        left, right, (((1,), (1,)), ((), ())), preferred_element_type=jnp.float32
    )


def body(layer_input, out_cotangent, w_query, w_key, w_value, w_mlp_in, w_attn_out, w_mlp_out):
    n_gx, n_gy, n_gz = (lax.axis_size(name) for name in ("gx", "gy", "gz"))
    tokens = layer_input.shape[0] * n_gx * n_gy
    paired = n_gz == 2 and tokens % (2 * IMG_TOK) == 0
    kept = tokens // 2 if paired else tokens
    me_z = lax.axis_index("gz")
    swap_z = [(0, 1), (1, 0)]

    def halves(block):
        if not paired:
            return block, None
        mine = lax.dynamic_slice_in_dim(block, me_z * kept, kept, 0)
        other = lax.dynamic_slice_in_dim(block, (1 - me_z) * kept, kept, 0)
        return mine, other

    def sum_gz(term, mine, other):
        if not paired:
            return lax.psum(term(mine).astype(jnp.bfloat16), "gz").astype(jnp.float32)
        got = lax.ppermute(term(other).astype(jnp.bfloat16), "gz", swap_z)
        return term(mine) + got.astype(jnp.float32)

    def from_pair(block):
        return lax.ppermute(block, "gz", swap_z)

    def spread_rows(mine, other):
        if paired:
            first = jnp.where(me_z == 0, mine, other)
            second = jnp.where(me_z == 0, other, mine)
            mine = jnp.concatenate([first, second], axis=0)
        return lax.psum_scatter(
            mine, ("gx", "gy"), scatter_dimension=0, tiled=True
        ).astype(jnp.float32)

    def columns_of(weight):
        return lax.all_to_all(weight, "gx", split_axis=1, concat_axis=0, tiled=True)

    wide = layer_input.astype(jnp.float32)
    total, squares = lax.psum((jnp.sum(wide, axis=1), jnp.sum(wide * wide, axis=1)), "gz")
    center = total / D
    spread = squares / D - center * center
    inverse = lax.rsqrt(spread + EPSILON)
    normed = (wide - center[:, None]) * inverse[:, None]
    gathered_in = lax.all_gather(normed.astype(jnp.bfloat16), ("gx", "gy"), axis=0, tiled=True)
    gathered_cot = lax.all_gather(out_cotangent, ("gx", "gy"), axis=0, tiled=True)
    in_mine, in_other = halves(gathered_in)
    cot_mine, cot_other = halves(gathered_cot)

    rows_query, rows_key, rows_value = columns_of(w_query), columns_of(w_key), columns_of(w_value)
    rows_mlp_in = columns_of(w_mlp_in)

    def project(weight):
        return sum_gz(lambda rows: dot(rows, weight), in_mine, in_other)

    def project_back(weight):
        return sum_gz(lambda rows: back_dot(rows, weight), cot_mine, cot_other).astype(jnp.bfloat16)

    mixed_grad, act_grad = project_back(w_attn_out), project_back(w_mlp_out)
    query, keys, values = project(rows_query), project(rows_key), project(rows_value)
    heads_here = query.shape[1] // HEAD_DIM

    def split_heads(block):
        return block.reshape(kept // IMG_TOK, IMG_TOK, heads_here, HEAD_DIM)

    mixed, attend_back = jax.vjp(attend, split_heads(query), split_heads(keys), split_heads(values))
    mixed_rows = mixed.reshape(kept, query.shape[1])
    query_grad, key_grad, value_grad = attend_back(split_heads(mixed_grad))
    query_half = query_grad.reshape(kept, -1).astype(jnp.bfloat16)
    key_half = key_grad.reshape(kept, -1).astype(jnp.bfloat16)
    value_half = value_grad.reshape(kept, -1).astype(jnp.bfloat16)

    hidden_pre = project(rows_mlp_in)
    activated = gelu(hidden_pre).astype(jnp.bfloat16)
    hidden_grad = gelu_back(hidden_pre, act_grad)

    def forward_term(mixed_part, act_part):
        return (dot(mixed_part, w_attn_out) + dot(act_part, w_mlp_out)).astype(jnp.bfloat16)

    def backward_term(query_part, key_part, value_part, hidden_part):
        result = back_dot(query_part, rows_query)
        result = result + back_dot(key_part, rows_key)
        result = result + back_dot(value_part, rows_value)
        return (result + back_dot(hidden_part, rows_mlp_in)).astype(jnp.bfloat16)

    forward_in = (mixed_rows, activated)
    backward_in = (query_half, key_half, value_half, hidden_grad)
    forward_mine = forward_term(*forward_in)
    backward_mine = backward_term(*backward_in)
    forward_other = backward_other = None
    if paired:
        forward_other = forward_term(*(from_pair(part) for part in forward_in))
        backward_other = backward_term(*(from_pair(part) for part in backward_in))
    summed = spread_rows(forward_mine, forward_other)
    layer_out = (wide + summed).astype(jnp.bfloat16)
    normed_grad = spread_rows(backward_mine, backward_other)
    first, second = lax.psum(
        (jnp.sum(normed_grad, axis=1), jnp.sum(normed_grad * normed, axis=1)), "gz"
    )
    grad_full = out_cotangent.astype(jnp.float32) + inverse[:, None] * (
        normed_grad - (first / D)[:, None] - normed * (second / D)[:, None]
    )
    return (layer_out, grad_full.astype(jnp.bfloat16))


def solution(mesh):
    in_specs = (
        P(("gx", "gy"), "gz"),
        P(("gx", "gy"), "gz"),
        P(("gz", "gx"), "gy"),
        P(("gz", "gx"), "gy"),
        P(("gz", "gx"), "gy"),
        P(("gz", "gx"), "gy"),
        P(("gy", "gx"), "gz"),
        P(("gy", "gx"), "gz"),
    )
    out_specs = (P(("gx", "gy"), "gz"), P(("gx", "gy"), "gz"))
    return jax.shard_map(body, mesh=mesh, in_specs=in_specs, out_specs=out_specs, check_vma=False)
```

```python
import functools
import math

import jax
import jax.numpy as jnp
from jax import lax
from jax.experimental import pallas as pl
from jax.experimental.pallas import tpu as pltpu
from jax.sharding import PartitionSpec as P

D = 6144
HEAD_DIM = 128
IMG_TOK = 256


EPSILON = 1e-06
ROOT_HALF = 0.7071067811865476
ROOT_TWO_PI_INV = 0.3989422804014327


def attend_kernel(
    q_own, q_got, k_own, k_got, v_own, v_got, g_own, g_got, mixed_ref, dq_ref, dk_ref, dv_ref, *, scale
):
    def total(own, got):
        return own[...].astype(jnp.float32) + got[...].astype(jnp.float32)

    def norm(values):
        center = values - jnp.mean(values, axis=-1, keepdims=True)
        spread = jnp.mean(center * center, axis=-1, keepdims=True)
        inverse = lax.rsqrt(spread + EPSILON)
        return center * inverse, inverse

    def norm_back(grad, normed, inverse):
        slope = inverse * (grad - normed * jnp.mean(grad * normed, axis=-1, keepdims=True))
        return (slope - jnp.mean(slope, axis=-1, keepdims=True)).astype(jnp.bfloat16)

    def contract(left, right, left_dim, right_dim):
        return lax.dot_general(
            left,
            right,
            (((left_dim,), (right_dim,)), ((), ())),
            preferred_element_type=jnp.float32,
        )

    def half(values):
        return values.astype(jnp.bfloat16)

    q_norm, q_inverse = norm(total(q_own, q_got))
    k_norm, k_inverse = norm(total(k_own, k_got))
    q_half, k_half = half(q_norm), half(k_norm)
    v_half = half(total(v_own, v_got))
    grad = half(total(g_own, g_got))
    weights = jnp.exp(contract(q_half, k_half, 1, 1) * scale)
    probs = weights / jnp.sum(weights, axis=-1, keepdims=True)
    probs_half = half(probs)
    mixed_ref[...] = half(contract(probs_half, v_half, 1, 0))
    dv_ref[...] = half(contract(probs_half, grad, 0, 0))
    probs_grad = half(contract(grad, v_half, 1, 1)).astype(jnp.float32)
    inner = jnp.sum(probs_grad * probs, axis=-1, keepdims=True)
    score_grad = half(probs * (probs_grad - inner) * scale)
    q_grad = half(contract(score_grad, k_half, 1, 0)).astype(jnp.float32)
    k_grad = half(contract(score_grad, q_half, 0, 0)).astype(jnp.float32)
    dq_ref[...] = norm_back(q_grad, q_norm, q_inverse)
    dk_ref[...] = norm_back(k_grad, k_norm, k_inverse)


def attend(own, got, grad_own, grad_got):
    rows, width = grad_own.shape
    heads = width // HEAD_DIM

    def block(part):
        return pl.BlockSpec((IMG_TOK, HEAD_DIM), lambda image, head: (image, part * heads + head))

    half = jax.ShapeDtypeStruct((rows, width), jnp.bfloat16)
    return pl.pallas_call(
        functools.partial(attend_kernel, scale=1.0 / math.sqrt(HEAD_DIM)),
        grid=(rows // IMG_TOK, heads),
        in_specs=[block(0), block(0), block(1), block(1), block(2), block(2), block(0), block(0)],
        out_specs=[block(0)] * 4,
        out_shape=[half] * 4,
        compiler_params=pltpu.CompilerParams(vmem_limit_bytes=32 * 1024 * 1024),
        cost_estimate=pl.CostEstimate(
            flops=12 * rows * IMG_TOK * width,
            bytes_accessed=24 * rows * width,
            transcendentals=rows * IMG_TOK * heads,
        ),
        name="attend",
    )(own, got, own, got, own, got, grad_own, grad_got)


def gelu(pre):
    return pre * 0.5 * (1.0 + lax.erf(pre * ROOT_HALF))


def gelu_back(pre, grad_half):
    cdf = 0.5 * (1.0 + lax.erf(pre * ROOT_HALF))
    pdf = jnp.exp(-0.5 * pre * pre) * ROOT_TWO_PI_INV
    return (grad_half.astype(jnp.float32) * (cdf + pre * pdf)).astype(jnp.bfloat16)


def dot(left, right):
    return jnp.dot(left, right, preferred_element_type=jnp.float32)


def back_dot(left, right):
    return lax.dot_general(
        left, right, (((1,), (1,)), ((), ())), preferred_element_type=jnp.float32
    )


def half(values):
    return values.astype(jnp.bfloat16)


def wide_sum(own, got):
    return own.astype(jnp.float32) + got.astype(jnp.float32)


def trade(block, axis, bit):
    pairs = [(index, index ^ bit) for index in range(lax.axis_size(axis))]
    return lax.ppermute(block, axis, pairs)


def body(layer_input, out_cotangent, w_query, w_key, w_value, w_mlp_in, w_attn_out, w_mlp_out):
    n_gx, n_gy, n_gz = (lax.axis_size(name) for name in ("gx", "gy", "gz"))
    me_x, me_y = lax.axis_index("gx"), lax.axis_index("gy")
    own_rows = layer_input.shape[0]
    image_rows = own_rows * n_gy
    order = (3, 1, 2, 0)

    def all_rows(block):
        gathered = lax.all_gather(block, ("gx", "gy"), axis=0, tiled=True)
        return jnp.concatenate(
            [
                lax.dynamic_slice_in_dim(gathered, (me_x ^ bit) * image_rows, image_rows, 0)
                for bit in order
            ],
            axis=0,
        )

    def others(part):
        if n_gz == 2:
            return trade(part, "gz", 1)
        return half(lax.psum(part.astype(jnp.float32), "gz") - part.astype(jnp.float32))

    def by_owner(weight):
        rows, columns = weight.shape
        return weight.reshape(rows, n_gx, columns // n_gx).transpose(1, 0, 2)

    def swap(weight):
        swapped = lax.all_to_all(weight, "gx", split_axis=0, concat_axis=0, tiled=True)
        return swapped.reshape(n_gx * weight.shape[1], weight.shape[2])

    def after(value, earlier):
        return lax.optimization_barrier((value, earlier))

    wide = layer_input.astype(jnp.float32)
    total, squares = lax.psum((jnp.sum(wide, axis=1), jnp.sum(wide * wide, axis=1)), "gz")
    center = total / D
    spread = squares / D - center * center
    inverse = lax.rsqrt(spread + EPSILON)
    normed = (wide - center[:, None]) * inverse[:, None]
    gathered_in = all_rows(half(normed))

    heads_in = jnp.concatenate([by_owner(w) for w in (w_query, w_key, w_value)], axis=2)
    mlp_in = by_owner(w_mlp_in)
    cut = mlp_in.shape[2] // 2
    in_heads = swap(heads_in)
    first_mlp, in_heads = after(mlp_in[:, :, :cut], in_heads)
    in_first = swap(first_mlp)
    second_mlp, in_first = after(mlp_in[:, :, cut:], in_first)
    in_second = swap(second_mlp)

    heads_own = half(dot(gathered_in, in_heads))
    heads_got = others(heads_own)
    first_own = half(dot(gathered_in, in_first))
    first_got = others(first_own)

    gathered_cot = all_rows(out_cotangent)
    mixed_own = half(back_dot(gathered_cot, w_attn_out))
    mixed_got = others(mixed_own)
    second_own = half(dot(gathered_in, in_second))
    second_got = others(second_own)

    mixed, query_grad, key_grad, value_grad = attend(heads_own, heads_got, mixed_own, mixed_got)
    pre_first, pre_second = wide_sum(first_own, first_got), wide_sum(second_own, second_got)
    act_first, act_second = half(gelu(pre_first)), half(gelu(pre_second))
    heads_grad = jnp.concatenate([query_grad, key_grad, value_grad], axis=1)

    def block_of(value, start, count):
        return lax.slice_in_dim(value, start * image_rows, (start + count) * image_rows)

    def forward_term(start, count):
        result = dot(block_of(mixed, start, count), w_attn_out)
        result = result + dot(block_of(act_first, start, count), w_mlp_out[:cut])
        return result + dot(block_of(act_second, start, count), w_mlp_out[cut:])

    def backward_term(start, count):
        act_own = half(back_dot(block_of(gathered_cot, start, count), w_mlp_out))
        grad = half(wide_sum(act_own, others(act_own)))
        first = gelu_back(block_of(pre_first, start, count), grad[:, :cut])
        second = gelu_back(block_of(pre_second, start, count), grad[:, cut:])
        result = back_dot(block_of(heads_grad, start, count), in_heads)
        result = result + back_dot(first, in_first)
        return result + back_dot(second, in_second)

    def keep_and_send(value, sent_first):
        count = value.shape[0] // 2
        low, high = value[:count], value[count:]
        return jnp.where(sent_first, high, low), jnp.where(sent_first, low, high)

    def spread_rows(term):
        from_core = trade(half(term(0, 2)), "gx", 1)
        to_x = half(term(2, 1) + from_core[:image_rows].astype(jnp.float32))
        from_x = trade(to_x, "gx", 2)
        mine = wide_sum(from_core[image_rows:], from_x) + term(3, 1)
        quarters = mine.reshape(2, 2, own_rows, mine.shape[1])
        odd = me_y % 2 == 1
        kept = jnp.where(odd, quarters[:, 1], quarters[:, 0])
        sent = jnp.where(odd, quarters[:, 0], quarters[:, 1])
        pair = kept + trade(half(sent), "gy", 1).astype(jnp.float32)
        high = me_y >= 2
        kept = jnp.where(high, pair[1], pair[0])
        sent = jnp.where(high, pair[0], pair[1])
        return kept + trade(half(sent), "gy", 2).astype(jnp.float32)

    layer_out = half(wide + spread_rows(forward_term))
    normed_grad = spread_rows(backward_term)
    first, second = lax.psum(
        (jnp.sum(normed_grad, axis=1), jnp.sum(normed_grad * normed, axis=1)), "gz"
    )
    grad_full = out_cotangent.astype(jnp.float32) + inverse[:, None] * (
        normed_grad - (first / D)[:, None] - normed * (second / D)[:, None]
    )
    return (layer_out, half(grad_full))


def solution(mesh):
    in_specs = (
        P(("gx", "gy"), "gz"),
        P(("gx", "gy"), "gz"),
        P(("gz", "gx"), "gy"),
        P(("gz", "gx"), "gy"),
        P(("gz", "gx"), "gy"),
        P(("gz", "gx"), "gy"),
        P(("gy", "gx"), "gz"),
        P(("gy", "gx"), "gz"),
    )
    out_specs = (P(("gx", "gy"), "gz"), P(("gx", "gy"), "gz"))
    return jax.shard_map(body, mesh=mesh, in_specs=in_specs, out_specs=out_specs, check_vma=False)
```

```python
import functools
import math

import jax
import jax.numpy as jnp
from jax import lax
from jax.experimental import pallas as pl
from jax.experimental.pallas import tpu as pltpu
from jax.sharding import PartitionSpec as P

D = 6144
HEAD_DIM = 128
IMG_TOK = 256


EPSILON = 1e-06
ROOT_HALF = 0.7071067811865476
ROOT_TWO_PI_INV = 0.3989422804014327


def attend_kernel(
    q_own, q_got, k_own, k_got, v_own, v_got, g_own, g_got, mixed_ref, dq_ref, dk_ref, dv_ref, *, scale
):
    def total(own, got):
        return own[...].astype(jnp.float32) + got[...].astype(jnp.float32)

    def norm(values):
        center = values - jnp.mean(values, axis=-1, keepdims=True)
        spread = jnp.mean(center * center, axis=-1, keepdims=True)
        inverse = lax.rsqrt(spread + EPSILON)
        return center * inverse, inverse

    def norm_back(grad, normed, inverse):
        slope = inverse * (grad - normed * jnp.mean(grad * normed, axis=-1, keepdims=True))
        return (slope - jnp.mean(slope, axis=-1, keepdims=True)).astype(jnp.bfloat16)

    def contract(left, right, left_dim, right_dim):
        return lax.dot_general(
            left,
            right,
            (((left_dim,), (right_dim,)), ((), ())),
            preferred_element_type=jnp.float32,
        )

    def half(values):
        return values.astype(jnp.bfloat16)

    q_norm, q_inverse = norm(total(q_own, q_got))
    k_norm, k_inverse = norm(total(k_own, k_got))
    q_half, k_half = half(q_norm), half(k_norm)
    v_half = half(total(v_own, v_got))
    grad = half(total(g_own, g_got))
    weights = jnp.exp(contract(q_half, k_half, 1, 1) * scale)
    probs = weights / jnp.sum(weights, axis=-1, keepdims=True)
    probs_half = half(probs)
    mixed_ref[...] = half(contract(probs_half, v_half, 1, 0))
    dv_ref[...] = half(contract(probs_half, grad, 0, 0))
    probs_grad = half(contract(grad, v_half, 1, 1)).astype(jnp.float32)
    inner = jnp.sum(probs_grad * probs, axis=-1, keepdims=True)
    score_grad = half(probs * (probs_grad - inner) * scale)
    q_grad = half(contract(score_grad, k_half, 1, 0)).astype(jnp.float32)
    k_grad = half(contract(score_grad, q_half, 0, 0)).astype(jnp.float32)
    dq_ref[...] = norm_back(q_grad, q_norm, q_inverse)
    dk_ref[...] = norm_back(k_grad, k_norm, k_inverse)


def attend(own, got, grad_own, grad_got):
    rows, width = grad_own.shape
    heads = width // HEAD_DIM

    def block(part):
        return pl.BlockSpec((IMG_TOK, HEAD_DIM), lambda image, head: (image, part * heads + head))

    half = jax.ShapeDtypeStruct((rows, width), jnp.bfloat16)
    return pl.pallas_call(
        functools.partial(attend_kernel, scale=1.0 / math.sqrt(HEAD_DIM)),
        grid=(rows // IMG_TOK, heads),
        in_specs=[block(0), block(0), block(1), block(1), block(2), block(2), block(0), block(0)],
        out_specs=[block(0)] * 4,
        out_shape=[half] * 4,
        compiler_params=pltpu.CompilerParams(vmem_limit_bytes=32 * 1024 * 1024),
        cost_estimate=pl.CostEstimate(
            flops=12 * rows * IMG_TOK * width,
            bytes_accessed=24 * rows * width,
            transcendentals=rows * IMG_TOK * heads,
        ),
        name="attend",
    )(own, got, own, got, own, got, grad_own, grad_got)


def gelu(pre):
    return pre * 0.5 * (1.0 + lax.erf(pre * ROOT_HALF))


def gelu_back(pre, grad_half):
    cdf = 0.5 * (1.0 + lax.erf(pre * ROOT_HALF))
    pdf = jnp.exp(-0.5 * pre * pre) * ROOT_TWO_PI_INV
    return (grad_half.astype(jnp.float32) * (cdf + pre * pdf)).astype(jnp.bfloat16)


def dot(left, right):
    return jnp.dot(left, right, preferred_element_type=jnp.float32)


def back_dot(left, right):
    return lax.dot_general(
        left, right, (((1,), (1,)), ((), ())), preferred_element_type=jnp.float32
    )


def half(values):
    return values.astype(jnp.bfloat16)


def wide_sum(own, got):
    return own.astype(jnp.float32) + got.astype(jnp.float32)


def trade(block, axis, bit):
    pairs = [(index, index ^ bit) for index in range(lax.axis_size(axis))]
    return lax.ppermute(block, axis, pairs)


def body(layer_input, out_cotangent, w_query, w_key, w_value, w_mlp_in, w_attn_out, w_mlp_out):
    n_gx, n_gy, n_gz = (lax.axis_size(name) for name in ("gx", "gy", "gz"))
    me_x, me_y = lax.axis_index("gx"), lax.axis_index("gy")
    own_rows = layer_input.shape[0]
    image_rows = own_rows * n_gy
    depth = w_query.shape[0]
    row_order = (3, 1, 2, 0)

    def all_rows(block):
        gathered = lax.all_gather(block, ("gx", "gy"), axis=0, tiled=True)
        return jnp.concatenate(
            [
                lax.dynamic_slice_in_dim(gathered, (me_x ^ bit) * image_rows, image_rows, 0)
                for bit in row_order
            ],
            axis=0,
        )

    def relative(value):
        return jnp.concatenate(
            [
                lax.dynamic_slice_in_dim(value, (me_x ^ bit) * depth, depth, 1)
                for bit in range(n_gx)
            ],
            axis=1,
        )

    def same(value, bit):
        return value

    def reordered(value, bit):
        return jnp.concatenate(
            [
                lax.slice_in_dim(value, (place ^ bit) * depth, ((place ^ bit) + 1) * depth, axis=1)
                for place in range(n_gx)
            ],
            axis=1,
        )

    def others(part):
        if n_gz == 2:
            return trade(part, "gz", 1)
        return half(lax.psum(part.astype(jnp.float32), "gz") - part.astype(jnp.float32))

    def columns_of(weights, cut, cuts):
        pieces = []
        for bit in range(n_gx):
            slices = []
            for weight in weights:
                owned = weight.shape[1] // n_gx
                count = owned // cuts
                start = (me_x ^ bit) * owned + cut * count
                slices.append(lax.dynamic_slice_in_dim(weight, start, count, 1))
            piece = jnp.concatenate(slices, axis=1) if len(slices) > 1 else slices[0]
            pieces.append(piece if bit == 0 else trade(piece, "gx", bit))
        return jnp.concatenate(pieces, axis=0)

    def after(value, earlier):
        return lax.optimization_barrier((value, earlier))[0]

    mlp_cuts = 3
    in_heads = columns_of((w_query, w_key, w_value), 0, 1)
    in_mlp = [columns_of((w_mlp_in,), cut, mlp_cuts) for cut in range(mlp_cuts)]

    wide = layer_input.astype(jnp.float32)
    total, squares = lax.psum((jnp.sum(wide, axis=1), jnp.sum(wide * wide, axis=1)), "gz")
    center = total / D
    spread = squares / D - center * center
    inverse = lax.rsqrt(spread + EPSILON)
    normed = (wide - center[:, None]) * inverse[:, None]
    gathered_in = relative(all_rows(half(normed)))

    heads_own = half(dot(gathered_in, in_heads))
    heads_got = others(heads_own)
    mlp_own = [half(dot(gathered_in, weight)) for weight in in_mlp]
    mlp_got = [others(own) for own in mlp_own]

    gathered_cot = all_rows(out_cotangent)
    mixed_own = half(back_dot(gathered_cot, w_attn_out))
    mixed_got = others(mixed_own)

    mixed, query_grad, key_grad, value_grad = attend(heads_own, heads_got, mixed_own, mixed_got)
    pre = [wide_sum(own, got) for own, got in zip(mlp_own, mlp_got)]
    acts = jnp.concatenate([mixed] + [half(gelu(part)) for part in pre], axis=1)
    w_out = jnp.concatenate([w_attn_out, w_mlp_out], axis=0)
    w_in = jnp.concatenate([in_heads] + in_mlp, axis=1)
    late_cot = after(gathered_cot, mlp_own[-1])

    def block_of(value, start, count):
        return lax.slice_in_dim(value, start * image_rows, (start + count) * image_rows)

    def forward_term(start, count):
        return dot(block_of(acts, start, count), w_out)

    def backward_term(start, count):
        act_own = half(back_dot(block_of(late_cot, start, count), w_mlp_out))
        grad = half(wide_sum(act_own, others(act_own)))
        parts = [block_of(value, start, count) for value in (query_grad, key_grad, value_grad)]
        width = grad.shape[1] // mlp_cuts
        for cut in range(mlp_cuts):
            columns = grad[:, cut * width : (cut + 1) * width]
            parts.append(gelu_back(block_of(pre[cut], start, count), columns))
        return back_dot(jnp.concatenate(parts, axis=1), w_in)

    def spread_rows(term, mapped):
        from_core = mapped(trade(half(term(0, 2)), "gx", 1), 1)
        to_x = half(term(2, 1) + from_core[:image_rows].astype(jnp.float32))
        from_x = mapped(trade(to_x, "gx", 2), 2)
        mine = term(3, 1) + wide_sum(from_core[image_rows:], from_x)
        quarters = mine.reshape(2, 2, own_rows, mine.shape[1])
        odd = me_y % 2 == 1
        kept = jnp.where(odd, quarters[:, 1], quarters[:, 0])
        sent = jnp.where(odd, quarters[:, 0], quarters[:, 1])
        pair = kept + trade(half(sent), "gy", 1).astype(jnp.float32)
        high = me_y >= 2
        kept = jnp.where(high, pair[1], pair[0])
        sent = jnp.where(high, pair[0], pair[1])
        return kept + trade(half(sent), "gy", 2).astype(jnp.float32)

    layer_out = half(wide + spread_rows(forward_term, same))
    normed_grad = relative(spread_rows(backward_term, reordered))
    first, second = lax.psum(
        (jnp.sum(normed_grad, axis=1), jnp.sum(normed_grad * normed, axis=1)), "gz"
    )
    grad_full = out_cotangent.astype(jnp.float32) + inverse[:, None] * (
        normed_grad - (first / D)[:, None] - normed * (second / D)[:, None]
    )
    return (layer_out, half(grad_full))


def solution(mesh):
    in_specs = (
        P(("gx", "gy"), "gz"),
        P(("gx", "gy"), "gz"),
        P(("gz", "gx"), "gy"),
        P(("gz", "gx"), "gy"),
        P(("gz", "gx"), "gy"),
        P(("gz", "gx"), "gy"),
        P(("gy", "gx"), "gz"),
        P(("gy", "gx"), "gz"),
    )
    out_specs = (P(("gx", "gy"), "gz"), P(("gx", "gy"), "gz"))
    return jax.shard_map(body, mesh=mesh, in_specs=in_specs, out_specs=out_specs, check_vma=False)
```

```python
import functools
import math

import jax
import jax.numpy as jnp
from jax import lax
from jax.experimental import pallas as pl
from jax.experimental.pallas import tpu as pltpu
from jax.sharding import PartitionSpec as P

D = 6144
HEAD_DIM = 128
IMG_TOK = 256


EPSILON = 1e-06
ROOT_HALF = 0.7071067811865476
ROOT_TWO_PI_INV = 0.3989422804014327


def attend_kernel(
    q_own, q_got, k_own, k_got, v_own, v_got, g_own, g_got, mixed_ref, dq_ref, dk_ref, dv_ref, *, scale
):
    def total(own, got):
        return own[...].astype(jnp.float32) + got[...].astype(jnp.float32)

    def norm(values):
        center = values - jnp.mean(values, axis=-1, keepdims=True)
        spread = jnp.mean(center * center, axis=-1, keepdims=True)
        inverse = lax.rsqrt(spread + EPSILON)
        return center * inverse, inverse

    def norm_back(grad, normed, inverse):
        slope = inverse * (grad - normed * jnp.mean(grad * normed, axis=-1, keepdims=True))
        return (slope - jnp.mean(slope, axis=-1, keepdims=True)).astype(jnp.bfloat16)

    def contract(left, right, left_dim, right_dim):
        return lax.dot_general(
            left,
            right,
            (((left_dim,), (right_dim,)), ((), ())),
            preferred_element_type=jnp.float32,
        )

    def half(values):
        return values.astype(jnp.bfloat16)

    q_norm, q_inverse = norm(total(q_own, q_got))
    k_norm, k_inverse = norm(total(k_own, k_got))
    q_half, k_half = half(q_norm), half(k_norm)
    v_half = half(total(v_own, v_got))
    grad = half(total(g_own, g_got))
    weights = jnp.exp(contract(q_half, k_half, 1, 1) * scale)
    probs = weights / jnp.sum(weights, axis=-1, keepdims=True)
    probs_half = half(probs)
    mixed_ref[...] = half(contract(probs_half, v_half, 1, 0))
    dv_ref[...] = half(contract(probs_half, grad, 0, 0))
    probs_grad = half(contract(grad, v_half, 1, 1)).astype(jnp.float32)
    inner = jnp.sum(probs_grad * probs, axis=-1, keepdims=True)
    score_grad = half(probs * (probs_grad - inner) * scale)
    q_grad = half(contract(score_grad, k_half, 1, 0)).astype(jnp.float32)
    k_grad = half(contract(score_grad, q_half, 0, 0)).astype(jnp.float32)
    dq_ref[...] = norm_back(q_grad, q_norm, q_inverse)
    dk_ref[...] = norm_back(k_grad, k_norm, k_inverse)


def attend(own, got, grad_own, grad_got):
    rows, width = grad_own.shape
    heads = width // HEAD_DIM

    def block(part):
        return pl.BlockSpec((IMG_TOK, HEAD_DIM), lambda image, head: (image, part * heads + head))

    half = jax.ShapeDtypeStruct((rows, width), jnp.bfloat16)
    return pl.pallas_call(
        functools.partial(attend_kernel, scale=1.0 / math.sqrt(HEAD_DIM)),
        grid=(rows // IMG_TOK, heads),
        in_specs=[block(0), block(0), block(1), block(1), block(2), block(2), block(0), block(0)],
        out_specs=[block(0)] * 4,
        out_shape=[half] * 4,
        compiler_params=pltpu.CompilerParams(vmem_limit_bytes=32 * 1024 * 1024),
        cost_estimate=pl.CostEstimate(
            flops=12 * rows * IMG_TOK * width,
            bytes_accessed=24 * rows * width,
            transcendentals=rows * IMG_TOK * heads,
        ),
        name="attend",
    )(own, got, own, got, own, got, grad_own, grad_got)


def gelu(pre):
    return pre * 0.5 * (1.0 + lax.erf(pre * ROOT_HALF))


def gelu_back(pre, grad_half):
    cdf = 0.5 * (1.0 + lax.erf(pre * ROOT_HALF))
    pdf = jnp.exp(-0.5 * pre * pre) * ROOT_TWO_PI_INV
    return (grad_half.astype(jnp.float32) * (cdf + pre * pdf)).astype(jnp.bfloat16)


def dot(left, right):
    return jnp.dot(left, right, preferred_element_type=jnp.float32)


def back_dot(left, right):
    return lax.dot_general(
        left, right, (((1,), (1,)), ((), ())), preferred_element_type=jnp.float32
    )


def half(values):
    return values.astype(jnp.bfloat16)


def wide_sum(own, got):
    return own.astype(jnp.float32) + got.astype(jnp.float32)


def trade(block, axis, bit):
    pairs = [(index, index ^ bit) for index in range(lax.axis_size(axis))]
    return lax.ppermute(block, axis, pairs)


VMEM_LIMIT = 48 * 1024 * 1024


def params():
    return pltpu.CompilerParams(vmem_limit_bytes=VMEM_LIMIT)


def cost(flops, *arrays):
    moved = sum(math.prod(array.shape) * array.dtype.itemsize for array in arrays)
    return pl.CostEstimate(flops=flops, bytes_accessed=moved, transcendentals=0)


def copy_kernel(rows_ref, columns_ref, value_ref, out_ref):
    out_ref[...] = value_ref[...]


def pick_blocks(value, row_index, column_index):
    rows, columns = value.shape
    block = (rows // row_index.shape[0], columns // column_index.shape[0])
    if block[1] % 128:
        grid_of = (row_index.shape[0], block[0], column_index.shape[0], block[1])
        picked = value.reshape(grid_of)[row_index][:, :, column_index]
        return picked.reshape(rows, columns)
    return pl.pallas_call(
        copy_kernel,
        grid_spec=pltpu.PrefetchScalarGridSpec(
            num_scalar_prefetch=2,
            grid=(row_index.shape[0], column_index.shape[0]),
            in_specs=[pl.BlockSpec(block, lambda i, j, row, column: (row[i], column[j]))],
            out_specs=pl.BlockSpec(block, lambda i, j, row, column: (i, j)),
        ),
        out_shape=jax.ShapeDtypeStruct(value.shape, value.dtype),
        compiler_params=params(),
        cost_estimate=cost(0, value, value),
        name="pick_blocks",
    )(row_index, column_index, value)


def in_kernel(rows_ref, *refs):
    pieces, out_ref = refs[:-1], refs[-1]
    depth = pieces[0].shape[0]
    total = None
    for place, piece in enumerate(pieces):
        part = dot(rows_ref[:, place * depth : (place + 1) * depth], piece[...])
        total = part if total is None else total + part
    out_ref[...] = total.astype(out_ref.dtype)


def in_product(rows, pieces):
    count = rows.shape[0]
    depth, columns = pieces[0].shape
    tile = 384 if columns % 384 == 0 else 256
    out = jax.ShapeDtypeStruct((count, columns), jnp.bfloat16)
    return pl.pallas_call(
        in_kernel,
        grid=(columns // tile,),
        in_specs=[pl.BlockSpec(rows.shape, lambda n: (0, 0))]
        + [pl.BlockSpec((depth, tile), lambda n: (0, n)) for _ in pieces],
        out_specs=pl.BlockSpec((count, tile), lambda n: (0, n)),
        out_shape=out,
        compiler_params=params(),
        cost_estimate=cost(2 * count * columns * rows.shape[1], rows, out, *pieces),
        name="in_product",
    )(rows, *pieces)


def out_product(mixed, acts, w_attn_out, w_mlp_out, start, count, add, add_start, kind):
    columns = w_attn_out.shape[1]
    tile = 512 if columns % 512 == 0 else 256

    def rows_spec(value):
        return pl.BlockSpec((count, value.shape[1]), lambda n: (start // count, 0))

    def columns_spec(value):
        return pl.BlockSpec((value.shape[0], tile), lambda n: (0, n))

    operands = [mixed, *acts, w_attn_out, w_mlp_out]
    specs = [rows_spec(mixed), *(rows_spec(act) for act in acts)]
    specs += [columns_spec(w_attn_out), columns_spec(w_mlp_out)]
    if add is not None:
        operands.append(add)
        specs.append(pl.BlockSpec((count, tile), lambda n: (add_start // count, n)))
    depth = w_attn_out.shape[0] + w_mlp_out.shape[0]

    def kernel(*refs):
        n_acts = len(acts)
        attn_ref, mlp_ref, out_ref = refs[n_acts + 1], refs[n_acts + 2], refs[-1]
        total = dot(refs[0][...], attn_ref[...])
        row = 0
        for act in refs[1 : n_acts + 1]:
            total = total + dot(act[...], mlp_ref[row : row + act.shape[1], :])
            row += act.shape[1]
        if add is not None:
            total = total + refs[n_acts + 3][...].astype(jnp.float32)
        out_ref[...] = total.astype(out_ref.dtype)

    out = jax.ShapeDtypeStruct((count, columns), kind)
    return pl.pallas_call(
        kernel,
        grid=(columns // tile,),
        in_specs=specs,
        out_specs=pl.BlockSpec((count, tile), lambda n: (0, n)),
        out_shape=out,
        compiler_params=params(),
        cost_estimate=cost(2 * count * columns * depth, out, w_attn_out, w_mlp_out),
        name="out_product",
    )(*operands)


def back_product(head_grads, mlp_grads, head_pieces, mlp_pieces, start, add, add_start, flip, kind):
    count = mlp_grads[0].shape[0]
    n_pieces, depth = len(head_pieces), head_pieces[0].shape[0]
    tile = 256 if depth % 256 == 0 else depth
    heads_width = head_grads[0].shape[1]
    n_heads, n_mlp = len(head_grads), len(mlp_grads)
    operands = [*head_grads, *mlp_grads]
    specs = [pl.BlockSpec((count, heads_width), lambda n: (start // count, 0))] * n_heads
    specs += [pl.BlockSpec(grad.shape, lambda n: (0, 0)) for grad in mlp_grads]
    for place in range(n_pieces):
        for piece in (head_pieces[place], *(cut[place] for cut in mlp_pieces)):
            operands.append(piece)
            specs.append(pl.BlockSpec((tile, piece.shape[1]), lambda n: (n, 0)))
    if add is not None:
        operands.append(add)
        specs.append(
            pl.BlockSpec((n_pieces, count, tile), lambda n: (0, add_start // count, n))
        )

    def kernel(*refs):
        grads, weights = refs[: n_heads + n_mlp], refs[n_heads + n_mlp :]
        out_ref = refs[-1]
        for place in range(n_pieces):
            group = weights[place * (n_mlp + 1) : (place + 1) * (n_mlp + 1)]
            total = None
            for index in range(n_heads):
                columns = slice(index * heads_width, (index + 1) * heads_width)
                part = back_dot(grads[index][...], group[0][:, columns])
                total = part if total is None else total + part
            for grad, weight in zip(grads[n_heads:], group[1:]):
                total = total + back_dot(grad[...], weight[...])
            if add is not None:
                total = total + refs[-2][place ^ flip].astype(jnp.float32)
            out_ref[place] = total.astype(out_ref.dtype)

    width = n_heads * heads_width + sum(grad.shape[1] for grad in mlp_grads)
    out = jax.ShapeDtypeStruct((n_pieces, count, depth), kind)
    return pl.pallas_call(
        kernel,
        grid=(depth // tile,),
        in_specs=specs,
        out_specs=pl.BlockSpec((n_pieces, count, tile), lambda n: (0, 0, n)),
        out_shape=out,
        compiler_params=params(),
        cost_estimate=cost(2 * count * depth * n_pieces * width, out, *operands),
        name="back_product",
    )(*operands)


def body(layer_input, out_cotangent, w_query, w_key, w_value, w_mlp_in, w_attn_out, w_mlp_out):
    n_gx, n_gy, n_gz = (lax.axis_size(name) for name in ("gx", "gy", "gz"))
    me_x, me_y = lax.axis_index("gx"), lax.axis_index("gy")
    own_rows = layer_input.shape[0]
    image_rows = own_rows * n_gy
    depth = w_query.shape[0]
    row_index = me_x ^ jnp.array((3, 1, 2, 0), jnp.int32)
    feature_index = me_x ^ jnp.arange(n_gx, dtype=jnp.int32)

    def after(value, earlier):
        return lax.optimization_barrier((value, earlier))[0]

    def others(part):
        if n_gz == 2:
            return trade(part, "gz", 1)
        return half(lax.psum(part.astype(jnp.float32), "gz") - part.astype(jnp.float32))

    def columns_of(weights, cut, cuts, earlier):
        pieces = []
        for bit in range(n_gx):
            slices = []
            for weight in weights:
                owned = weight.shape[1] // n_gx
                count = owned // cuts
                start = (me_x ^ bit) * owned + cut * count
                slices.append(lax.dynamic_slice_in_dim(weight, start, count, 1))
            pieces.append(jnp.concatenate(slices, axis=1) if len(slices) > 1 else slices[0])
        if earlier is not None:
            pieces = after(pieces, earlier)
        return [piece if bit == 0 else trade(piece, "gx", bit) for bit, piece in enumerate(pieces)]

    mlp_cuts = 3
    in_heads = columns_of((w_query, w_key, w_value), 0, 1, None)
    in_mlp = []
    earlier = in_heads[2]
    for cut in range(mlp_cuts):
        in_mlp.append(columns_of((w_mlp_in,), cut, mlp_cuts, earlier))
        earlier = in_mlp[-1][2]

    wide = layer_input.astype(jnp.float32)
    total, squares = lax.psum((jnp.sum(wide, axis=1), jnp.sum(wide * wide, axis=1)), "gz")
    center = total / D
    spread = squares / D - center * center
    inverse = lax.rsqrt(spread + EPSILON)
    normed = (wide - center[:, None]) * inverse[:, None]
    normed_half = half(normed)
    all_in = lax.all_gather(normed_half, ("gx", "gy"), axis=0, tiled=True)
    all_cot = lax.all_gather(
        after(out_cotangent, normed_half), ("gx", "gy"), axis=0, tiled=True
    )
    gathered_in = pick_blocks(all_in, row_index, feature_index)
    gathered_cot = pick_blocks(all_cot, row_index, jnp.zeros((1,), jnp.int32))

    heads_own = in_product(gathered_in, in_heads)
    heads_got = others(heads_own)
    mlp_own = [in_product(gathered_in, pieces) for pieces in in_mlp]
    mlp_got = [others(own) for own in mlp_own]

    mixed_own = half(back_dot(gathered_cot, w_attn_out))
    mixed_got = others(mixed_own)

    mixed, *head_grads = attend(heads_own, heads_got, mixed_own, mixed_got)
    pre = [wide_sum(own, got) for own, got in zip(mlp_own, mlp_got)]
    acts = [half(gelu(part)) for part in pre]
    late_cot = after(gathered_cot, mlp_own[-1])

    def block_of(value, start, count):
        return lax.slice_in_dim(value, start, start + count)

    def forward_term(start, count, add, add_start, flip, kind):
        return out_product(mixed, acts, w_attn_out, w_mlp_out, start, count, add, add_start, kind)

    def backward_term(start, count, add, add_start, flip, kind):
        act_own = half(back_dot(block_of(late_cot, start, count), w_mlp_out))
        grad = half(wide_sum(act_own, others(act_own)))
        width = grad.shape[1] // mlp_cuts
        mlp_grads = [
            gelu_back(block_of(pre[cut], start, count), grad[:, cut * width : (cut + 1) * width])
            for cut in range(mlp_cuts)
        ]
        return back_product(
            head_grads, mlp_grads, in_heads, in_mlp, start, add, add_start, flip, kind
        )

    def spread_rows(term, rows_axis, settled):
        count = image_rows
        from_core = trade(term(0, 2 * count, None, 0, 0, jnp.bfloat16), "gx", 1)
        to_x = term(2 * count, count, from_core, 0, 1, jnp.bfloat16)
        from_x = trade(to_x, "gx", 2)
        mine = term(3 * count, count, from_core, count, 1, jnp.float32)
        mine = mine + settled(from_x, 2).astype(jnp.float32)
        lead = mine.shape[:rows_axis]
        quarters = mine.reshape(lead + (2, 2, own_rows, mine.shape[-1]))

        def at(value, axis, index):
            return lax.index_in_dim(value, index, axis, keepdims=False)

        odd = me_y % 2 == 1
        even_part, odd_part = (at(quarters, rows_axis + 1, index) for index in (0, 1))
        kept, sent = jnp.where(odd, odd_part, even_part), jnp.where(odd, even_part, odd_part)
        pair = kept + trade(half(sent), "gy", 1).astype(jnp.float32)
        high = me_y >= 2
        low_part, high_part = (at(pair, rows_axis, index) for index in (0, 1))
        kept, sent = jnp.where(high, high_part, low_part), jnp.where(high, low_part, high_part)
        return kept + trade(half(sent), "gy", 2).astype(jnp.float32)

    layer_out = half(wide + spread_rows(forward_term, 0, lambda value, flip: value))

    def settled(value, flip):
        return jnp.stack([value[place ^ flip] for place in range(n_gx)])

    by_piece = spread_rows(backward_term, 1, settled)
    normed_grad = jnp.concatenate(
        [
            lax.dynamic_index_in_dim(by_piece, me_x ^ block, 0, keepdims=False)
            for block in range(n_gx)
        ],
        axis=1,
    )
    first, second = lax.psum(
        (jnp.sum(normed_grad, axis=1), jnp.sum(normed_grad * normed, axis=1)), "gz"
    )
    grad_full = out_cotangent.astype(jnp.float32) + inverse[:, None] * (
        normed_grad - (first / D)[:, None] - normed * (second / D)[:, None]
    )
    return (layer_out, half(grad_full))


def solution(mesh):
    in_specs = (
        P(("gx", "gy"), "gz"),
        P(("gx", "gy"), "gz"),
        P(("gz", "gx"), "gy"),
        P(("gz", "gx"), "gy"),
        P(("gz", "gx"), "gy"),
        P(("gz", "gx"), "gy"),
        P(("gy", "gx"), "gz"),
        P(("gy", "gx"), "gz"),
    )
    out_specs = (P(("gx", "gy"), "gz"), P(("gx", "gy"), "gz"))
    return jax.shard_map(body, mesh=mesh, in_specs=in_specs, out_specs=out_specs, check_vma=False)
```

```python
import functools
import math

import jax
import jax.numpy as jnp
from jax import lax
from jax.experimental import pallas as pl
from jax.experimental.pallas import tpu as pltpu
from jax.sharding import PartitionSpec as P

D = 6144
HEAD_DIM = 128
IMG_TOK = 256


EPSILON = 1e-06
ROOT_HALF = 0.7071067811865476
ROOT_TWO_PI_INV = 0.3989422804014327


def attend_kernel(
    q_own, q_got, k_own, k_got, v_own, v_got, g_ref, mixed_ref, dq_ref, dk_ref, dv_ref, *, scale
):
    def total(own, got):
        return own[...].astype(jnp.float32) + got[...].astype(jnp.float32)

    def norm(values):
        center = values - jnp.mean(values, axis=-1, keepdims=True)
        spread = jnp.mean(center * center, axis=-1, keepdims=True)
        inverse = lax.rsqrt(spread + EPSILON)
        return center * inverse, inverse

    def norm_back(grad, normed, inverse):
        slope = inverse * (grad - normed * jnp.mean(grad * normed, axis=-1, keepdims=True))
        return (slope - jnp.mean(slope, axis=-1, keepdims=True)).astype(jnp.bfloat16)

    def contract(left, right, left_dim, right_dim):
        return lax.dot_general(
            left,
            right,
            (((left_dim,), (right_dim,)), ((), ())),
            preferred_element_type=jnp.float32,
        )

    def half(values):
        return values.astype(jnp.bfloat16)

    q_norm, q_inverse = norm(total(q_own, q_got))
    k_norm, k_inverse = norm(total(k_own, k_got))
    q_half, k_half = half(q_norm), half(k_norm)
    v_half = half(total(v_own, v_got))
    grad = g_ref[...]
    weights = jnp.exp(contract(q_half, k_half, 1, 1) * scale)
    probs = weights / jnp.sum(weights, axis=-1, keepdims=True)
    probs_half = half(probs)
    mixed_ref[...] = half(contract(probs_half, v_half, 1, 0))
    dv_ref[...] = half(contract(probs_half, grad, 0, 0))
    probs_grad = half(contract(grad, v_half, 1, 1)).astype(jnp.float32)
    inner = jnp.sum(probs_grad * probs, axis=-1, keepdims=True)
    score_grad = half(probs * (probs_grad - inner) * scale)
    q_grad = half(contract(score_grad, k_half, 1, 0)).astype(jnp.float32)
    k_grad = half(contract(score_grad, q_half, 0, 0)).astype(jnp.float32)
    dq_ref[...] = norm_back(q_grad, q_norm, q_inverse)
    dk_ref[...] = norm_back(k_grad, k_norm, k_inverse)


def attend(own, got, grad):
    rows, width = own.shape[0], own.shape[1] // 3
    heads = width // HEAD_DIM

    def block(part):
        return pl.BlockSpec((IMG_TOK, HEAD_DIM), lambda image, head: (image, part * heads + head))

    half = jax.ShapeDtypeStruct((rows, width), jnp.bfloat16)
    return pl.pallas_call(
        functools.partial(attend_kernel, scale=1.0 / math.sqrt(HEAD_DIM)),
        grid=(rows // IMG_TOK, heads),
        in_specs=[block(0), block(0), block(1), block(1), block(2), block(2), block(0)],
        out_specs=[block(0)] * 4,
        out_shape=[half] * 4,
        compiler_params=pltpu.CompilerParams(vmem_limit_bytes=32 * 1024 * 1024),
        cost_estimate=pl.CostEstimate(
            flops=12 * rows * IMG_TOK * width,
            bytes_accessed=24 * rows * width,
            transcendentals=rows * IMG_TOK * heads,
        ),
        name="attend",
    )(own, got, own, got, own, got, grad)


def gelu(pre):
    return pre * 0.5 * (1.0 + lax.erf(pre * ROOT_HALF))


def gelu_back(pre, grad_half):
    cdf = 0.5 * (1.0 + lax.erf(pre * ROOT_HALF))
    pdf = jnp.exp(-0.5 * pre * pre) * ROOT_TWO_PI_INV
    return (grad_half.astype(jnp.float32) * (cdf + pre * pdf)).astype(jnp.bfloat16)


def dot(left, right):
    return jnp.dot(left, right, preferred_element_type=jnp.float32)


def back_dot(left, right):
    return lax.dot_general(
        left, right, (((1,), (1,)), ((), ())), preferred_element_type=jnp.float32
    )


def half(values):
    return values.astype(jnp.bfloat16)


def wide_sum(own, got):
    return own.astype(jnp.float32) + got.astype(jnp.float32)


def trade(block, axis, bit):
    pairs = [(index, index ^ bit) for index in range(lax.axis_size(axis))]
    return lax.ppermute(block, axis, pairs)


VMEM_LIMIT = 48 * 1024 * 1024


def params():
    return pltpu.CompilerParams(vmem_limit_bytes=VMEM_LIMIT)


def cost(flops, *arrays):
    moved = sum(math.prod(array.shape) * array.dtype.itemsize for array in arrays)
    return pl.CostEstimate(flops=flops, bytes_accessed=moved, transcendentals=0)


def pack_kernel(*refs):
    out_ref, start = refs[-1], 0
    for ref in refs[:-1]:
        out_ref[0, :, start : start + ref.shape[1]] = ref[...]
        start += ref.shape[1]


def pack(weights, owners, start, width, tile):
    rows, columns = weights[0].shape
    first, blocks = start // tile, columns // owners // tile
    out = jax.ShapeDtypeStruct((owners, rows, len(weights) * width), weights[0].dtype)
    spec = pl.BlockSpec((rows, tile), lambda owner, n: (0, owner * blocks + first + n))
    return pl.pallas_call(
        pack_kernel,
        grid=(owners, width // tile),
        in_specs=[spec] * len(weights),
        out_specs=pl.BlockSpec((1, rows, len(weights) * tile), lambda owner, n: (owner, 0, n)),
        out_shape=out,
        compiler_params=params(),
        cost_estimate=cost(0, out, out),
        name="pack",
    )(*weights)


IMAGE_ORDER = ((1, 1), (0, 1), (1, 0), (0, 0))


def assemble_kernel(*refs):
    parts, out_ref = refs[:-1], refs[-1]
    rows = parts[0].shape[1]
    start = 0
    for x_bit, core_bit in IMAGE_ORDER:
        for part in range(len(parts) // 2):
            out_ref[start : start + rows, :] = parts[2 * part + core_bit][x_bit]
            start += rows


def assemble(parts):
    flat = [value for part in parts for value in part]
    _, rows, features = flat[0].shape
    tile = 768
    out = jax.ShapeDtypeStruct((len(flat) * 2 * rows, features), flat[0].dtype)
    return pl.pallas_call(
        assemble_kernel,
        grid=(features // tile,),
        in_specs=[pl.BlockSpec((2, rows, tile), lambda n: (0, 0, n))] * len(flat),
        out_specs=pl.BlockSpec((out.shape[0], tile), lambda n: (0, n)),
        out_shape=out,
        compiler_params=params(),
        cost_estimate=cost(0, out, out),
        name="assemble",
    )(*flat)


def cot_kernel(own_ref, other_ref, attn_ref, mlp_ref, out_ref, rows_ref):
    rows = own_ref.shape[1]
    step = pl.program_id(0)

    @pl.when(step == 0)
    def _():
        for place, (x_bit, core_bit) in enumerate(IMAGE_ORDER):
            part = other_ref if core_bit else own_ref
            rows_ref[place * rows : (place + 1) * rows, :] = part[x_bit]
        out_ref[...] = half(back_dot(rows_ref[...], attn_ref[...]))

    @pl.when(step > 0)
    def _():
        out_ref[...] = half(back_dot(rows_ref[...], mlp_ref[...]))


def cot_product(part, w_attn_out, w_mlp_out):
    own, other = part
    _, rows, features = own.shape
    tile = w_attn_out.shape[0]
    columns = tile + w_mlp_out.shape[0]
    count = len(IMAGE_ORDER) * rows
    out = jax.ShapeDtypeStruct((count, columns), jnp.bfloat16)
    whole = pl.BlockSpec(own.shape, lambda n: (0, 0, 0))
    return pl.pallas_call(
        cot_kernel,
        grid=(columns // tile,),
        in_specs=[
            whole,
            whole,
            pl.BlockSpec((tile, features), lambda n: (0, 0)),
            pl.BlockSpec((tile, features), lambda n: (jnp.maximum(n - 1, 0), 0)),
        ],
        out_specs=pl.BlockSpec((count, tile), lambda n: (0, n)),
        out_shape=out,
        scratch_shapes=[pltpu.VMEM((count, features), jnp.bfloat16)],
        compiler_params=params(),
        cost_estimate=cost(2 * count * columns * features, out, w_attn_out, w_mlp_out),
        name="cot_product",
    )(own, other, w_attn_out, w_mlp_out)


def add_kernel(*refs):
    terms, out_ref = refs[:-1], refs[-1]
    count = len(terms) // 2
    for part in range(count):
        out_ref[0, part] = half(wide_sum(terms[part][0], terms[count + part][0]))


def add_parts(owns, gots):
    images, parts = len(IMAGE_ORDER), len(owns)
    rows, columns = owns[0].shape[0] // images, owns[0].shape[1]
    out = jax.ShapeDtypeStruct((images, parts, rows, columns), jnp.bfloat16)
    terms = [value.reshape(images, rows, columns) for value in (*owns, *gots)]
    added = pl.pallas_call(
        add_kernel,
        grid=(images,),
        in_specs=[pl.BlockSpec((1, rows, columns), lambda image: (image, 0, 0))] * len(terms),
        out_specs=pl.BlockSpec((1, parts, rows, columns), lambda image: (image, 0, 0, 0)),
        out_shape=out,
        compiler_params=params(),
        cost_estimate=cost(0, out, out, out),
        name="add_parts",
    )(*terms)
    return added.reshape(images * parts * rows, columns)


def in_kernel(rows_ref, weight_ref, out_ref):
    out_ref[...] = half(dot(rows_ref[...], weight_ref[...]))


def in_product(rows, weight):
    count, features = rows.shape
    columns = weight.shape[1]
    tile = 384 if columns % 384 == 0 else 256
    out = jax.ShapeDtypeStruct((count, columns), jnp.bfloat16)
    return pl.pallas_call(
        in_kernel,
        grid=(columns // tile,),
        in_specs=[
            pl.BlockSpec((count, features), lambda n: (0, 0)),
            pl.BlockSpec((features, tile), lambda n: (0, n)),
        ],
        out_specs=pl.BlockSpec((count, tile), lambda n: (0, n)),
        out_shape=out,
        compiler_params=params(),
        cost_estimate=cost(2 * count * columns * features, rows, out, weight),
        name="in_product",
    )(rows, weight)


def out_product(mixed, acts, w_attn_out, w_mlp_out, start, count, add, add_start, kind):
    columns = w_attn_out.shape[1]
    tile = 512 if columns % 512 == 0 else 256
    n_acts = len(acts)

    def rows_spec(value):
        return pl.BlockSpec((count, value.shape[1]), lambda n: (start // count, 0))

    def columns_spec(value):
        return pl.BlockSpec((value.shape[0], tile), lambda n: (0, n))

    operands = [mixed, *acts, w_attn_out, w_mlp_out]
    specs = [rows_spec(mixed), *(rows_spec(act) for act in acts)]
    specs += [columns_spec(w_attn_out), columns_spec(w_mlp_out)]
    if add is not None:
        operands.append(add)
        specs.append(pl.BlockSpec((count, tile), lambda n: (add_start // count, n)))

    def kernel(*refs):
        attn_ref, mlp_ref, out_ref = refs[n_acts + 1], refs[n_acts + 2], refs[-1]
        total = dot(refs[0][...], attn_ref[...])
        row = 0
        for act in refs[1 : n_acts + 1]:
            total = total + dot(act[...], mlp_ref[row : row + act.shape[1], :])
            row += act.shape[1]
        if add is not None:
            total = total + refs[n_acts + 3][...].astype(jnp.float32)
        out_ref[...] = total.astype(out_ref.dtype)

    depth = w_attn_out.shape[0] + w_mlp_out.shape[0]
    out = jax.ShapeDtypeStruct((count, columns), kind)
    return pl.pallas_call(
        kernel,
        grid=(columns // tile,),
        in_specs=specs,
        out_specs=pl.BlockSpec((count, tile), lambda n: (0, n)),
        out_shape=out,
        compiler_params=params(),
        cost_estimate=cost(2 * count * columns * depth, out, w_attn_out, w_mlp_out),
        name="out_product",
    )(*operands)


def back_product(head_grads, mlp_grads, in_heads, in_mlp, start, count, add):
    features = in_heads.shape[0]
    tile = 512 if features % 512 == 0 else 256
    n_heads = len(head_grads)
    grads = [*head_grads, *mlp_grads]
    weights = [in_heads, *in_mlp]
    specs = [pl.BlockSpec((count, grad.shape[1]), lambda n: (start // count, 0)) for grad in grads]
    specs += [pl.BlockSpec((tile, weight.shape[1]), lambda n: (n, 0)) for weight in weights]
    operands = grads + weights
    if add is not None:
        operands.append(add)
        specs.append(pl.BlockSpec((count, tile), lambda n: (0, n)))

    def kernel(*refs):
        out_ref, heads_ref = refs[-1], refs[len(grads)]
        mlp_refs = refs[len(grads) + 1 : len(grads) + len(weights)]
        total, column = None, 0
        for grad in refs[:n_heads]:
            part = back_dot(grad[...], heads_ref[:, column : column + grad.shape[1]])
            total = part if total is None else total + part
            column += grad.shape[1]
        for grad, weight in zip(refs[n_heads : len(grads)], mlp_refs):
            total = total + back_dot(grad[...], weight[...])
        if add is not None:
            total = total + refs[-2][...].astype(jnp.float32)
        out_ref[...] = total.astype(out_ref.dtype)

    width = sum(grad.shape[1] for grad in grads)
    out = jax.ShapeDtypeStruct((count, features), jnp.bfloat16)
    return pl.pallas_call(
        kernel,
        grid=(features // tile,),
        in_specs=specs,
        out_specs=pl.BlockSpec((count, tile), lambda n: (0, n)),
        out_shape=out,
        compiler_params=params(),
        cost_estimate=cost(2 * count * features * width, out, *weights),
        name="back_product",
    )(*operands)


MLP_CUTS = (256, 512, 512, 256)


def body(layer_input, out_cotangent, w_query, w_key, w_value, w_mlp_in, w_attn_out, w_mlp_out):
    n_gx, n_gz = lax.axis_size("gx"), lax.axis_size("gz")
    own_rows, features = layer_input.shape
    count = own_rows * lax.axis_size("gy")

    def after(value, *earlier):
        return lax.optimization_barrier((value, earlier))[0]

    def others(part):
        if n_gz == 2:
            return trade(part, "gz", 1)
        return half(lax.psum(part.astype(jnp.float32), "gz") - part.astype(jnp.float32))

    def gather_parts(block):
        pair = jnp.stack([block, trade(block, "gx", 2)])
        near, far = trade(pair, "gy", 1), trade(pair, "gy", 2)
        parts = [pair, near, far, trade(far, "gy", 1)]
        return [(part, trade(part, "gx", 1)) for part in parts]

    def swap(packed):
        swapped = lax.all_to_all(packed, "gx", split_axis=0, concat_axis=0, tiled=True)
        return swapped.reshape(n_gx * packed.shape[1], packed.shape[2])

    heads_width = w_query.shape[1] // n_gx
    packed_heads = pack((w_query, w_key, w_value), n_gx, 0, heads_width, heads_width)
    starts = [sum(MLP_CUTS[:cut]) for cut in range(len(MLP_CUTS))]
    packed_mlp = [
        pack((w_mlp_in,), n_gx, start, width, 256) for start, width in zip(starts, MLP_CUTS)
    ]
    in_heads = swap(packed_heads)

    cot_owns = [
        cot_product(part, w_attn_out, w_mlp_out) for part in gather_parts(out_cotangent)
    ]
    cot_gots = [others(own) for own in cot_owns]

    wide = layer_input.astype(jnp.float32)
    total, squares = lax.psum((jnp.sum(wide, axis=1), jnp.sum(wide * wide, axis=1)), "gz")
    center = total / D
    spread = squares / D - center * center
    inverse = lax.rsqrt(spread + EPSILON)
    normed = (wide - center[:, None]) * inverse[:, None]
    all_in = assemble(gather_parts(half(normed)))

    heads_own = in_product(all_in, in_heads)
    heads_got = others(heads_own)
    in_mlp, mlp_own, mlp_got = [], [], []
    turn = (in_heads, *cot_owns)
    for cut in range(len(MLP_CUTS)):
        weight = swap(after(packed_mlp[cut], *turn))
        turn = (weight, mlp_own[-1] if mlp_own else heads_own)
        in_mlp.append(weight)
        mlp_own.append(in_product(all_in, weight))
        mlp_got.append(others(mlp_own[-1]))

    out_grad = add_parts(cot_owns, cot_gots)
    mixed, *head_grads = attend(heads_own, heads_got, out_grad)
    acts, mlp_grads = [], []
    for start, own, got in zip(starts, mlp_own, mlp_got):
        pre = wide_sum(own, got)
        acts.append(half(gelu(pre)))
        first = heads_width + start
        mlp_grads.append(gelu_back(pre, out_grad[:, first : first + own.shape[1]]))

    def forward_term(start, size, add, add_start, kind):
        return out_product(mixed, acts, w_attn_out, w_mlp_out, start, size, add, add_start, kind)

    def backward_term(start, size, add):
        return back_product(head_grads, mlp_grads, in_heads, in_mlp, start, size, add)

    def wider(value):
        return value.astype(jnp.float32)

    from_core = trade(forward_term(0, 2 * count, None, 0, jnp.bfloat16), "gx", 1)
    from_x = trade(forward_term(2 * count, count, from_core, 0, jnp.bfloat16), "gx", 2)
    mine = forward_term(3 * count, count, from_core, count, jnp.float32) + wider(from_x)
    mine = mine.reshape(2, 2, own_rows, features)
    pair = mine[:, 0] + wider(trade(half(mine[:, 1]), "gy", 1))
    summed = pair[0] + wider(trade(half(pair[1]), "gy", 2))
    layer_out = half(wide + summed)

    from_core = trade(backward_term(0, 2 * count, None), "gx", 1)
    both = backward_term(2 * count, 2 * count, from_core).reshape(2, 2, 2, own_rows, features)
    pair = wide_sum(both[:, :, 0], trade(both[:, :, 1], "gy", 1))
    ends = pair[:, 0] + wider(trade(half(pair[:, 1]), "gy", 2))
    normed_grad = ends[1] + wider(trade(half(ends[0]), "gx", 2))
    first, second = lax.psum(
        (jnp.sum(normed_grad, axis=1), jnp.sum(normed_grad * normed, axis=1)), "gz"
    )
    grad_full = out_cotangent.astype(jnp.float32) + inverse[:, None] * (
        normed_grad - (first / D)[:, None] - normed * (second / D)[:, None]
    )
    return (layer_out, half(grad_full))


def solution(mesh):
    in_specs = (
        P(("gx", "gy"), "gz"),
        P(("gx", "gy"), "gz"),
        P(("gz", "gx"), "gy"),
        P(("gz", "gx"), "gy"),
        P(("gz", "gx"), "gy"),
        P(("gz", "gx"), "gy"),
        P(("gy", "gx"), "gz"),
        P(("gy", "gx"), "gz"),
    )
    out_specs = (P(("gx", "gy"), "gz"), P(("gx", "gy"), "gz"))
    return jax.shard_map(body, mesh=mesh, in_specs=in_specs, out_specs=out_specs, check_vma=False)
```

```python
import functools
import math

import jax
import jax.numpy as jnp
from jax import lax
from jax.experimental import pallas as pl
from jax.experimental.pallas import tpu as pltpu
from jax.sharding import PartitionSpec as P

D = 6144
HEAD_DIM = 128
IMG_TOK = 256


EPSILON = 1e-06
ROOT_HALF = 0.7071067811865476
ROOT_TWO_PI_INV = 0.3989422804014327


def attend_kernel(
    q_own, q_got, k_own, k_got, v_own, v_got, g_ref, mixed_ref, dq_ref, dk_ref, dv_ref, *, scale
):
    def total(own, got):
        return own[...].astype(jnp.float32) + got[...].astype(jnp.float32)

    def norm(values):
        center = values - jnp.mean(values, axis=-1, keepdims=True)
        spread = jnp.mean(center * center, axis=-1, keepdims=True)
        inverse = lax.rsqrt(spread + EPSILON)
        return center * inverse, inverse

    def norm_back(grad, normed, inverse):
        slope = inverse * (grad - normed * jnp.mean(grad * normed, axis=-1, keepdims=True))
        return (slope - jnp.mean(slope, axis=-1, keepdims=True)).astype(jnp.bfloat16)

    def contract(left, right, left_dim, right_dim):
        return lax.dot_general(
            left,
            right,
            (((left_dim,), (right_dim,)), ((), ())),
            preferred_element_type=jnp.float32,
        )

    def half(values):
        return values.astype(jnp.bfloat16)

    q_norm, q_inverse = norm(total(q_own, q_got))
    k_norm, k_inverse = norm(total(k_own, k_got))
    q_half, k_half = half(q_norm), half(k_norm)
    v_half = half(total(v_own, v_got))
    grad = g_ref[...]
    weights = jnp.exp(contract(q_half, k_half, 1, 1) * scale)
    probs = weights / jnp.sum(weights, axis=-1, keepdims=True)
    probs_half = half(probs)
    mixed_ref[...] = half(contract(probs_half, v_half, 1, 0))
    dv_ref[...] = half(contract(probs_half, grad, 0, 0))
    probs_grad = half(contract(grad, v_half, 1, 1)).astype(jnp.float32)
    inner = jnp.sum(probs_grad * probs, axis=-1, keepdims=True)
    score_grad = half(probs * (probs_grad - inner) * scale)
    q_grad = half(contract(score_grad, k_half, 1, 0)).astype(jnp.float32)
    k_grad = half(contract(score_grad, q_half, 0, 0)).astype(jnp.float32)
    dq_ref[...] = norm_back(q_grad, q_norm, q_inverse)
    dk_ref[...] = norm_back(k_grad, k_norm, k_inverse)


def attend(own, got, grad):
    rows, width = own.shape[0], own.shape[1] // 3
    heads = width // HEAD_DIM

    def block(part):
        return pl.BlockSpec((IMG_TOK, HEAD_DIM), lambda image, head: (image, part * heads + head))

    half = jax.ShapeDtypeStruct((rows, width), jnp.bfloat16)
    return pl.pallas_call(
        functools.partial(attend_kernel, scale=1.0 / math.sqrt(HEAD_DIM)),
        grid=(rows // IMG_TOK, heads),
        in_specs=[block(0), block(0), block(1), block(1), block(2), block(2), block(0)],
        out_specs=[block(0)] * 4,
        out_shape=[half] * 4,
        compiler_params=pltpu.CompilerParams(vmem_limit_bytes=32 * 1024 * 1024),
        cost_estimate=pl.CostEstimate(
            flops=12 * rows * IMG_TOK * width,
            bytes_accessed=24 * rows * width,
            transcendentals=rows * IMG_TOK * heads,
        ),
        name="attend",
    )(own, got, own, got, own, got, grad)


def gelu(pre):
    return pre * 0.5 * (1.0 + lax.erf(pre * ROOT_HALF))


def gelu_back(pre, grad_half):
    cdf = 0.5 * (1.0 + lax.erf(pre * ROOT_HALF))
    pdf = jnp.exp(-0.5 * pre * pre) * ROOT_TWO_PI_INV
    return (grad_half.astype(jnp.float32) * (cdf + pre * pdf)).astype(jnp.bfloat16)


def dot(left, right):
    return jnp.dot(left, right, preferred_element_type=jnp.float32)


def back_dot(left, right):
    return lax.dot_general(
        left, right, (((1,), (1,)), ((), ())), preferred_element_type=jnp.float32
    )


def half(values):
    return values.astype(jnp.bfloat16)


def wide_sum(own, got):
    return own.astype(jnp.float32) + got.astype(jnp.float32)


def trade(block, axis, bit):
    pairs = [(index, index ^ bit) for index in range(lax.axis_size(axis))]
    return lax.ppermute(block, axis, pairs)


VMEM_LIMIT = 48 * 1024 * 1024


def params():
    return pltpu.CompilerParams(vmem_limit_bytes=VMEM_LIMIT)


def cost(flops, *arrays):
    moved = sum(math.prod(array.shape) * array.dtype.itemsize for array in arrays)
    return pl.CostEstimate(flops=flops, bytes_accessed=moved, transcendentals=0)


def pack_kernel(*refs):
    out_ref, start = refs[-1], 0
    for ref in refs[:-1]:
        out_ref[0, :, start : start + ref.shape[1]] = ref[...]
        start += ref.shape[1]


def pack(weights, owners, start, width, tile):
    rows, columns = weights[0].shape
    first, blocks = start // tile, columns // owners // tile
    out = jax.ShapeDtypeStruct((owners, rows, len(weights) * width), weights[0].dtype)
    spec = pl.BlockSpec((rows, tile), lambda owner, n: (0, owner * blocks + first + n))
    return pl.pallas_call(
        pack_kernel,
        grid=(owners, width // tile),
        in_specs=[spec] * len(weights),
        out_specs=pl.BlockSpec((1, rows, len(weights) * tile), lambda owner, n: (owner, 0, n)),
        out_shape=out,
        compiler_params=params(),
        cost_estimate=cost(0, out, out),
        name="pack",
    )(*weights)


IMAGE_ORDER = ((1, 1), (0, 1), (1, 0), (0, 0))


def assemble_kernel(*refs):
    parts, out_ref = refs[:-1], refs[-1]
    rows = parts[0].shape[1]
    start = 0
    for x_bit, core_bit in IMAGE_ORDER:
        for part in range(len(parts) // 2):
            out_ref[start : start + rows, :] = parts[2 * part + core_bit][x_bit]
            start += rows


def assemble(parts):
    flat = [value for part in parts for value in part]
    _, rows, features = flat[0].shape
    tile = 768
    out = jax.ShapeDtypeStruct((len(flat) * 2 * rows, features), flat[0].dtype)
    return pl.pallas_call(
        assemble_kernel,
        grid=(features // tile,),
        in_specs=[pl.BlockSpec((2, rows, tile), lambda n: (0, 0, n))] * len(flat),
        out_specs=pl.BlockSpec((out.shape[0], tile), lambda n: (0, n)),
        out_shape=out,
        compiler_params=params(),
        cost_estimate=cost(0, out, out),
        name="assemble",
    )(*flat)


def cot_kernel(own_ref, other_ref, attn_ref, mlp_ref, out_ref, rows_ref):
    rows = own_ref.shape[1]
    step = pl.program_id(0)

    @pl.when(step == 0)
    def _():
        for place, (x_bit, core_bit) in enumerate(IMAGE_ORDER):
            part = other_ref if core_bit else own_ref
            rows_ref[place * rows : (place + 1) * rows, :] = part[x_bit]
        out_ref[...] = half(back_dot(rows_ref[...], attn_ref[...]))

    @pl.when(step > 0)
    def _():
        out_ref[...] = half(back_dot(rows_ref[...], mlp_ref[...]))


def cot_product(part, w_attn_out, w_mlp_out):
    own, other = part
    _, rows, features = own.shape
    tile = w_attn_out.shape[0]
    columns = tile + w_mlp_out.shape[0]
    count = len(IMAGE_ORDER) * rows
    out = jax.ShapeDtypeStruct((count, columns), jnp.bfloat16)
    whole = pl.BlockSpec(own.shape, lambda n: (0, 0, 0))
    return pl.pallas_call(
        cot_kernel,
        grid=(columns // tile,),
        in_specs=[
            whole,
            whole,
            pl.BlockSpec((tile, features), lambda n: (0, 0)),
            pl.BlockSpec((tile, features), lambda n: (jnp.maximum(n - 1, 0), 0)),
        ],
        out_specs=pl.BlockSpec((count, tile), lambda n: (0, n)),
        out_shape=out,
        scratch_shapes=[pltpu.VMEM((count, features), jnp.bfloat16)],
        compiler_params=params(),
        cost_estimate=cost(2 * count * columns * features, out, w_attn_out, w_mlp_out),
        name="cot_product",
    )(own, other, w_attn_out, w_mlp_out)


def add_kernel(*refs):
    terms, out_ref = refs[:-1], refs[-1]
    count = len(terms) // 2
    for part in range(count):
        out_ref[0, part] = half(wide_sum(terms[part][0], terms[count + part][0]))


def add_parts(owns, gots):
    images, parts = len(IMAGE_ORDER), len(owns)
    rows, columns = owns[0].shape[0] // images, owns[0].shape[1]
    out = jax.ShapeDtypeStruct((images, parts, rows, columns), jnp.bfloat16)
    terms = [value.reshape(images, rows, columns) for value in (*owns, *gots)]
    added = pl.pallas_call(
        add_kernel,
        grid=(images,),
        in_specs=[pl.BlockSpec((1, rows, columns), lambda image: (image, 0, 0))] * len(terms),
        out_specs=pl.BlockSpec((1, parts, rows, columns), lambda image: (image, 0, 0, 0)),
        out_shape=out,
        compiler_params=params(),
        cost_estimate=cost(0, out, out, out),
        name="add_parts",
    )(*terms)
    return added.reshape(images * parts * rows, columns)


def in_kernel(rows_ref, weight_ref, out_ref):
    out_ref[...] = half(dot(rows_ref[...], weight_ref[...]))


def in_product(rows, weight):
    count, features = rows.shape
    columns = weight.shape[1]
    tile = 384 if columns % 384 == 0 else 256
    out = jax.ShapeDtypeStruct((count, columns), jnp.bfloat16)
    return pl.pallas_call(
        in_kernel,
        grid=(columns // tile,),
        in_specs=[
            pl.BlockSpec((count, features), lambda n: (0, 0)),
            pl.BlockSpec((features, tile), lambda n: (0, n)),
        ],
        out_specs=pl.BlockSpec((count, tile), lambda n: (0, n)),
        out_shape=out,
        compiler_params=params(),
        cost_estimate=cost(2 * count * columns * features, rows, out, weight),
        name="in_product",
    )(rows, weight)


def product(terms, weights, adds, start, count, kind, transposed):
    columns = weights[0].shape[0 if transposed else 1]
    tile = 512 if columns % 512 == 0 else 256
    specs = [
        pl.BlockSpec((count, value.shape[1]), lambda n: (start // count, 0))
        for value, _, _ in terms
    ]
    for weight in weights:
        if transposed:
            specs.append(pl.BlockSpec((tile, weight.shape[1]), lambda n: (n, 0)))
        else:
            specs.append(pl.BlockSpec((weight.shape[0], tile), lambda n: (0, n)))
    for _, first in adds:
        specs.append(pl.BlockSpec((count, tile), lambda n, place=first // count: (place, n)))

    def kernel(*refs):
        weight_refs = refs[len(terms) : len(terms) + len(weights)]
        total = None
        for ref, (value, index, offset) in zip(refs, terms):
            summed = slice(offset, offset + value.shape[1])
            if transposed:
                part = back_dot(ref[...], weight_refs[index][:, summed])
            else:
                part = dot(ref[...], weight_refs[index][summed, :])
            total = part if total is None else total + part
        for ref in refs[len(terms) + len(weights) : -1]:
            total = total + ref[...].astype(jnp.float32)
        refs[-1][...] = total.astype(kind)

    depth = sum(value.shape[1] for value, _, _ in terms)
    out = jax.ShapeDtypeStruct((count, columns), kind)
    return pl.pallas_call(
        kernel,
        grid=(columns // tile,),
        in_specs=specs,
        out_specs=pl.BlockSpec((count, tile), lambda n: (0, n)),
        out_shape=out,
        compiler_params=params(),
        cost_estimate=cost(2 * count * columns * depth, out, *weights),
        name="back_product" if transposed else "out_product",
    )(*(value for value, _, _ in terms), *weights, *(add for add, _ in adds))


MLP_CUTS = (256, 512, 512, 256)
EARLY_CUTS = 2


def body(layer_input, out_cotangent, w_query, w_key, w_value, w_mlp_in, w_attn_out, w_mlp_out):
    n_gx, n_gz = lax.axis_size("gx"), lax.axis_size("gz")
    own_rows, features = layer_input.shape
    count = own_rows * lax.axis_size("gy")

    def after(value, *earlier):
        return lax.optimization_barrier((value, earlier))[0]

    def others(part):
        if n_gz == 2:
            return trade(part, "gz", 1)
        return half(lax.psum(part.astype(jnp.float32), "gz") - part.astype(jnp.float32))

    def with_x(block):
        return jnp.stack([block, trade(block, "gx", 2)])

    def gather_parts(pair):
        near, far = trade(pair, "gy", 1), trade(pair, "gy", 2)
        parts = [pair, near, far, trade(far, "gy", 1)]
        return [(part, trade(part, "gx", 1)) for part in parts]

    def swap(packed):
        swapped = lax.all_to_all(packed, "gx", split_axis=0, concat_axis=0, tiled=True)
        return swapped.reshape(n_gx * packed.shape[1], packed.shape[2])

    heads_width = w_query.shape[1] // n_gx
    packed_heads = pack((w_query, w_key, w_value), n_gx, 0, heads_width, heads_width)
    starts = [sum(MLP_CUTS[:cut]) for cut in range(len(MLP_CUTS))]
    packed_mlp = [
        pack((w_mlp_in,), n_gx, start, width, 256) for start, width in zip(starts, MLP_CUTS)
    ]

    cot_pair = with_x(out_cotangent)
    in_mlp = [swap(after(packed_mlp[0], cot_pair))]

    wide = layer_input.astype(jnp.float32)
    total, squares = lax.psum((jnp.sum(wide, axis=1), jnp.sum(wide * wide, axis=1)), "gz")
    center = total / D
    spread = squares / D - center * center
    inverse = lax.rsqrt(spread + EPSILON)
    normed = (wide - center[:, None]) * inverse[:, None]
    normed_pair = with_x(half(normed))
    in_heads = swap(after(packed_heads, normed_pair, in_mlp[0]))

    cot_owns, cot_gots = [], []
    for place, (own, other) in enumerate(gather_parts(cot_pair)):
        if place >= 2:
            own = after(own, cot_gots[place - 2])
        cot_owns.append(cot_product((own, other), w_attn_out, w_mlp_out))
        cot_gots.append(others(cot_owns[-1]))

    all_in = assemble(gather_parts(normed_pair))
    mlp_own = [in_product(after(all_in, cot_gots[2]), in_mlp[0])]
    mlp_got = [others(mlp_own[0])]
    heads_own = in_product(after(all_in, cot_gots[3], mlp_own[0]), in_heads)
    heads_got = others(heads_own)
    in_mlp.append(swap(after(packed_mlp[1], in_heads, mlp_own[0])))
    mlp_own.append(in_product(after(all_in, mlp_got[0]), in_mlp[1]))
    mlp_got.append(others(mlp_own[1]))
    in_mlp.append(swap(after(packed_mlp[2], in_mlp[1], heads_own)))
    mlp_own.append(in_product(after(all_in, heads_got), in_mlp[2]))
    mlp_got.append(others(mlp_own[2]))
    in_mlp.append(swap(after(packed_mlp[3], in_mlp[2], mlp_own[1])))

    out_grad = add_parts(cot_owns, cot_gots)
    mixed, *head_grads = attend(heads_own, heads_got, out_grad)
    mlp_own.append(in_product(after(all_in, mlp_got[1], mixed), in_mlp[3]))
    mlp_got.append(others(mlp_own[3]))

    forward_terms, backward_terms = [(mixed, 0, 0)], []
    for index, grad in enumerate(head_grads):
        backward_terms.append((grad, 0, index * heads_width))

    def add_terms(cut, own):
        pre = wide_sum(own, mlp_got[cut])
        first = heads_width + starts[cut]
        grad = gelu_back(pre, out_grad[:, first : first + own.shape[1]])
        forward_terms.append((half(gelu(pre)), 1, starts[cut]))
        backward_terms.append((grad, 1 + cut, 0))

    out_weights, in_weights = [w_attn_out, w_mlp_out], [in_heads, *in_mlp]
    for cut in range(EARLY_CUTS):
        add_terms(cut, mlp_own[cut])
    rows = 4 * count
    forward_early = product(forward_terms, out_weights, [], 0, rows, jnp.bfloat16, False)
    backward_early = product(
        backward_terms, in_weights[: 1 + EARLY_CUTS], [], 0, rows, jnp.bfloat16, True
    )
    del forward_terms[:], backward_terms[:]
    for cut in range(EARLY_CUTS, len(MLP_CUTS)):
        add_terms(cut, after(mlp_own[cut], forward_early, backward_early))
    late_weights = in_weights[1 + EARLY_CUTS :]
    backward_terms = [
        (grad, index - 1 - EARLY_CUTS, offset) for grad, index, offset in backward_terms
    ]
    forward_terms = [(act, 0, offset) for act, _, offset in forward_terms]

    def forward_term(start, size, adds, kind):
        adds = [(forward_early, start), *adds]
        return product(forward_terms, [w_mlp_out], adds, start, size, kind, False)

    def backward_term(start, size, adds):
        adds = [(backward_early, start), *adds]
        return product(backward_terms, late_weights, adds, start, size, jnp.bfloat16, True)

    def wider(value):
        return value.astype(jnp.float32)

    from_core = trade(forward_term(0, 2 * count, [], jnp.bfloat16), "gx", 1)
    from_x = trade(forward_term(2 * count, count, [(from_core, 0)], jnp.bfloat16), "gx", 2)
    mine = forward_term(3 * count, count, [(from_core, count)], jnp.float32) + wider(from_x)
    mine = mine.reshape(2, 2, own_rows, features)
    pair = mine[:, 0] + wider(trade(half(mine[:, 1]), "gy", 1))
    summed = pair[0] + wider(trade(half(pair[1]), "gy", 2))
    layer_out = half(wide + summed)

    from_core = trade(backward_term(0, 2 * count, []), "gx", 1)
    both = backward_term(2 * count, 2 * count, [(from_core, 0)]).reshape(2, 2, 2, own_rows, features)
    pair = wide_sum(both[:, :, 0], trade(both[:, :, 1], "gy", 1))
    ends = pair[:, 0] + wider(trade(half(pair[:, 1]), "gy", 2))
    normed_grad = ends[1] + wider(trade(half(ends[0]), "gx", 2))
    first, second = lax.psum(
        (jnp.sum(normed_grad, axis=1), jnp.sum(normed_grad * normed, axis=1)), "gz"
    )
    grad_full = out_cotangent.astype(jnp.float32) + inverse[:, None] * (
        normed_grad - (first / D)[:, None] - normed * (second / D)[:, None]
    )
    return (layer_out, half(grad_full))


def solution(mesh):
    in_specs = (
        P(("gx", "gy"), "gz"),
        P(("gx", "gy"), "gz"),
        P(("gz", "gx"), "gy"),
        P(("gz", "gx"), "gy"),
        P(("gz", "gx"), "gy"),
        P(("gz", "gx"), "gy"),
        P(("gy", "gx"), "gz"),
        P(("gy", "gx"), "gz"),
    )
    out_specs = (P(("gx", "gy"), "gz"), P(("gx", "gy"), "gz"))
    return jax.shard_map(body, mesh=mesh, in_specs=in_specs, out_specs=out_specs, check_vma=False)
```

```python
import functools
import math

import jax
import jax.numpy as jnp
from jax import lax
from jax.experimental import pallas as pl
from jax.experimental.pallas import tpu as pltpu
from jax.sharding import PartitionSpec as P

D = 6144
HEAD_DIM = 128
IMG_TOK = 256


EPSILON = 1e-06
ROOT_HALF = 0.7071067811865476
ROOT_TWO_PI_INV = 0.3989422804014327


def attend_kernel(
    q_own, q_got, k_own, k_got, v_own, v_got, g_ref, mixed_ref, dq_ref, dk_ref, dv_ref, *, scale
):
    def total(own, got):
        return own[...].astype(jnp.float32) + got[...].astype(jnp.float32)

    def norm(values):
        center = values - jnp.mean(values, axis=-1, keepdims=True)
        spread = jnp.mean(center * center, axis=-1, keepdims=True)
        inverse = lax.rsqrt(spread + EPSILON)
        return center * inverse, inverse

    def norm_back(grad, normed, inverse):
        slope = inverse * (grad - normed * jnp.mean(grad * normed, axis=-1, keepdims=True))
        return (slope - jnp.mean(slope, axis=-1, keepdims=True)).astype(jnp.bfloat16)

    def contract(left, right, left_dim, right_dim):
        return lax.dot_general(
            left,
            right,
            (((left_dim,), (right_dim,)), ((), ())),
            preferred_element_type=jnp.float32,
        )

    def half(values):
        return values.astype(jnp.bfloat16)

    q_norm, q_inverse = norm(total(q_own, q_got))
    k_norm, k_inverse = norm(total(k_own, k_got))
    q_half, k_half = half(q_norm), half(k_norm)
    v_half = half(total(v_own, v_got))
    grad = g_ref[...]
    weights = jnp.exp(contract(q_half, k_half, 1, 1) * scale)
    probs = weights / jnp.sum(weights, axis=-1, keepdims=True)
    probs_half = half(probs)
    mixed_ref[...] = half(contract(probs_half, v_half, 1, 0))
    dv_ref[...] = half(contract(probs_half, grad, 0, 0))
    probs_grad = half(contract(grad, v_half, 1, 1)).astype(jnp.float32)
    inner = jnp.sum(probs_grad * probs, axis=-1, keepdims=True)
    score_grad = half(probs * (probs_grad - inner) * scale)
    q_grad = half(contract(score_grad, k_half, 1, 0)).astype(jnp.float32)
    k_grad = half(contract(score_grad, q_half, 0, 0)).astype(jnp.float32)
    dq_ref[...] = norm_back(q_grad, q_norm, q_inverse)
    dk_ref[...] = norm_back(k_grad, k_norm, k_inverse)


def attend(own, got, grad):
    rows, width = own.shape[0], own.shape[1] // 3
    heads = width // HEAD_DIM

    def block(part):
        return pl.BlockSpec((IMG_TOK, HEAD_DIM), lambda image, head: (image, part * heads + head))

    half = jax.ShapeDtypeStruct((rows, width), jnp.bfloat16)
    return pl.pallas_call(
        functools.partial(attend_kernel, scale=1.0 / math.sqrt(HEAD_DIM)),
        grid=(rows // IMG_TOK, heads),
        in_specs=[block(0), block(0), block(1), block(1), block(2), block(2), block(0)],
        out_specs=[block(0)] * 4,
        out_shape=[half] * 4,
        compiler_params=pltpu.CompilerParams(vmem_limit_bytes=32 * 1024 * 1024),
        cost_estimate=pl.CostEstimate(
            flops=rows * IMG_TOK * width // 8,
            bytes_accessed=rows * width // 4,
            transcendentals=0,
        ),
        name="attend",
    )(own, got, own, got, own, got, grad)


def gelu(pre):
    return pre * 0.5 * (1.0 + lax.erf(pre * ROOT_HALF))


def gelu_back(pre, grad_half):
    cdf = 0.5 * (1.0 + lax.erf(pre * ROOT_HALF))
    pdf = jnp.exp(-0.5 * pre * pre) * ROOT_TWO_PI_INV
    return (grad_half.astype(jnp.float32) * (cdf + pre * pdf)).astype(jnp.bfloat16)


def dot(left, right):
    return jnp.dot(left, right, preferred_element_type=jnp.float32)


def back_dot(left, right):
    return lax.dot_general(
        left, right, (((1,), (1,)), ((), ())), preferred_element_type=jnp.float32
    )


def half(values):
    return values.astype(jnp.bfloat16)


def wide_sum(own, got):
    return own.astype(jnp.float32) + got.astype(jnp.float32)


def trade(block, axis, bit):
    pairs = [(index, index ^ bit) for index in range(lax.axis_size(axis))]
    return lax.ppermute(block, axis, pairs)


VMEM_LIMIT = 48 * 1024 * 1024


def params():
    return pltpu.CompilerParams(vmem_limit_bytes=VMEM_LIMIT)


def cost(flops, *arrays):
    moved = sum(math.prod(array.shape) * array.dtype.itemsize for array in arrays)
    return pl.CostEstimate(flops=flops // 64, bytes_accessed=moved // 64, transcendentals=0)


def pack_kernel(*refs):
    out_ref, start = refs[-1], 0
    for ref in refs[:-1]:
        out_ref[0, :, start : start + ref.shape[1]] = ref[...]
        start += ref.shape[1]


def pack(weights, owners, start, width, tile):
    rows, columns = weights[0].shape
    first, blocks = start // tile, columns // owners // tile
    out = jax.ShapeDtypeStruct((owners, rows, len(weights) * width), weights[0].dtype)
    spec = pl.BlockSpec((rows, tile), lambda owner, n: (0, owner * blocks + first + n))
    return pl.pallas_call(
        pack_kernel,
        grid=(owners, width // tile),
        in_specs=[spec] * len(weights),
        out_specs=pl.BlockSpec((1, rows, len(weights) * tile), lambda owner, n: (owner, 0, n)),
        out_shape=out,
        compiler_params=params(),
        cost_estimate=cost(0, out, out),
        name="pack",
    )(*weights)


IMAGE_ORDER = ((1, 1), (0, 1), (1, 0), (0, 0))


def assemble_kernel(*refs):
    parts, out_ref = refs[:-1], refs[-1]
    rows = parts[0].shape[1]
    start = 0
    for x_bit, core_bit in IMAGE_ORDER:
        for part in range(len(parts) // 2):
            out_ref[start : start + rows, :] = parts[2 * part + core_bit][x_bit]
            start += rows


def assemble(parts):
    flat = [value for part in parts for value in part]
    _, rows, features = flat[0].shape
    tile = 768
    out = jax.ShapeDtypeStruct((len(flat) * 2 * rows, features), flat[0].dtype)
    return pl.pallas_call(
        assemble_kernel,
        grid=(features // tile,),
        in_specs=[pl.BlockSpec((2, rows, tile), lambda n: (0, 0, n))] * len(flat),
        out_specs=pl.BlockSpec((out.shape[0], tile), lambda n: (0, n)),
        out_shape=out,
        compiler_params=params(),
        cost_estimate=cost(0, out, out),
        name="assemble",
    )(*flat)


def cot_kernel(own_ref, other_ref, attn_ref, mlp_ref, out_ref, rows_ref):
    rows = own_ref.shape[1]
    step = pl.program_id(0)

    @pl.when(step == 0)
    def _():
        for place, (x_bit, core_bit) in enumerate(IMAGE_ORDER):
            part = other_ref if core_bit else own_ref
            rows_ref[place * rows : (place + 1) * rows, :] = part[x_bit]
        out_ref[...] = half(back_dot(rows_ref[...], attn_ref[...]))

    @pl.when(step > 0)
    def _():
        out_ref[...] = half(back_dot(rows_ref[...], mlp_ref[...]))


def cot_product(part, w_attn_out, w_mlp_out):
    own, other = part
    _, rows, features = own.shape
    tile = w_attn_out.shape[0]
    columns = tile + w_mlp_out.shape[0]
    count = len(IMAGE_ORDER) * rows
    out = jax.ShapeDtypeStruct((count, columns), jnp.bfloat16)
    whole = pl.BlockSpec(own.shape, lambda n: (0, 0, 0))
    return pl.pallas_call(
        cot_kernel,
        grid=(columns // tile,),
        in_specs=[
            whole,
            whole,
            pl.BlockSpec((tile, features), lambda n: (0, 0)),
            pl.BlockSpec((tile, features), lambda n: (jnp.maximum(n - 1, 0), 0)),
        ],
        out_specs=pl.BlockSpec((count, tile), lambda n: (0, n)),
        out_shape=out,
        scratch_shapes=[pltpu.VMEM((count, features), jnp.bfloat16)],
        compiler_params=params(),
        cost_estimate=cost(2 * count * columns * features, out, w_attn_out, w_mlp_out),
        name="cot_product",
    )(own, other, w_attn_out, w_mlp_out)


def add_kernel(*refs):
    terms, out_ref = refs[:-1], refs[-1]
    count = len(terms) // 2
    for part in range(count):
        out_ref[0, part] = half(wide_sum(terms[part][0], terms[count + part][0]))


def add_parts(owns, gots):
    images, parts = len(IMAGE_ORDER), len(owns)
    rows, columns = owns[0].shape[0] // images, owns[0].shape[1]
    out = jax.ShapeDtypeStruct((images, parts, rows, columns), jnp.bfloat16)
    terms = [value.reshape(images, rows, columns) for value in (*owns, *gots)]
    added = pl.pallas_call(
        add_kernel,
        grid=(images,),
        in_specs=[pl.BlockSpec((1, rows, columns), lambda image: (image, 0, 0))] * len(terms),
        out_specs=pl.BlockSpec((1, parts, rows, columns), lambda image: (image, 0, 0, 0)),
        out_shape=out,
        compiler_params=params(),
        cost_estimate=cost(0, out, out, out),
        name="add_parts",
    )(*terms)
    return added.reshape(images * parts * rows, columns)


def in_kernel(rows_ref, weight_ref, out_ref):
    out_ref[...] = half(dot(rows_ref[...], weight_ref[...]))


def in_product(rows, weight):
    count, features = rows.shape
    columns = weight.shape[1]
    tile = 384 if columns % 384 == 0 else 256
    out = jax.ShapeDtypeStruct((count, columns), jnp.bfloat16)
    return pl.pallas_call(
        in_kernel,
        grid=(columns // tile,),
        in_specs=[
            pl.BlockSpec((count, features), lambda n: (0, 0)),
            pl.BlockSpec((features, tile), lambda n: (0, n)),
        ],
        out_specs=pl.BlockSpec((count, tile), lambda n: (0, n)),
        out_shape=out,
        compiler_params=params(),
        cost_estimate=cost(2 * count * columns * features, rows, out, weight),
        name="in_product",
    )(rows, weight)


def product(terms, weights, adds, start, count, kind, transposed, window=None):
    whole = weights[0].shape[0 if transposed else 1]
    first_column, columns = window or (0, whole)
    tile = 512 if columns % 512 == 0 else 384 if columns % 384 == 0 else 256
    skip = first_column // tile
    specs = [
        pl.BlockSpec((count, value.shape[1]), lambda n: (start // count, 0))
        for value, _, _ in terms
    ]
    for weight in weights:
        if transposed:
            specs.append(pl.BlockSpec((tile, weight.shape[1]), lambda n: (n + skip, 0)))
        else:
            specs.append(pl.BlockSpec((weight.shape[0], tile), lambda n: (0, n + skip)))
    for _, first in adds:
        specs.append(
            pl.BlockSpec((count, tile), lambda n, place=first // count: (place, n + skip))
        )

    def kernel(*refs):
        weight_refs = refs[len(terms) : len(terms) + len(weights)]
        total = None
        for ref, (value, index, offset) in zip(refs, terms):
            summed = slice(offset, offset + value.shape[1])
            if transposed:
                part = back_dot(ref[...], weight_refs[index][:, summed])
            else:
                part = dot(ref[...], weight_refs[index][summed, :])
            total = part if total is None else total + part
        for ref in refs[len(terms) + len(weights) : -1]:
            total = total + ref[...].astype(jnp.float32)
        refs[-1][...] = total.astype(kind)

    depth = sum(value.shape[1] for value, _, _ in terms)
    out = jax.ShapeDtypeStruct((count, columns), kind)
    return pl.pallas_call(
        kernel,
        grid=(columns // tile,),
        in_specs=specs,
        out_specs=pl.BlockSpec((count, tile), lambda n: (0, n)),
        out_shape=out,
        compiler_params=params(),
        cost_estimate=cost(2 * count * columns * depth, out, *weights),
        name="back_product" if transposed else "out_product",
    )(*(value for value, _, _ in terms), *weights, *(add for add, _ in adds))


MLP_CUTS = (256, 512, 512, 256)
EARLY_CUTS = 2


def body(layer_input, out_cotangent, w_query, w_key, w_value, w_mlp_in, w_attn_out, w_mlp_out):
    n_gx, n_gz = lax.axis_size("gx"), lax.axis_size("gz")
    own_rows, features = layer_input.shape
    count = own_rows * lax.axis_size("gy")

    def after(value, *earlier):
        return lax.optimization_barrier((value, earlier))[0]

    def others(part):
        if n_gz == 2:
            return trade(part, "gz", 1)
        return half(lax.psum(part.astype(jnp.float32), "gz") - part.astype(jnp.float32))

    def with_x(block):
        return jnp.stack([block, trade(block, "gx", 2)])

    def gather_parts(pair):
        near, far = trade(pair, "gy", 1), trade(pair, "gy", 2)
        parts = [pair, near, far, trade(far, "gy", 1)]
        return [(part, trade(part, "gx", 1)) for part in parts]

    def swap(packed):
        swapped = lax.all_to_all(packed, "gx", split_axis=0, concat_axis=0, tiled=True)
        return swapped.reshape(n_gx * packed.shape[1], packed.shape[2])

    heads_width = w_query.shape[1] // n_gx
    packed_heads = pack((w_query, w_key, w_value), n_gx, 0, heads_width, heads_width)
    starts = [sum(MLP_CUTS[:cut]) for cut in range(len(MLP_CUTS))]
    packed_mlp = [
        pack((w_mlp_in,), n_gx, start, width, 256) for start, width in zip(starts, MLP_CUTS)
    ]

    cot_pair = with_x(out_cotangent)
    in_mlp = [swap(after(packed_mlp[0], cot_pair))]

    wide = layer_input.astype(jnp.float32)
    total, squares = lax.psum((jnp.sum(wide, axis=1), jnp.sum(wide * wide, axis=1)), "gz")
    center = total / D
    spread = squares / D - center * center
    inverse = lax.rsqrt(spread + EPSILON)
    normed = (wide - center[:, None]) * inverse[:, None]
    normed_pair = with_x(half(normed))
    in_heads = swap(after(packed_heads, normed_pair, in_mlp[0]))

    cot_owns, cot_gots = [], []
    for place, (own, other) in enumerate(gather_parts(cot_pair)):
        if place >= 2:
            own = after(own, cot_gots[place - 2])
        cot_owns.append(cot_product((own, other), w_attn_out, w_mlp_out))
        cot_gots.append(others(cot_owns[-1]))

    all_in = assemble(gather_parts(normed_pair))
    mlp_own = [in_product(after(all_in, cot_gots[2]), in_mlp[0])]
    mlp_got = [others(mlp_own[0])]
    heads_own = in_product(after(all_in, cot_gots[3], mlp_own[0]), in_heads)
    heads_got = others(heads_own)
    in_mlp.append(swap(after(packed_mlp[1], in_heads)))
    mlp_own.append(in_product(after(all_in, mlp_got[0]), in_mlp[1]))
    mlp_got.append(others(mlp_own[1]))
    in_mlp.append(swap(after(packed_mlp[2], in_mlp[1], mlp_own[0])))
    mlp_own.append(in_product(after(all_in, heads_got), in_mlp[2]))
    mlp_got.append(others(mlp_own[2]))
    in_mlp.append(swap(after(packed_mlp[3], in_mlp[2], heads_own)))

    out_grad = add_parts(cot_owns, cot_gots)
    mixed, *head_grads = attend(heads_own, heads_got, out_grad)
    mlp_own.append(in_product(after(all_in, mlp_got[1], mixed), in_mlp[3]))
    mlp_got.append(others(mlp_own[3]))

    forward_terms, backward_terms = [(mixed, 0, 0)], []
    for index, grad in enumerate(head_grads):
        backward_terms.append((grad, 0, index * heads_width))

    def add_terms(cut, own):
        pre = wide_sum(own, mlp_got[cut])
        first = heads_width + starts[cut]
        grad = gelu_back(pre, out_grad[:, first : first + own.shape[1]])
        forward_terms.append((half(gelu(pre)), 1, starts[cut]))
        backward_terms.append((grad, 1 + cut, 0))

    out_weights, in_weights = [w_attn_out, w_mlp_out], [in_heads, *in_mlp]
    for cut in range(EARLY_CUTS):
        add_terms(cut, mlp_own[cut])
    rows = 4 * count
    forward_early = product(forward_terms, out_weights, [], 0, rows, jnp.bfloat16, False)
    backward_early = product(
        backward_terms, in_weights[: 1 + EARLY_CUTS], [], 0, rows, jnp.bfloat16, True
    )
    del forward_terms[:], backward_terms[:]
    for cut in range(EARLY_CUTS, len(MLP_CUTS)):
        add_terms(cut, after(mlp_own[cut], forward_early, backward_early))
    late_weights = in_weights[1 + EARLY_CUTS :]
    backward_terms = [
        (grad, index - 1 - EARLY_CUTS, offset) for grad, index, offset in backward_terms
    ]
    forward_terms = [(act, 0, offset) for act, _, offset in forward_terms]

    def forward_term(start, size, adds, window=None):
        adds = [(forward_early, start), *adds]
        return product(
            forward_terms, [w_mlp_out], adds, start, size, jnp.bfloat16, False, window
        )

    def backward_term(start, size, adds, window=None):
        adds = [(backward_early, start), *adds]
        return product(
            backward_terms, late_weights, adds, start, size, jnp.bfloat16, True, window
        )

    def wider(value):
        return value.astype(jnp.float32)

    def spread_rows(term):
        half_width = features // 2
        low, high = (0, half_width), (half_width, half_width)
        from_core = trade(term(0, 2 * count, []), "gx", 1)
        from_x = trade(term(2 * count, count, [(from_core, 0)], low), "gx", 2)
        both = term(2 * count, 2 * count, [(from_core, 0)], high)
        both = both.reshape(2, 2, 2, own_rows, half_width)
        pair = wide_sum(both[:, :, 0], trade(both[:, :, 1], "gy", 1))
        ends = pair[:, 0] + wider(trade(half(pair[:, 1]), "gy", 2))
        high_sum = ends[1] + wider(trade(half(ends[0]), "gx", 2))
        mine = wide_sum(term(3 * count, count, [(from_core, count)], low), from_x)
        mine = mine.reshape(2, 2, own_rows, half_width)
        pair = mine[:, 0] + wider(trade(half(mine[:, 1]), "gy", 1))
        low_sum = pair[0] + wider(trade(half(pair[1]), "gy", 2))
        return jnp.concatenate([low_sum, high_sum], axis=1)

    layer_out = half(wide + spread_rows(forward_term))
    normed_grad = spread_rows(backward_term)
    first, second = lax.psum(
        (jnp.sum(normed_grad, axis=1), jnp.sum(normed_grad * normed, axis=1)), "gz"
    )
    grad_full = out_cotangent.astype(jnp.float32) + inverse[:, None] * (
        normed_grad - (first / D)[:, None] - normed * (second / D)[:, None]
    )
    return (layer_out, half(grad_full))


def solution(mesh):
    in_specs = (
        P(("gx", "gy"), "gz"),
        P(("gx", "gy"), "gz"),
        P(("gz", "gx"), "gy"),
        P(("gz", "gx"), "gy"),
        P(("gz", "gx"), "gy"),
        P(("gz", "gx"), "gy"),
        P(("gy", "gx"), "gz"),
        P(("gy", "gx"), "gz"),
    )
    out_specs = (P(("gx", "gy"), "gz"), P(("gx", "gy"), "gz"))
    return jax.shard_map(body, mesh=mesh, in_specs=in_specs, out_specs=out_specs, check_vma=False)
```

```python
import functools
import math

import jax
import jax.numpy as jnp
from jax import lax
from jax.experimental import pallas as pl
from jax.experimental.pallas import tpu as pltpu
from jax.sharding import PartitionSpec as P

D = 6144
HEAD_DIM = 128
IMG_TOK = 256


EPSILON = 1e-06
ROOT_HALF = 0.7071067811865476
ROOT_TWO_PI_INV = 0.3989422804014327


def attend_kernel(
    q_own, q_got, k_own, k_got, v_own, v_got, g_ref, mixed_ref, dq_ref, dk_ref, dv_ref, *, scale
):
    def total(own, got):
        return own[...].astype(jnp.float32) + got[...].astype(jnp.float32)

    def norm(values):
        center = values - jnp.mean(values, axis=-1, keepdims=True)
        spread = jnp.mean(center * center, axis=-1, keepdims=True)
        inverse = lax.rsqrt(spread + EPSILON)
        return center * inverse, inverse

    def norm_back(grad, normed, inverse):
        slope = inverse * (grad - normed * jnp.mean(grad * normed, axis=-1, keepdims=True))
        return (slope - jnp.mean(slope, axis=-1, keepdims=True)).astype(jnp.bfloat16)

    def contract(left, right, left_dim, right_dim):
        return lax.dot_general(
            left,
            right,
            (((left_dim,), (right_dim,)), ((), ())),
            preferred_element_type=jnp.float32,
        )

    def half(values):
        return values.astype(jnp.bfloat16)

    q_norm, q_inverse = norm(total(q_own, q_got))
    k_norm, k_inverse = norm(total(k_own, k_got))
    q_half, k_half = half(q_norm), half(k_norm)
    v_half = half(total(v_own, v_got))
    grad = g_ref[...]
    weights = jnp.exp(contract(q_half, k_half, 1, 1) * scale)
    probs = weights / jnp.sum(weights, axis=-1, keepdims=True)
    probs_half = half(probs)
    mixed_ref[...] = half(contract(probs_half, v_half, 1, 0))
    dv_ref[...] = half(contract(probs_half, grad, 0, 0))
    probs_grad = half(contract(grad, v_half, 1, 1)).astype(jnp.float32)
    inner = jnp.sum(probs_grad * probs, axis=-1, keepdims=True)
    score_grad = half(probs * (probs_grad - inner) * scale)
    q_grad = half(contract(score_grad, k_half, 1, 0)).astype(jnp.float32)
    k_grad = half(contract(score_grad, q_half, 0, 0)).astype(jnp.float32)
    dq_ref[...] = norm_back(q_grad, q_norm, q_inverse)
    dk_ref[...] = norm_back(k_grad, k_norm, k_inverse)


def attend(own, got, grad):
    rows, width = own.shape[0], own.shape[1] // 3
    heads = width // HEAD_DIM

    def block(part):
        return pl.BlockSpec((IMG_TOK, HEAD_DIM), lambda image, head: (image, part * heads + head))

    half = jax.ShapeDtypeStruct((rows, width), jnp.bfloat16)
    return pl.pallas_call(
        functools.partial(attend_kernel, scale=1.0 / math.sqrt(HEAD_DIM)),
        grid=(rows // IMG_TOK, heads),
        in_specs=[block(0), block(0), block(1), block(1), block(2), block(2), block(0)],
        out_specs=[block(0)] * 4,
        out_shape=[half] * 4,
        compiler_params=pltpu.CompilerParams(vmem_limit_bytes=32 * 1024 * 1024),
        cost_estimate=pl.CostEstimate(
            flops=rows * IMG_TOK * width // 8,
            bytes_accessed=rows * width // 4,
            transcendentals=0,
        ),
        name="attend",
    )(own, got, own, got, own, got, grad)


def gelu(pre):
    return pre * 0.5 * (1.0 + lax.erf(pre * ROOT_HALF))


def gelu_back(pre, grad_half):
    cdf = 0.5 * (1.0 + lax.erf(pre * ROOT_HALF))
    pdf = jnp.exp(-0.5 * pre * pre) * ROOT_TWO_PI_INV
    return (grad_half.astype(jnp.float32) * (cdf + pre * pdf)).astype(jnp.bfloat16)


def dot(left, right):
    return jnp.dot(left, right, preferred_element_type=jnp.float32)


def back_dot(left, right):
    return lax.dot_general(
        left, right, (((1,), (1,)), ((), ())), preferred_element_type=jnp.float32
    )


def half(values):
    return values.astype(jnp.bfloat16)


def wide_sum(own, got):
    return own.astype(jnp.float32) + got.astype(jnp.float32)


def trade(block, axis, bit):
    pairs = [(index, index ^ bit) for index in range(lax.axis_size(axis))]
    return lax.ppermute(block, axis, pairs)


VMEM_LIMIT = 48 * 1024 * 1024


def params():
    return pltpu.CompilerParams(vmem_limit_bytes=VMEM_LIMIT)


def cost(flops, *arrays):
    moved = sum(math.prod(array.shape) * array.dtype.itemsize for array in arrays)
    return pl.CostEstimate(flops=flops // 64, bytes_accessed=moved // 64, transcendentals=0)


def pack_kernel(*refs):
    out_ref, start = refs[-1], 0
    for ref in refs[:-1]:
        out_ref[0, :, start : start + ref.shape[1]] = ref[...]
        start += ref.shape[1]


def pack(weights, owners, start, width, tile):
    rows, columns = weights[0].shape
    first, blocks = start // tile, columns // owners // tile
    out = jax.ShapeDtypeStruct((owners, rows, len(weights) * width), weights[0].dtype)
    spec = pl.BlockSpec((rows, tile), lambda owner, n: (0, owner * blocks + first + n))
    return pl.pallas_call(
        pack_kernel,
        grid=(owners, width // tile),
        in_specs=[spec] * len(weights),
        out_specs=pl.BlockSpec((1, rows, len(weights) * tile), lambda owner, n: (owner, 0, n)),
        out_shape=out,
        compiler_params=params(),
        cost_estimate=cost(0, out, out),
        name="pack",
    )(*weights)


IMAGE_ORDER = ((1, 1), (0, 1), (1, 0), (0, 0))


def assemble_kernel(*refs):
    parts, out_ref = refs[:-1], refs[-1]
    rows = parts[0].shape[1]
    start = 0
    for x_bit, core_bit in IMAGE_ORDER:
        for part in range(len(parts) // 2):
            out_ref[start : start + rows, :] = parts[2 * part + core_bit][x_bit]
            start += rows


def assemble(parts):
    flat = [value for part in parts for value in part]
    _, rows, features = flat[0].shape
    tile = 768
    out = jax.ShapeDtypeStruct((len(flat) * 2 * rows, features), flat[0].dtype)
    return pl.pallas_call(
        assemble_kernel,
        grid=(features // tile,),
        in_specs=[pl.BlockSpec((2, rows, tile), lambda n: (0, 0, n))] * len(flat),
        out_specs=pl.BlockSpec((out.shape[0], tile), lambda n: (0, n)),
        out_shape=out,
        compiler_params=params(),
        cost_estimate=cost(0, out, out),
        name="assemble",
    )(*flat)


def cot_kernel(own_ref, other_ref, attn_ref, mlp_ref, out_ref, rows_ref):
    rows = own_ref.shape[1]
    step = pl.program_id(0)

    @pl.when(step == 0)
    def _():
        for place, (x_bit, core_bit) in enumerate(IMAGE_ORDER):
            part = other_ref if core_bit else own_ref
            rows_ref[place * rows : (place + 1) * rows, :] = part[x_bit]
        out_ref[...] = half(back_dot(rows_ref[...], attn_ref[...]))

    @pl.when(step > 0)
    def _():
        out_ref[...] = half(back_dot(rows_ref[...], mlp_ref[...]))


def cot_product(part, w_attn_out, w_mlp_out):
    own, other = part
    _, rows, features = own.shape
    tile = w_attn_out.shape[0]
    columns = tile + w_mlp_out.shape[0]
    count = len(IMAGE_ORDER) * rows
    out = jax.ShapeDtypeStruct((count, columns), jnp.bfloat16)
    whole = pl.BlockSpec(own.shape, lambda n: (0, 0, 0))
    return pl.pallas_call(
        cot_kernel,
        grid=(columns // tile,),
        in_specs=[
            whole,
            whole,
            pl.BlockSpec((tile, features), lambda n: (0, 0)),
            pl.BlockSpec((tile, features), lambda n: (jnp.maximum(n - 1, 0), 0)),
        ],
        out_specs=pl.BlockSpec((count, tile), lambda n: (0, n)),
        out_shape=out,
        scratch_shapes=[pltpu.VMEM((count, features), jnp.bfloat16)],
        compiler_params=params(),
        cost_estimate=cost(2 * count * columns * features, out, w_attn_out, w_mlp_out),
        name="cot_product",
    )(own, other, w_attn_out, w_mlp_out)


def add_kernel(*refs):
    terms, out_ref = refs[:-1], refs[-1]
    count = len(terms) // 2
    for part in range(count):
        out_ref[0, part] = half(wide_sum(terms[part][0], terms[count + part][0]))


def add_parts(owns, gots):
    images, parts = len(IMAGE_ORDER), len(owns)
    rows, columns = owns[0].shape[0] // images, owns[0].shape[1]
    out = jax.ShapeDtypeStruct((images, parts, rows, columns), jnp.bfloat16)
    terms = [value.reshape(images, rows, columns) for value in (*owns, *gots)]
    added = pl.pallas_call(
        add_kernel,
        grid=(images,),
        in_specs=[pl.BlockSpec((1, rows, columns), lambda image: (image, 0, 0))] * len(terms),
        out_specs=pl.BlockSpec((1, parts, rows, columns), lambda image: (image, 0, 0, 0)),
        out_shape=out,
        compiler_params=params(),
        cost_estimate=cost(0, out, out, out),
        name="add_parts",
    )(*terms)
    return added.reshape(images * parts * rows, columns)


def in_kernel(rows_ref, weight_ref, out_ref):
    out_ref[...] = half(dot(rows_ref[...], weight_ref[...]))


def in_product(rows, weight):
    count, features = rows.shape
    columns = weight.shape[1]
    tile = 384 if columns % 384 == 0 else 256
    out = jax.ShapeDtypeStruct((count, columns), jnp.bfloat16)
    return pl.pallas_call(
        in_kernel,
        grid=(columns // tile,),
        in_specs=[
            pl.BlockSpec((count, features), lambda n: (0, 0)),
            pl.BlockSpec((features, tile), lambda n: (0, n)),
        ],
        out_specs=pl.BlockSpec((count, tile), lambda n: (0, n)),
        out_shape=out,
        compiler_params=params(),
        cost_estimate=cost(2 * count * columns * features, rows, out, weight),
        name="in_product",
    )(rows, weight)


def product(terms, weights, adds, start, count, kind, transposed, window=None, rows=None):
    whole = weights[0].shape[0 if transposed else 1]
    first_column, columns = window or (0, whole)
    tile = 512 if columns % 512 == 0 else 384 if columns % 384 == 0 else 256
    skip = first_column // tile
    specs = [
        pl.BlockSpec((count, value.shape[1]), lambda n: (start // count, 0))
        for value, _, _ in terms
    ]
    for weight in weights:
        if transposed:
            specs.append(pl.BlockSpec((tile, weight.shape[1]), lambda n: (n + skip, 0)))
        else:
            block, size = rows or (0, weight.shape[0])
            specs.append(pl.BlockSpec((size, tile), lambda n, block=block: (block, n + skip)))
    for _, first in adds:
        specs.append(
            pl.BlockSpec((count, tile), lambda n, place=first // count: (place, n + skip))
        )

    def kernel(*refs):
        weight_refs = refs[len(terms) : len(terms) + len(weights)]
        total = None
        for ref, (value, index, offset) in zip(refs, terms):
            summed = slice(offset, offset + value.shape[1])
            if transposed:
                part = back_dot(ref[...], weight_refs[index][:, summed])
            else:
                part = dot(ref[...], weight_refs[index][summed, :])
            total = part if total is None else total + part
        for ref in refs[len(terms) + len(weights) : -1]:
            total = total + ref[...].astype(jnp.float32)
        refs[-1][...] = total.astype(kind)

    depth = sum(value.shape[1] for value, _, _ in terms)
    out = jax.ShapeDtypeStruct((count, columns), kind)
    return pl.pallas_call(
        kernel,
        grid=(columns // tile,),
        in_specs=specs,
        out_specs=pl.BlockSpec((count, tile), lambda n: (0, n)),
        out_shape=out,
        compiler_params=params(),
        cost_estimate=cost(2 * count * columns * depth, out, *weights),
        name="back_product" if transposed else "out_product",
    )(*(value for value, _, _ in terms), *weights, *(add for add, _ in adds))


MLP_CUTS = (256, 512, 512, 256)
EARLY_CUTS = 2


def body(layer_input, out_cotangent, w_query, w_key, w_value, w_mlp_in, w_attn_out, w_mlp_out):
    n_gx, n_gz = lax.axis_size("gx"), lax.axis_size("gz")
    own_rows, features = layer_input.shape
    count = own_rows * lax.axis_size("gy")

    def after(value, *earlier):
        return lax.optimization_barrier((value, earlier))[0]

    def others(part):
        if n_gz == 2:
            return trade(part, "gz", 1)
        return half(lax.psum(part.astype(jnp.float32), "gz") - part.astype(jnp.float32))

    def with_x(block):
        return jnp.stack([block, trade(block, "gx", 2)])

    def gather_parts(pair):
        near, far = trade(pair, "gy", 1), trade(pair, "gy", 2)
        parts = [pair, near, far, trade(far, "gy", 1)]
        return [(part, trade(part, "gx", 1)) for part in parts]

    def swap(packed):
        swapped = lax.all_to_all(packed, "gx", split_axis=0, concat_axis=0, tiled=True)
        return swapped.reshape(n_gx * packed.shape[1], packed.shape[2])

    heads_width = w_query.shape[1] // n_gx
    packed_heads = pack((w_query, w_key, w_value), n_gx, 0, heads_width, heads_width)
    starts = [sum(MLP_CUTS[:cut]) for cut in range(len(MLP_CUTS))]
    packed_mlp = [
        pack((w_mlp_in,), n_gx, start, width, 256) for start, width in zip(starts, MLP_CUTS)
    ]

    cot_pair = with_x(out_cotangent)
    wide = layer_input.astype(jnp.float32)
    total, squares = lax.psum((jnp.sum(wide, axis=1), jnp.sum(wide * wide, axis=1)), "gz")
    center = total / D
    spread = squares / D - center * center
    inverse = lax.rsqrt(spread + EPSILON)
    normed = (wide - center[:, None]) * inverse[:, None]
    normed_pair = with_x(half(normed))

    cot_owns, cot_gots = [], []
    for place, (own, other) in enumerate(gather_parts(cot_pair)):
        if place >= 2:
            own = after(own, cot_gots[place - 2])
        cot_owns.append(cot_product((own, other), w_attn_out, w_mlp_out))
        cot_gots.append(others(cot_owns[-1]))
    all_in = assemble(gather_parts(normed_pair))

    in_heads = swap(after(packed_heads, normed_pair, cot_owns[0]))
    in_mlp = [swap(after(packed_mlp[0], in_heads, cot_owns[2]))]
    in_mlp.append(swap(after(packed_mlp[1], in_mlp[0], cot_owns[3])))
    heads_own = in_product(after(all_in, cot_gots[2]), in_heads)
    heads_got = others(heads_own)
    mlp_own = [in_product(after(all_in, cot_gots[3], heads_own), in_mlp[0])]
    mlp_got = [others(mlp_own[0])]
    in_mlp.append(swap(after(packed_mlp[2], in_mlp[1], heads_own)))
    mlp_own.append(in_product(after(all_in, mlp_own[0]), in_mlp[1]))
    mlp_got.append(others(mlp_own[1]))
    in_mlp.append(swap(after(packed_mlp[3], in_mlp[2], mlp_own[0])))
    mlp_own.append(in_product(after(all_in, heads_got), in_mlp[2]))
    mlp_got.append(others(mlp_own[2]))

    out_grad = add_parts(cot_owns, cot_gots)
    mixed, *head_grads = attend(heads_own, heads_got, out_grad)
    mlp_own.append(in_product(after(all_in, mlp_got[0], mixed), in_mlp[3]))
    mlp_got.append(others(mlp_own[3]))

    forward_terms, backward_terms = [(mixed, 0, 0)], []
    for index, grad in enumerate(head_grads):
        backward_terms.append((grad, 0, index * heads_width))

    def add_terms(cut, own):
        pre = wide_sum(own, mlp_got[cut])
        first = heads_width + starts[cut]
        grad = gelu_back(pre, out_grad[:, first : first + own.shape[1]])
        forward_terms.append((half(gelu(pre)), 1, starts[cut]))
        backward_terms.append((grad, 1 + cut, 0))

    out_weights, in_weights = [w_attn_out, w_mlp_out], [in_heads, *in_mlp]
    for cut in range(EARLY_CUTS):
        add_terms(cut, mlp_own[cut])
    rows = 4 * count
    forward_early = product(forward_terms, out_weights, [], 0, rows, jnp.bfloat16, False)
    backward_early = product(
        backward_terms, in_weights[: 1 + EARLY_CUTS], [], 0, rows, jnp.bfloat16, True
    )
    del forward_terms[:], backward_terms[:]
    for cut in range(EARLY_CUTS, len(MLP_CUTS)):
        add_terms(cut, after(mlp_own[cut], forward_early, backward_early))
    late_weights = in_weights[1 + EARLY_CUTS :]
    backward_terms = [
        (grad, index - 1 - EARLY_CUTS, offset) for grad, index, offset in backward_terms
    ]
    early, all_columns = starts[EARLY_CUTS], sum(MLP_CUTS)
    late_rows = (early // (all_columns - early), all_columns - early)
    forward_terms = [(act, 0, offset - early) for act, _, offset in forward_terms]

    def forward_term(start, size, adds, window=None):
        adds = [(forward_early, start), *adds]
        return product(
            forward_terms, [w_mlp_out], adds, start, size, jnp.bfloat16, False, window, late_rows
        )

    def backward_term(start, size, adds, window=None):
        adds = [(backward_early, start), *adds]
        return product(
            backward_terms, late_weights, adds, start, size, jnp.bfloat16, True, window
        )

    def wider(value):
        return value.astype(jnp.float32)

    def over_x_z(term, from_core, window):
        from_x = trade(term(2 * count, count, [(from_core, 0)], window), "gx", 2)
        mine = wide_sum(term(3 * count, count, [(from_core, count)], window), from_x)
        mine = mine.reshape(2, 2, own_rows, window[1])
        pair = mine[:, 0] + wider(trade(half(mine[:, 1]), "gy", 1))
        return pair[0] + wider(trade(half(pair[1]), "gy", 2))

    def over_z_x(term, from_core, window):
        both = term(2 * count, 2 * count, [(from_core, 0)], window)
        both = both.reshape(2, 2, 2, own_rows, window[1])
        pair = wide_sum(both[:, :, 0], trade(both[:, :, 1], "gy", 1))
        ends = pair[:, 0] + wider(trade(half(pair[:, 1]), "gy", 2))
        return ends[1] + wider(trade(half(ends[0]), "gx", 2))

    def spread_rows(term, ways):
        width = features // len(ways)
        from_core = trade(term(0, 2 * count, []), "gx", 1)
        sums = [way(term, from_core, (place * width, width)) for place, way in enumerate(ways)]
        return jnp.concatenate(sums, axis=1)

    normed_grad = spread_rows(backward_term, (over_x_z, over_z_x))
    layer_out = half(wide + spread_rows(forward_term, (over_x_z, over_x_z)))
    first, second = lax.psum(
        (jnp.sum(normed_grad, axis=1), jnp.sum(normed_grad * normed, axis=1)), "gz"
    )
    grad_full = out_cotangent.astype(jnp.float32) + inverse[:, None] * (
        normed_grad - (first / D)[:, None] - normed * (second / D)[:, None]
    )
    return (layer_out, half(grad_full))


def solution(mesh):
    in_specs = (
        P(("gx", "gy"), "gz"),
        P(("gx", "gy"), "gz"),
        P(("gz", "gx"), "gy"),
        P(("gz", "gx"), "gy"),
        P(("gz", "gx"), "gy"),
        P(("gz", "gx"), "gy"),
        P(("gy", "gx"), "gz"),
        P(("gy", "gx"), "gz"),
    )
    out_specs = (P(("gx", "gy"), "gz"), P(("gx", "gy"), "gz"))
    return jax.shard_map(body, mesh=mesh, in_specs=in_specs, out_specs=out_specs, check_vma=False)
```

```python
import functools
import math

import jax
import jax.numpy as jnp
from jax import lax
from jax.experimental import pallas as pl
from jax.experimental.pallas import tpu as pltpu
from jax.sharding import PartitionSpec as P

D = 6144
HEAD_DIM = 128
IMG_TOK = 256


EPSILON = 1e-06
ROOT_HALF = 0.7071067811865476
ROOT_TWO_PI_INV = 0.3989422804014327


def attend_kernel(
    q_own, q_got, k_own, k_got, v_own, v_got, g_ref, mixed_ref, dq_ref, dk_ref, dv_ref, *, scale
):
    def total(own, got):
        return own[...].astype(jnp.float32) + got[...].astype(jnp.float32)

    def norm(values):
        center = values - jnp.mean(values, axis=-1, keepdims=True)
        spread = jnp.mean(center * center, axis=-1, keepdims=True)
        inverse = lax.rsqrt(spread + EPSILON)
        return center * inverse, inverse

    def norm_back(grad, normed, inverse):
        slope = inverse * (grad - normed * jnp.mean(grad * normed, axis=-1, keepdims=True))
        return (slope - jnp.mean(slope, axis=-1, keepdims=True)).astype(jnp.bfloat16)

    def contract(left, right, left_dim, right_dim):
        return lax.dot_general(
            left,
            right,
            (((left_dim,), (right_dim,)), ((), ())),
            preferred_element_type=jnp.float32,
        )

    def half(values):
        return values.astype(jnp.bfloat16)

    q_norm, q_inverse = norm(total(q_own, q_got))
    k_norm, k_inverse = norm(total(k_own, k_got))
    q_half, k_half = half(q_norm), half(k_norm)
    v_half = half(total(v_own, v_got))
    grad = g_ref[...]
    weights = jnp.exp(contract(q_half, k_half, 1, 1) * scale)
    probs = weights / jnp.sum(weights, axis=-1, keepdims=True)
    probs_half = half(probs)
    mixed_ref[...] = half(contract(probs_half, v_half, 1, 0))
    dv_ref[...] = half(contract(probs_half, grad, 0, 0))
    probs_grad = half(contract(grad, v_half, 1, 1)).astype(jnp.float32)
    inner = jnp.sum(probs_grad * probs, axis=-1, keepdims=True)
    score_grad = half(probs * (probs_grad - inner) * scale)
    q_grad = half(contract(score_grad, k_half, 1, 0)).astype(jnp.float32)
    k_grad = half(contract(score_grad, q_half, 0, 0)).astype(jnp.float32)
    dq_ref[...] = norm_back(q_grad, q_norm, q_inverse)
    dk_ref[...] = norm_back(k_grad, k_norm, k_inverse)


def attend(own, got, grad):
    rows, width = own.shape[0], own.shape[1] // 3
    heads = width // HEAD_DIM

    def block(part):
        return pl.BlockSpec((IMG_TOK, HEAD_DIM), lambda image, head: (image, part * heads + head))

    half = jax.ShapeDtypeStruct((rows, width), jnp.bfloat16)
    return pl.pallas_call(
        functools.partial(attend_kernel, scale=1.0 / math.sqrt(HEAD_DIM)),
        grid=(rows // IMG_TOK, heads),
        in_specs=[block(0), block(0), block(1), block(1), block(2), block(2), block(0)],
        out_specs=[block(0)] * 4,
        out_shape=[half] * 4,
        compiler_params=pltpu.CompilerParams(vmem_limit_bytes=32 * 1024 * 1024),
        cost_estimate=pl.CostEstimate(
            flops=rows * IMG_TOK * width // 8,
            bytes_accessed=rows * width // 4,
            transcendentals=0,
        ),
        name="attend",
    )(own, got, own, got, own, got, grad)


def gelu(pre):
    return pre * 0.5 * (1.0 + lax.erf(pre * ROOT_HALF))


def gelu_back(pre, grad_half):
    cdf = 0.5 * (1.0 + lax.erf(pre * ROOT_HALF))
    pdf = jnp.exp(-0.5 * pre * pre) * ROOT_TWO_PI_INV
    return (grad_half.astype(jnp.float32) * (cdf + pre * pdf)).astype(jnp.bfloat16)


def dot(left, right):
    return jnp.dot(left, right, preferred_element_type=jnp.float32)


def back_dot(left, right):
    return lax.dot_general(
        left, right, (((1,), (1,)), ((), ())), preferred_element_type=jnp.float32
    )


def half(values):
    return values.astype(jnp.bfloat16)


def wide_sum(own, got):
    return own.astype(jnp.float32) + got.astype(jnp.float32)


def trade(block, axis, bit):
    pairs = [(index, index ^ bit) for index in range(lax.axis_size(axis))]
    return lax.ppermute(block, axis, pairs)


VMEM_LIMIT = 48 * 1024 * 1024


def params():
    return pltpu.CompilerParams(vmem_limit_bytes=VMEM_LIMIT)


def cost(flops, *arrays):
    moved = sum(math.prod(array.shape) * array.dtype.itemsize for array in arrays)
    return pl.CostEstimate(flops=flops // 64, bytes_accessed=moved // 64, transcendentals=0)


def pack_kernel(*refs):
    out_ref, start = refs[-1], 0
    for ref in refs[:-1]:
        out_ref[0, :, start : start + ref.shape[1]] = ref[...]
        start += ref.shape[1]


def pack(weights, owners, start, width, tile):
    rows, columns = weights[0].shape
    first, blocks = start // tile, columns // owners // tile
    out = jax.ShapeDtypeStruct((owners, rows, len(weights) * width), weights[0].dtype)
    spec = pl.BlockSpec((rows, tile), lambda owner, n: (0, owner * blocks + first + n))
    return pl.pallas_call(
        pack_kernel,
        grid=(owners, width // tile),
        in_specs=[spec] * len(weights),
        out_specs=pl.BlockSpec((1, rows, len(weights) * tile), lambda owner, n: (owner, 0, n)),
        out_shape=out,
        compiler_params=params(),
        cost_estimate=cost(0, out, out),
        name="pack",
    )(*weights)


IMAGE_ORDER = ((1, 1), (0, 1), (1, 0), (0, 0))


def copy_kernel(index_ref, value_ref, out_ref):
    out_ref[...] = value_ref[...]


def pick_rows(value, index):
    block = (value.shape[0] // index.shape[0], value.shape[1])
    return pl.pallas_call(
        copy_kernel,
        grid_spec=pltpu.PrefetchScalarGridSpec(
            num_scalar_prefetch=1,
            grid=index.shape,
            in_specs=[pl.BlockSpec(block, lambda i, index: (index[i], 0))],
            out_specs=pl.BlockSpec(block, lambda i, index: (i, 0)),
        ),
        out_shape=jax.ShapeDtypeStruct(value.shape, value.dtype),
        compiler_params=params(),
        cost_estimate=cost(0, value, value),
        name="pick_rows",
    )(index, value)


def cot_kernel(own_ref, other_ref, attn_ref, mlp_ref, out_ref, rows_ref):
    rows = own_ref.shape[1]
    step = pl.program_id(0)

    @pl.when(step == 0)
    def _():
        for place, (x_bit, core_bit) in enumerate(IMAGE_ORDER):
            part = other_ref if core_bit else own_ref
            rows_ref[place * rows : (place + 1) * rows, :] = part[x_bit]
        out_ref[...] = half(back_dot(rows_ref[...], attn_ref[...]))

    @pl.when(step > 0)
    def _():
        out_ref[...] = half(back_dot(rows_ref[...], mlp_ref[...]))


def cot_product(part, w_attn_out, w_mlp_out):
    own, other = part
    _, rows, features = own.shape
    tile = w_attn_out.shape[0]
    columns = tile + w_mlp_out.shape[0]
    count = len(IMAGE_ORDER) * rows
    out = jax.ShapeDtypeStruct((count, columns), jnp.bfloat16)
    whole = pl.BlockSpec(own.shape, lambda n: (0, 0, 0))
    return pl.pallas_call(
        cot_kernel,
        grid=(columns // tile,),
        in_specs=[
            whole,
            whole,
            pl.BlockSpec((tile, features), lambda n: (0, 0)),
            pl.BlockSpec((tile, features), lambda n: (jnp.maximum(n - 1, 0), 0)),
        ],
        out_specs=pl.BlockSpec((count, tile), lambda n: (0, n)),
        out_shape=out,
        scratch_shapes=[pltpu.VMEM((count, features), jnp.bfloat16)],
        compiler_params=params(),
        cost_estimate=cost(2 * count * columns * features, out, w_attn_out, w_mlp_out),
        name="cot_product",
    )(own, other, w_attn_out, w_mlp_out)


def add_kernel(*refs):
    terms, out_ref = refs[:-1], refs[-1]
    count = len(terms) // 2
    for part in range(count):
        out_ref[0, part] = half(wide_sum(terms[part][0], terms[count + part][0]))


def add_parts(owns, gots):
    images, parts = len(IMAGE_ORDER), len(owns)
    rows, columns = owns[0].shape[0] // images, owns[0].shape[1]
    out = jax.ShapeDtypeStruct((images, parts, rows, columns), jnp.bfloat16)
    terms = [value.reshape(images, rows, columns) for value in (*owns, *gots)]
    added = pl.pallas_call(
        add_kernel,
        grid=(images,),
        in_specs=[pl.BlockSpec((1, rows, columns), lambda image: (image, 0, 0))] * len(terms),
        out_specs=pl.BlockSpec((1, parts, rows, columns), lambda image: (image, 0, 0, 0)),
        out_shape=out,
        compiler_params=params(),
        cost_estimate=cost(0, out, out, out),
        name="add_parts",
    )(*terms)
    return added.reshape(images * parts * rows, columns)


def in_kernel(rows_ref, weight_ref, out_ref):
    out_ref[...] = half(dot(rows_ref[...], weight_ref[...]))


def in_product(rows, weight):
    count, features = rows.shape
    columns = weight.shape[1]
    tile = 384 if columns % 384 == 0 else 256
    out = jax.ShapeDtypeStruct((count, columns), jnp.bfloat16)
    return pl.pallas_call(
        in_kernel,
        grid=(columns // tile,),
        in_specs=[
            pl.BlockSpec((count, features), lambda n: (0, 0)),
            pl.BlockSpec((features, tile), lambda n: (0, n)),
        ],
        out_specs=pl.BlockSpec((count, tile), lambda n: (0, n)),
        out_shape=out,
        compiler_params=params(),
        cost_estimate=cost(2 * count * columns * features, rows, out, weight),
        name="in_product",
    )(rows, weight)


def product(terms, weights, adds, start, count, kind, transposed, window=None, rows=None):
    whole = weights[0].shape[0 if transposed else 1]
    first_column, columns = window or (0, whole)
    tile = 512 if columns % 512 == 0 else 384 if columns % 384 == 0 else 256
    skip = first_column // tile
    specs = [
        pl.BlockSpec((count, value.shape[1]), lambda n: (start // count, 0))
        for value, _, _ in terms
    ]
    for weight in weights:
        if transposed:
            specs.append(pl.BlockSpec((tile, weight.shape[1]), lambda n: (n + skip, 0)))
        else:
            block, size = rows or (0, weight.shape[0])
            specs.append(pl.BlockSpec((size, tile), lambda n, block=block: (block, n + skip)))
    for _, first in adds:
        specs.append(
            pl.BlockSpec((count, tile), lambda n, place=first // count: (place, n + skip))
        )

    def kernel(*refs):
        weight_refs = refs[len(terms) : len(terms) + len(weights)]
        total = None
        for ref, (value, index, offset) in zip(refs, terms):
            summed = slice(offset, offset + value.shape[1])
            if transposed:
                part = back_dot(ref[...], weight_refs[index][:, summed])
            else:
                part = dot(ref[...], weight_refs[index][summed, :])
            total = part if total is None else total + part
        for ref in refs[len(terms) + len(weights) : -1]:
            total = total + ref[...].astype(jnp.float32)
        refs[-1][...] = total.astype(kind)

    depth = sum(value.shape[1] for value, _, _ in terms)
    out = jax.ShapeDtypeStruct((count, columns), kind)
    return pl.pallas_call(
        kernel,
        grid=(columns // tile,),
        in_specs=specs,
        out_specs=pl.BlockSpec((count, tile), lambda n: (0, n)),
        out_shape=out,
        compiler_params=params(),
        cost_estimate=cost(2 * count * columns * depth, out, *weights),
        name="back_product" if transposed else "out_product",
    )(*(value for value, _, _ in terms), *weights, *(add for add, _ in adds))


MLP_CUTS = (256, 512, 512, 256)
EARLY_CUTS = 2


def body(layer_input, out_cotangent, w_query, w_key, w_value, w_mlp_in, w_attn_out, w_mlp_out):
    n_gx, n_gz = lax.axis_size("gx"), lax.axis_size("gz")
    own_rows, features = layer_input.shape
    count = own_rows * lax.axis_size("gy")

    def after(value, *earlier):
        return lax.optimization_barrier((value, earlier))[0]

    def others(part):
        if n_gz == 2:
            return trade(part, "gz", 1)
        return half(lax.psum(part.astype(jnp.float32), "gz") - part.astype(jnp.float32))

    def with_x(block):
        return jnp.stack([block, trade(block, "gx", 2)])

    def gather_parts(pair):
        near, far = trade(pair, "gy", 1), trade(pair, "gy", 2)
        parts = [pair, near, far, trade(far, "gy", 1)]
        return [(part, trade(part, "gx", 1)) for part in parts]

    def swap(packed):
        swapped = lax.all_to_all(packed, "gx", split_axis=0, concat_axis=0, tiled=True)
        return swapped.reshape(n_gx * packed.shape[1], packed.shape[2])

    heads_width = w_query.shape[1] // n_gx
    packed_heads = pack((w_query, w_key, w_value), n_gx, 0, heads_width, heads_width)
    starts = [sum(MLP_CUTS[:cut]) for cut in range(len(MLP_CUTS))]
    packed_mlp = [
        pack((w_mlp_in,), n_gx, start, width, 256) for start, width in zip(starts, MLP_CUTS)
    ]

    cot_pair = with_x(out_cotangent)
    wide = layer_input.astype(jnp.float32)
    total, squares = lax.psum((jnp.sum(wide, axis=1), jnp.sum(wide * wide, axis=1)), "gz")
    center = total / D
    spread = squares / D - center * center
    inverse = lax.rsqrt(spread + EPSILON)
    normed = (wide - center[:, None]) * inverse[:, None]
    gathered = lax.all_gather(half(normed), ("gx", "gy"), axis=0, tiled=True)
    n_gy = lax.axis_size("gy")
    image_of = lax.axis_index("gx") ^ jnp.array([2 * x + core for x, core in IMAGE_ORDER])
    block_of = image_of[:, None] * n_gy + (lax.axis_index("gy") ^ jnp.arange(n_gy))[None, :]
    all_in = pick_rows(gathered, block_of.reshape(-1).astype(jnp.int32))

    cot_owns, cot_gots = [], []
    for place, (own, other) in enumerate(gather_parts(cot_pair)):
        if place >= 2:
            own = after(own, cot_gots[place - 2])
        cot_owns.append(cot_product((own, other), w_attn_out, w_mlp_out))
        cot_gots.append(others(cot_owns[-1]))

    in_heads = swap(after(packed_heads, cot_owns[0]))
    in_mlp = [swap(after(packed_mlp[0], in_heads, cot_owns[1]))]
    in_mlp.append(swap(after(packed_mlp[1], in_mlp[0], cot_owns[2], cot_owns[3])))
    heads_own = in_product(after(all_in, cot_gots[1]), in_heads)
    heads_got = others(heads_own)
    mlp_own = [in_product(after(all_in, cot_gots[2], heads_own), in_mlp[0])]
    mlp_got = [others(mlp_own[0])]
    in_mlp.append(swap(after(packed_mlp[2], in_mlp[1], heads_own)))
    mlp_own.append(in_product(after(all_in, cot_gots[3], mlp_own[0]), in_mlp[1]))
    mlp_got.append(others(mlp_own[1]))
    in_mlp.append(swap(after(packed_mlp[3], in_mlp[2], mlp_own[0])))
    mlp_own.append(in_product(after(all_in, heads_got), in_mlp[2]))
    mlp_got.append(others(mlp_own[2]))

    out_grad = add_parts(after(cot_owns, mlp_own[1]), cot_gots)
    mixed, *head_grads = attend(heads_own, heads_got, out_grad)
    mlp_own.append(in_product(after(all_in, mlp_got[0], mixed), in_mlp[3]))
    mlp_got.append(others(mlp_own[3]))

    forward_terms, backward_terms = [(mixed, 0, 0)], []
    for index, grad in enumerate(head_grads):
        backward_terms.append((grad, 0, index * heads_width))

    def add_terms(cut, own):
        pre = wide_sum(own, mlp_got[cut])
        first = heads_width + starts[cut]
        grad = gelu_back(pre, out_grad[:, first : first + own.shape[1]])
        forward_terms.append((half(gelu(pre)), 1, starts[cut]))
        backward_terms.append((grad, 1 + cut, 0))

    out_weights, in_weights = [w_attn_out, w_mlp_out], [in_heads, *in_mlp]
    for cut in range(EARLY_CUTS):
        add_terms(cut, mlp_own[cut])
    rows = 4 * count
    forward_early = product(forward_terms, out_weights, [], 0, rows, jnp.bfloat16, False)
    backward_early = product(
        backward_terms, in_weights[: 1 + EARLY_CUTS], [], 0, rows, jnp.bfloat16, True
    )
    del forward_terms[:], backward_terms[:]
    for cut in range(EARLY_CUTS, len(MLP_CUTS)):
        add_terms(cut, after(mlp_own[cut], forward_early, backward_early))
    late_weights = in_weights[1 + EARLY_CUTS :]
    backward_terms = [
        (grad, index - 1 - EARLY_CUTS, offset) for grad, index, offset in backward_terms
    ]
    early, all_columns = starts[EARLY_CUTS], sum(MLP_CUTS)
    late_rows = (early // (all_columns - early), all_columns - early)
    forward_terms = [(act, 0, offset - early) for act, _, offset in forward_terms]

    def forward_term(start, size, adds, window=None):
        adds = [(forward_early, start), *adds]
        return product(
            forward_terms, [w_mlp_out], adds, start, size, jnp.bfloat16, False, window, late_rows
        )

    def backward_term(start, size, adds, window=None):
        adds = [(backward_early, start), *adds]
        return product(
            backward_terms, late_weights, adds, start, size, jnp.bfloat16, True, window
        )

    def wider(value):
        return value.astype(jnp.float32)

    def over_x_z(term, from_core, window):
        from_x = trade(term(2 * count, count, [(from_core, 0)], window), "gx", 2)
        mine = wide_sum(term(3 * count, count, [(from_core, count)], window), from_x)
        mine = mine.reshape(2, 2, own_rows, window[1])
        pair = mine[:, 0] + wider(trade(half(mine[:, 1]), "gy", 1))
        return pair[0] + wider(trade(half(pair[1]), "gy", 2))

    def over_z_x(term, from_core, window):
        both = term(2 * count, 2 * count, [(from_core, 0)], window)
        both = both.reshape(2, 2, 2, own_rows, window[1])
        pair = wide_sum(both[:, :, 0], trade(both[:, :, 1], "gy", 1))
        ends = pair[:, 0] + wider(trade(half(pair[:, 1]), "gy", 2))
        return ends[1] + wider(trade(half(ends[0]), "gx", 2))

    def spread_rows(term, ways):
        width = features // len(ways)
        from_core = trade(term(0, 2 * count, []), "gx", 1)
        sums = [way(term, from_core, (place * width, width)) for place, way in enumerate(ways)]
        return jnp.concatenate(sums, axis=1)

    normed_grad = spread_rows(backward_term, (over_x_z, over_z_x))
    layer_out = half(wide + spread_rows(forward_term, (over_x_z, over_x_z)))
    first, second = lax.psum(
        (jnp.sum(normed_grad, axis=1), jnp.sum(normed_grad * normed, axis=1)), "gz"
    )
    grad_full = out_cotangent.astype(jnp.float32) + inverse[:, None] * (
        normed_grad - (first / D)[:, None] - normed * (second / D)[:, None]
    )
    return (layer_out, half(grad_full))


def solution(mesh):
    in_specs = (
        P(("gx", "gy"), "gz"),
        P(("gx", "gy"), "gz"),
        P(("gz", "gx"), "gy"),
        P(("gz", "gx"), "gy"),
        P(("gz", "gx"), "gy"),
        P(("gz", "gx"), "gy"),
        P(("gy", "gx"), "gz"),
        P(("gy", "gx"), "gz"),
    )
    out_specs = (P(("gx", "gy"), "gz"), P(("gx", "gy"), "gz"))
    return jax.shard_map(body, mesh=mesh, in_specs=in_specs, out_specs=out_specs, check_vma=False)
```

```python
import functools
import math

import jax
import jax.numpy as jnp
from jax import lax
from jax.experimental import pallas as pl
from jax.experimental.pallas import tpu as pltpu
from jax.sharding import PartitionSpec as P

D = 6144
HEAD_DIM = 128
IMG_TOK = 256


EPSILON = 1e-06
ROOT_HALF = 0.7071067811865476
ROOT_TWO_PI_INV = 0.3989422804014327


def attend_kernel(
    q_own, q_got, k_own, k_got, v_own, v_got, g_ref, mixed_ref, dq_ref, dk_ref, dv_ref, *, scale
):
    def total(own, got):
        return own[...].astype(jnp.float32) + got[...].astype(jnp.float32)

    def norm(values):
        center = values - jnp.mean(values, axis=-1, keepdims=True)
        spread = jnp.mean(center * center, axis=-1, keepdims=True)
        inverse = lax.rsqrt(spread + EPSILON)
        return center * inverse, inverse

    def norm_back(grad, normed, inverse):
        slope = inverse * (grad - normed * jnp.mean(grad * normed, axis=-1, keepdims=True))
        return (slope - jnp.mean(slope, axis=-1, keepdims=True)).astype(jnp.bfloat16)

    def contract(left, right, left_dim, right_dim):
        return lax.dot_general(
            left,
            right,
            (((left_dim,), (right_dim,)), ((), ())),
            preferred_element_type=jnp.float32,
        )

    def half(values):
        return values.astype(jnp.bfloat16)

    q_norm, q_inverse = norm(total(q_own, q_got))
    k_norm, k_inverse = norm(total(k_own, k_got))
    q_half, k_half = half(q_norm), half(k_norm)
    v_half = half(total(v_own, v_got))
    grad = g_ref[...]
    weights = jnp.exp(contract(q_half, k_half, 1, 1) * scale)
    probs = weights / jnp.sum(weights, axis=-1, keepdims=True)
    probs_half = half(probs)
    mixed_ref[...] = half(contract(probs_half, v_half, 1, 0))
    dv_ref[...] = half(contract(probs_half, grad, 0, 0))
    probs_grad = half(contract(grad, v_half, 1, 1)).astype(jnp.float32)
    inner = jnp.sum(probs_grad * probs, axis=-1, keepdims=True)
    score_grad = half(probs * (probs_grad - inner) * scale)
    q_grad = half(contract(score_grad, k_half, 1, 0)).astype(jnp.float32)
    k_grad = half(contract(score_grad, q_half, 0, 0)).astype(jnp.float32)
    dq_ref[...] = norm_back(q_grad, q_norm, q_inverse)
    dk_ref[...] = norm_back(k_grad, k_norm, k_inverse)


def attend(own, got, grad):
    rows, width = own.shape[0], own.shape[1] // 3
    heads = width // HEAD_DIM

    def block(part):
        return pl.BlockSpec((IMG_TOK, HEAD_DIM), lambda image, head: (image, part * heads + head))

    half = jax.ShapeDtypeStruct((rows, width), jnp.bfloat16)
    return pl.pallas_call(
        functools.partial(attend_kernel, scale=1.0 / math.sqrt(HEAD_DIM)),
        grid=(rows // IMG_TOK, heads),
        in_specs=[block(0), block(0), block(1), block(1), block(2), block(2), block(0)],
        out_specs=[block(0)] * 4,
        out_shape=[half] * 4,
        compiler_params=pltpu.CompilerParams(vmem_limit_bytes=32 * 1024 * 1024),
        cost_estimate=pl.CostEstimate(
            flops=rows * IMG_TOK * width // 8,
            bytes_accessed=rows * width // 4,
            transcendentals=0,
        ),
        name="attend",
    )(own, got, own, got, own, got, grad)


def gelu(pre):
    return pre * 0.5 * (1.0 + lax.erf(pre * ROOT_HALF))


def gelu_back(pre, grad_half):
    cdf = 0.5 * (1.0 + lax.erf(pre * ROOT_HALF))
    pdf = jnp.exp(-0.5 * pre * pre) * ROOT_TWO_PI_INV
    return (grad_half.astype(jnp.float32) * (cdf + pre * pdf)).astype(jnp.bfloat16)


def dot(left, right):
    return jnp.dot(left, right, preferred_element_type=jnp.float32)


def back_dot(left, right):
    return lax.dot_general(
        left, right, (((1,), (1,)), ((), ())), preferred_element_type=jnp.float32
    )


def half(values):
    return values.astype(jnp.bfloat16)


def wide_sum(own, got):
    return own.astype(jnp.float32) + got.astype(jnp.float32)


def trade(block, axis, bit):
    pairs = [(index, index ^ bit) for index in range(lax.axis_size(axis))]
    return lax.ppermute(block, axis, pairs)


VMEM_LIMIT = 48 * 1024 * 1024


def params():
    return pltpu.CompilerParams(vmem_limit_bytes=VMEM_LIMIT)


def cost(flops, *arrays):
    moved = sum(math.prod(array.shape) * array.dtype.itemsize for array in arrays)
    return pl.CostEstimate(flops=flops // 64, bytes_accessed=moved // 64, transcendentals=0)


def pack_kernel(*refs):
    out_ref, start = refs[-1], 0
    for ref in refs[:-1]:
        out_ref[0, :, start : start + ref.shape[1]] = ref[...]
        start += ref.shape[1]


def pack(weights, owners, start, width, tile):
    rows, columns = weights[0].shape
    first, blocks = start // tile, columns // owners // tile
    out = jax.ShapeDtypeStruct((owners, rows, len(weights) * width), weights[0].dtype)
    spec = pl.BlockSpec((rows, tile), lambda owner, n: (0, owner * blocks + first + n))
    return pl.pallas_call(
        pack_kernel,
        grid=(owners, width // tile),
        in_specs=[spec] * len(weights),
        out_specs=pl.BlockSpec((1, rows, len(weights) * tile), lambda owner, n: (owner, 0, n)),
        out_shape=out,
        compiler_params=params(),
        cost_estimate=cost(0, out, out),
        name="pack",
    )(*weights)


IMAGE_ORDER = (3, 1, 2, 0)


def store_images(place_ref, out_ref, value):
    size = value.shape[0] // len(IMAGE_ORDER)
    for image in range(len(IMAGE_ORDER)):
        start = pl.multiple_of(place_ref[image] * size, size)
        out_ref[pl.ds(start, size), :] = value[image * size : (image + 1) * size]


def cot_kernel(place_ref, rows_ref, attn_ref, mlp_ref, out_ref):
    step = pl.program_id(0)

    @pl.when(step == 0)
    def _():
        store_images(place_ref, out_ref, half(back_dot(rows_ref[...], attn_ref[...])))

    @pl.when(step > 0)
    def _():
        store_images(place_ref, out_ref, half(back_dot(rows_ref[...], mlp_ref[...])))


def cot_product(place, rows, w_attn_out, w_mlp_out):
    count, features = rows.shape
    tile = w_attn_out.shape[0]
    columns = tile + w_mlp_out.shape[0]
    out = jax.ShapeDtypeStruct((count, columns), jnp.bfloat16)
    return pl.pallas_call(
        cot_kernel,
        grid_spec=pltpu.PrefetchScalarGridSpec(
            num_scalar_prefetch=1,
            grid=(columns // tile,),
            in_specs=[
                pl.BlockSpec((count, features), lambda n, place: (0, 0)),
                pl.BlockSpec((tile, features), lambda n, place: (0, 0)),
                pl.BlockSpec((tile, features), lambda n, place: (jnp.maximum(n - 1, 0), 0)),
            ],
            out_specs=pl.BlockSpec((count, tile), lambda n, place: (0, n)),
        ),
        out_shape=out,
        compiler_params=params(),
        cost_estimate=cost(2 * count * columns * features, out, w_attn_out, w_mlp_out),
        name="cot_product",
    )(place, rows, w_attn_out, w_mlp_out)


def add_kernel(*refs):
    terms, out_ref = refs[:-1], refs[-1]
    count = len(terms) // 2
    rows = terms[0].shape[2]
    for part in range(count):
        total = half(wide_sum(terms[part][0], terms[count + part][0]))
        out_ref[0, :, part * rows : (part + 1) * rows, :] = total


def add_parts(owns, gots, n_gy):
    images, parts, columns = len(IMAGE_ORDER), len(owns), owns[0].shape[1]
    rows = owns[0].shape[0] // images // n_gy
    out = jax.ShapeDtypeStruct((images, n_gy, parts * rows, columns), jnp.bfloat16)
    terms = [value.reshape(images, n_gy, rows, columns) for value in (*owns, *gots)]
    spec = pl.BlockSpec((1, n_gy, rows, columns), lambda image: (image, 0, 0, 0))
    added = pl.pallas_call(
        add_kernel,
        grid=(images,),
        in_specs=[spec] * len(terms),
        out_specs=pl.BlockSpec((1, *out.shape[1:]), lambda image: (image, 0, 0, 0)),
        out_shape=out,
        compiler_params=params(),
        cost_estimate=cost(0, out, out, out),
        name="add_parts",
    )(*terms)
    return added.reshape(images * n_gy * parts * rows, columns)


def in_kernel(place_ref, rows_ref, weight_ref, out_ref):
    store_images(place_ref, out_ref, half(dot(rows_ref[...], weight_ref[...])))


def in_product(place, rows, weight):
    count, features = rows.shape
    columns = weight.shape[1]
    tile = 384 if columns % 384 == 0 else 256
    out = jax.ShapeDtypeStruct((count, columns), jnp.bfloat16)
    return pl.pallas_call(
        in_kernel,
        grid_spec=pltpu.PrefetchScalarGridSpec(
            num_scalar_prefetch=1,
            grid=(columns // tile,),
            in_specs=[
                pl.BlockSpec((count, features), lambda n, place: (0, 0)),
                pl.BlockSpec((features, tile), lambda n, place: (0, n)),
            ],
            out_specs=pl.BlockSpec((count, tile), lambda n, place: (0, n)),
        ),
        out_shape=out,
        compiler_params=params(),
        cost_estimate=cost(2 * count * columns * features, rows, out, weight),
        name="in_product",
    )(place, rows, weight)


def product(terms, weights, adds, start, count, kind, transposed, window=None, rows=None):
    whole = weights[0].shape[0 if transposed else 1]
    first_column, columns = window or (0, whole)
    tile = 512 if columns % 512 == 0 else 384 if columns % 384 == 0 else 256
    skip = first_column // tile
    specs = [
        pl.BlockSpec((count, value.shape[1]), lambda n: (start // count, 0))
        for value, _, _ in terms
    ]
    for weight in weights:
        if transposed:
            specs.append(pl.BlockSpec((tile, weight.shape[1]), lambda n: (n + skip, 0)))
        else:
            block, size = rows or (0, weight.shape[0])
            specs.append(pl.BlockSpec((size, tile), lambda n, block=block: (block, n + skip)))
    for _, first in adds:
        specs.append(
            pl.BlockSpec((count, tile), lambda n, place=first // count: (place, n + skip))
        )

    def kernel(*refs):
        weight_refs = refs[len(terms) : len(terms) + len(weights)]
        total = None
        for ref, (value, index, offset) in zip(refs, terms):
            summed = slice(offset, offset + value.shape[1])
            if transposed:
                part = back_dot(ref[...], weight_refs[index][:, summed])
            else:
                part = dot(ref[...], weight_refs[index][summed, :])
            total = part if total is None else total + part
        for ref in refs[len(terms) + len(weights) : -1]:
            total = total + ref[...].astype(jnp.float32)
        refs[-1][...] = total.astype(kind)

    depth = sum(value.shape[1] for value, _, _ in terms)
    out = jax.ShapeDtypeStruct((count, columns), kind)
    return pl.pallas_call(
        kernel,
        grid=(columns // tile,),
        in_specs=specs,
        out_specs=pl.BlockSpec((count, tile), lambda n: (0, n)),
        out_shape=out,
        compiler_params=params(),
        cost_estimate=cost(2 * count * columns * depth, out, *weights),
        name="back_product" if transposed else "out_product",
    )(*(value for value, _, _ in terms), *weights, *(add for add, _ in adds))


MLP_CUTS = (256, 512, 512, 256)
EARLY_CUTS = 2


def body(layer_input, out_cotangent, w_query, w_key, w_value, w_mlp_in, w_attn_out, w_mlp_out):
    n_gx, n_gy, n_gz = (lax.axis_size(name) for name in ("gx", "gy", "gz"))
    me_y = lax.axis_index("gy")
    own_rows, features = layer_input.shape
    count = own_rows * n_gy
    places = jnp.array([IMAGE_ORDER.index(bits) for bits in range(n_gx)], jnp.int32)
    place = places[lax.axis_index("gx") ^ jnp.arange(n_gx)]

    def after(value, *earlier):
        return lax.optimization_barrier((value, earlier))[0]

    def others(part):
        if n_gz == 2:
            return trade(part, "gz", 1)
        return half(lax.psum(part.astype(jnp.float32), "gz") - part.astype(jnp.float32))

    def all_rows(block):
        return lax.all_gather(block, ("gx", "gy"), axis=0, tiled=True)

    def swap(packed):
        swapped = lax.all_to_all(packed, "gx", split_axis=0, concat_axis=0, tiled=True)
        return swapped.reshape(n_gx * packed.shape[1], packed.shape[2])

    heads_width = w_query.shape[1] // n_gx
    packed_heads = pack((w_query, w_key, w_value), n_gx, 0, heads_width, heads_width)
    starts = [sum(MLP_CUTS[:cut]) for cut in range(len(MLP_CUTS))]
    packed_mlp = [
        pack((w_mlp_in,), n_gx, start, width, 256) for start, width in zip(starts, MLP_CUTS)
    ]

    in_heads = swap(packed_heads)

    wide = layer_input.astype(jnp.float32)
    total, squares = lax.psum((jnp.sum(wide, axis=1), jnp.sum(wide * wide, axis=1)), "gz")
    center = total / D
    spread = squares / D - center * center
    inverse = lax.rsqrt(spread + EPSILON)
    normed = (wide - center[:, None]) * inverse[:, None]

    middle = own_rows // 2
    first_cot = all_rows(out_cotangent[:middle])
    second_cot = all_rows(after(out_cotangent[middle:], total))
    all_in = all_rows(after(half(normed), first_cot))

    cot_owns = [cot_product(place, first_cot, w_attn_out, w_mlp_out)]
    cot_gots = [others(cot_owns[0])]
    cot_owns.append(cot_product(place, after(second_cot, cot_gots[0]), w_attn_out, w_mlp_out))
    cot_gots.append(others(cot_owns[1]))

    in_mlp = [swap(after(packed_mlp[0], in_heads, cot_owns[0]))]
    in_mlp.append(swap(after(packed_mlp[1], in_mlp[0], cot_owns[1])))
    mlp_own = [in_product(place, after(all_in, cot_gots[1]), in_mlp[0])]
    mlp_got = [others(mlp_own[0])]
    heads_own = in_product(place, after(all_in, mlp_own[0]), in_heads)
    heads_got = others(heads_own)
    in_mlp.append(swap(after(packed_mlp[2], in_mlp[1], mlp_own[0])))
    mlp_own.append(in_product(place, after(all_in, mlp_got[0], heads_own), in_mlp[1]))
    mlp_got.append(others(mlp_own[1]))
    in_mlp.append(swap(after(packed_mlp[3], in_mlp[2], heads_own)))
    mlp_own.append(in_product(place, after(all_in, heads_got), in_mlp[2]))
    mlp_got.append(others(mlp_own[2]))

    out_grad = add_parts(after(cot_owns, mlp_own[1]), cot_gots, n_gy)
    mixed, *head_grads = attend(heads_own, heads_got, out_grad)
    mlp_own.append(in_product(place, after(all_in, mlp_got[1], mixed), in_mlp[3]))
    mlp_got.append(others(mlp_own[3]))

    forward_terms, backward_terms = [(mixed, 0, 0)], []
    for index, grad in enumerate(head_grads):
        backward_terms.append((grad, 0, index * heads_width))

    def add_terms(cut, own):
        pre = wide_sum(own, mlp_got[cut])
        first = heads_width + starts[cut]
        grad = gelu_back(pre, out_grad[:, first : first + own.shape[1]])
        forward_terms.append((half(gelu(pre)), 1, starts[cut]))
        backward_terms.append((grad, 1 + cut, 0))

    out_weights, in_weights = [w_attn_out, w_mlp_out], [in_heads, *in_mlp]
    for cut in range(EARLY_CUTS):
        add_terms(cut, mlp_own[cut])
    rows = 4 * count
    forward_early = product(forward_terms, out_weights, [], 0, rows, jnp.bfloat16, False)
    backward_early = product(
        backward_terms, in_weights[: 1 + EARLY_CUTS], [], 0, rows, jnp.bfloat16, True
    )
    del forward_terms[:], backward_terms[:]
    for cut in range(EARLY_CUTS, len(MLP_CUTS)):
        add_terms(cut, after(mlp_own[cut], forward_early, backward_early))
    late_weights = in_weights[1 + EARLY_CUTS :]
    backward_terms = [
        (grad, index - 1 - EARLY_CUTS, offset) for grad, index, offset in backward_terms
    ]
    early, all_columns = starts[EARLY_CUTS], sum(MLP_CUTS)
    late_rows = (early // (all_columns - early), all_columns - early)
    forward_terms = [(act, 0, offset - early) for act, _, offset in forward_terms]

    def forward_term(start, size, adds, window=None):
        adds = [(forward_early, start), *adds]
        return product(
            forward_terms, [w_mlp_out], adds, start, size, jnp.bfloat16, False, window, late_rows
        )

    def backward_term(start, size, adds, window=None):
        adds = [(backward_early, start), *adds]
        return product(
            backward_terms, late_weights, adds, start, size, jnp.bfloat16, True, window
        )

    def wider(value):
        return value.astype(jnp.float32)

    def at(value, axis, index):
        return lax.index_in_dim(value, index, axis, keepdims=False)

    def own_and_sent(value, axis, is_second):
        low, high = at(value, axis, 0), at(value, axis, 1)
        return jnp.where(is_second, high, low), half(jnp.where(is_second, low, high))

    def over_z(value, axis):
        kept, sent = own_and_sent(value, axis + 1, me_y % 2 == 1)
        value = wide_sum(kept, trade(sent, "gy", 1))
        kept, sent = own_and_sent(value, axis, me_y >= 2)
        return wide_sum(kept, trade(sent, "gy", 2))

    def over_x_z(term, from_core, window):
        from_x = trade(term(2 * count, count, [(from_core, 0)], window), "gx", 2)
        mine = wide_sum(term(3 * count, count, [(from_core, count)], window), from_x)
        return over_z(mine.reshape(2, 2, own_rows, window[1]), 0)

    def over_z_x(term, from_core, window):
        both = term(2 * count, 2 * count, [(from_core, 0)], window)
        ends = over_z(both.reshape(2, 2, 2, own_rows, window[1]), 1)
        return wide_sum(ends[1], trade(half(ends[0]), "gx", 2))

    def spread_rows(term, ways):
        width = features // len(ways)
        from_core = trade(term(0, 2 * count, []), "gx", 1)
        sums = [way(term, from_core, (place * width, width)) for place, way in enumerate(ways)]
        return jnp.concatenate(sums, axis=1)

    normed_grad = spread_rows(backward_term, (over_x_z, over_z_x))
    layer_out = half(wide + spread_rows(forward_term, (over_x_z, over_x_z)))
    first, second = lax.psum(
        (jnp.sum(normed_grad, axis=1), jnp.sum(normed_grad * normed, axis=1)), "gz"
    )
    grad_full = out_cotangent.astype(jnp.float32) + inverse[:, None] * (
        normed_grad - (first / D)[:, None] - normed * (second / D)[:, None]
    )
    return (layer_out, half(grad_full))


def solution(mesh):
    in_specs = (
        P(("gx", "gy"), "gz"),
        P(("gx", "gy"), "gz"),
        P(("gz", "gx"), "gy"),
        P(("gz", "gx"), "gy"),
        P(("gz", "gx"), "gy"),
        P(("gz", "gx"), "gy"),
        P(("gy", "gx"), "gz"),
        P(("gy", "gx"), "gz"),
    )
    out_specs = (P(("gx", "gy"), "gz"), P(("gx", "gy"), "gz"))
    return jax.shard_map(body, mesh=mesh, in_specs=in_specs, out_specs=out_specs, check_vma=False)
```

```python
import functools
import math

import jax
import jax.numpy as jnp
from jax import lax
from jax.experimental import pallas as pl
from jax.experimental.pallas import tpu as pltpu
from jax.sharding import PartitionSpec as P

D = 6144
HEAD_DIM = 128
IMG_TOK = 256


EPSILON = 1e-06
ROOT_HALF = 0.7071067811865476
ROOT_TWO_PI_INV = 0.3989422804014327


def attend_kernel(
    q_own, q_got, k_own, k_got, v_own, v_got, g_ref, mixed_ref, dq_ref, dk_ref, dv_ref, *, scale
):
    def total(own, got):
        return own[...].astype(jnp.float32) + got[...].astype(jnp.float32)

    def norm(values):
        center = values - jnp.mean(values, axis=-1, keepdims=True)
        spread = jnp.mean(center * center, axis=-1, keepdims=True)
        inverse = lax.rsqrt(spread + EPSILON)
        return center * inverse, inverse

    def norm_back(grad, normed, inverse):
        slope = inverse * (grad - normed * jnp.mean(grad * normed, axis=-1, keepdims=True))
        return (slope - jnp.mean(slope, axis=-1, keepdims=True)).astype(jnp.bfloat16)

    def contract(left, right, left_dim, right_dim):
        return lax.dot_general(
            left,
            right,
            (((left_dim,), (right_dim,)), ((), ())),
            preferred_element_type=jnp.float32,
        )

    def half(values):
        return values.astype(jnp.bfloat16)

    q_norm, q_inverse = norm(total(q_own, q_got))
    k_norm, k_inverse = norm(total(k_own, k_got))
    q_half, k_half = half(q_norm), half(k_norm)
    v_half = half(total(v_own, v_got))
    grad = g_ref[...]
    weights = jnp.exp(contract(q_half, k_half, 1, 1) * scale)
    probs = weights / jnp.sum(weights, axis=-1, keepdims=True)
    probs_half = half(probs)
    mixed_ref[...] = half(contract(probs_half, v_half, 1, 0))
    dv_ref[...] = half(contract(probs_half, grad, 0, 0))
    probs_grad = half(contract(grad, v_half, 1, 1)).astype(jnp.float32)
    inner = jnp.sum(probs_grad * probs, axis=-1, keepdims=True)
    score_grad = half(probs * (probs_grad - inner) * scale)
    q_grad = half(contract(score_grad, k_half, 1, 0)).astype(jnp.float32)
    k_grad = half(contract(score_grad, q_half, 0, 0)).astype(jnp.float32)
    dq_ref[...] = norm_back(q_grad, q_norm, q_inverse)
    dk_ref[...] = norm_back(k_grad, k_norm, k_inverse)


def attend(own, got, grad):
    rows, width = own.shape[0], own.shape[1] // 3
    heads = width // HEAD_DIM

    def block(part):
        return pl.BlockSpec((IMG_TOK, HEAD_DIM), lambda image, head: (image, part * heads + head))

    half = jax.ShapeDtypeStruct((rows, width), jnp.bfloat16)
    return pl.pallas_call(
        functools.partial(attend_kernel, scale=1.0 / math.sqrt(HEAD_DIM)),
        grid=(rows // IMG_TOK, heads),
        in_specs=[block(0), block(0), block(1), block(1), block(2), block(2), block(0)],
        out_specs=[block(0)] * 4,
        out_shape=[half] * 4,
        compiler_params=pltpu.CompilerParams(vmem_limit_bytes=32 * 1024 * 1024),
        cost_estimate=pl.CostEstimate(
            flops=rows * IMG_TOK * width // 8,
            bytes_accessed=rows * width // 4,
            transcendentals=0,
        ),
        name="attend",
    )(own, got, own, got, own, got, grad)


def gelu(pre):
    return pre * 0.5 * (1.0 + lax.erf(pre * ROOT_HALF))


def gelu_back(pre, grad_half):
    cdf = 0.5 * (1.0 + lax.erf(pre * ROOT_HALF))
    pdf = jnp.exp(-0.5 * pre * pre) * ROOT_TWO_PI_INV
    return (grad_half.astype(jnp.float32) * (cdf + pre * pdf)).astype(jnp.bfloat16)


def dot(left, right):
    return jnp.dot(left, right, preferred_element_type=jnp.float32)


def back_dot(left, right):
    return lax.dot_general(
        left, right, (((1,), (1,)), ((), ())), preferred_element_type=jnp.float32
    )


def half(values):
    return values.astype(jnp.bfloat16)


def wide_sum(own, got):
    return own.astype(jnp.float32) + got.astype(jnp.float32)


def trade(block, axis, bit):
    pairs = [(index, index ^ bit) for index in range(lax.axis_size(axis))]
    return lax.ppermute(block, axis, pairs)


VMEM_LIMIT = 48 * 1024 * 1024


def params():
    return pltpu.CompilerParams(vmem_limit_bytes=VMEM_LIMIT)


def cost(flops, *arrays):
    moved = sum(math.prod(array.shape) * array.dtype.itemsize for array in arrays)
    return pl.CostEstimate(flops=flops // 64, bytes_accessed=moved // 64, transcendentals=0)


def pack_kernel(*refs):
    out_ref, start = refs[-1], 0
    for ref in refs[:-1]:
        out_ref[0, :, start : start + ref.shape[1]] = ref[...]
        start += ref.shape[1]


def pack(weights, owners, start, width, tile):
    rows, columns = weights[0].shape
    first, blocks = start // tile, columns // owners // tile
    out = jax.ShapeDtypeStruct((owners, rows, len(weights) * width), weights[0].dtype)
    spec = pl.BlockSpec((rows, tile), lambda owner, n: (0, owner * blocks + first + n))
    return pl.pallas_call(
        pack_kernel,
        grid=(owners, width // tile),
        in_specs=[spec] * len(weights),
        out_specs=pl.BlockSpec((1, rows, len(weights) * tile), lambda owner, n: (owner, 0, n)),
        out_shape=out,
        compiler_params=params(),
        cost_estimate=cost(0, out, out),
        name="pack",
    )(*weights)


IMAGE_ORDER = ((1, 1), (0, 1), (1, 0), (0, 0))


def assemble_kernel(*refs):
    parts, out_ref = refs[:-1], refs[-1]
    rows = parts[0].shape[1]
    start = 0
    for x_bit, core_bit in IMAGE_ORDER:
        for part in range(len(parts) // 2):
            out_ref[start : start + rows, :] = parts[2 * part + core_bit][x_bit]
            start += rows


def assemble(parts):
    flat = [value for part in parts for value in part]
    _, rows, features = flat[0].shape
    tile = 768
    out = jax.ShapeDtypeStruct((len(flat) * 2 * rows, features), flat[0].dtype)
    return pl.pallas_call(
        assemble_kernel,
        grid=(features // tile,),
        in_specs=[pl.BlockSpec((2, rows, tile), lambda n: (0, 0, n))] * len(flat),
        out_specs=pl.BlockSpec((out.shape[0], tile), lambda n: (0, n)),
        out_shape=out,
        compiler_params=params(),
        cost_estimate=cost(0, out, out),
        name="assemble",
    )(*flat)


def cot_kernel(own_ref, other_ref, attn_ref, mlp_ref, out_ref, rows_ref):
    rows = own_ref.shape[1]
    step = pl.program_id(0)

    @pl.when(step == 0)
    def _():
        for place, (x_bit, core_bit) in enumerate(IMAGE_ORDER):
            part = other_ref if core_bit else own_ref
            rows_ref[place * rows : (place + 1) * rows, :] = part[x_bit]
        out_ref[...] = half(back_dot(rows_ref[...], attn_ref[...]))

    @pl.when(step > 0)
    def _():
        out_ref[...] = half(back_dot(rows_ref[...], mlp_ref[...]))


def cot_product(part, w_attn_out, w_mlp_out):
    own, other = part
    _, rows, features = own.shape
    tile = w_attn_out.shape[0]
    columns = tile + w_mlp_out.shape[0]
    count = len(IMAGE_ORDER) * rows
    out = jax.ShapeDtypeStruct((count, columns), jnp.bfloat16)
    whole = pl.BlockSpec(own.shape, lambda n: (0, 0, 0))
    return pl.pallas_call(
        cot_kernel,
        grid=(columns // tile,),
        in_specs=[
            whole,
            whole,
            pl.BlockSpec((tile, features), lambda n: (0, 0)),
            pl.BlockSpec((tile, features), lambda n: (jnp.maximum(n - 1, 0), 0)),
        ],
        out_specs=pl.BlockSpec((count, tile), lambda n: (0, n)),
        out_shape=out,
        scratch_shapes=[pltpu.VMEM((count, features), jnp.bfloat16)],
        compiler_params=params(),
        cost_estimate=cost(2 * count * columns * features, out, w_attn_out, w_mlp_out),
        name="cot_product",
    )(own, other, w_attn_out, w_mlp_out)


def add_kernel(*refs):
    terms, out_ref = refs[:-1], refs[-1]
    count = len(terms) // 2
    for part in range(count):
        out_ref[0, part] = half(wide_sum(terms[part][0], terms[count + part][0]))


def add_parts(owns, gots):
    images, parts = len(IMAGE_ORDER), len(owns)
    rows, columns = owns[0].shape[0] // images, owns[0].shape[1]
    out = jax.ShapeDtypeStruct((images, parts, rows, columns), jnp.bfloat16)
    terms = [value.reshape(images, rows, columns) for value in (*owns, *gots)]
    added = pl.pallas_call(
        add_kernel,
        grid=(images,),
        in_specs=[pl.BlockSpec((1, rows, columns), lambda image: (image, 0, 0))] * len(terms),
        out_specs=pl.BlockSpec((1, parts, rows, columns), lambda image: (image, 0, 0, 0)),
        out_shape=out,
        compiler_params=params(),
        cost_estimate=cost(0, out, out, out),
        name="add_parts",
    )(*terms)
    return added.reshape(images * parts * rows, columns)


def in_kernel(rows_ref, weight_ref, out_ref):
    out_ref[...] = half(dot(rows_ref[...], weight_ref[...]))


def in_product(rows, weight, half_index=None):
    count, features = rows.shape
    first = half_index or 0
    count = count if half_index is None else count // 2
    columns = weight.shape[1]
    tile = 384 if columns % 384 == 0 else 256
    out = jax.ShapeDtypeStruct((count, columns), jnp.bfloat16)
    return pl.pallas_call(
        in_kernel,
        grid=(columns // tile,),
        in_specs=[
            pl.BlockSpec((count, features), lambda n: (first, 0)),
            pl.BlockSpec((features, tile), lambda n: (0, n)),
        ],
        out_specs=pl.BlockSpec((count, tile), lambda n: (0, n)),
        out_shape=out,
        compiler_params=params(),
        cost_estimate=cost(2 * count * columns * features, rows, out, weight),
        name="in_product",
    )(rows, weight)


def product(terms, weights, adds, start, count, kind, transposed, window=None, rows=None):
    whole = weights[0].shape[0 if transposed else 1]
    first_column, columns = window or (0, whole)
    tile = 512 if columns % 512 == 0 else 384 if columns % 384 == 0 else 256
    skip = first_column // tile
    specs = [
        pl.BlockSpec(
            (count, value.shape[1]), lambda n, place=(start - row) // count: (place, 0)
        )
        for value, _, _, row in terms
    ]
    for weight in weights:
        if transposed:
            specs.append(pl.BlockSpec((tile, weight.shape[1]), lambda n: (n + skip, 0)))
        else:
            block, size = rows or (0, weight.shape[0])
            specs.append(pl.BlockSpec((size, tile), lambda n, block=block: (block, n + skip)))
    for _, first in adds:
        specs.append(
            pl.BlockSpec((count, tile), lambda n, place=first // count: (place, n + skip))
        )

    def kernel(*refs):
        weight_refs = refs[len(terms) : len(terms) + len(weights)]
        total = None
        for ref, (value, index, offset, _) in zip(refs, terms):
            summed = slice(offset, offset + value.shape[1])
            if transposed:
                part = back_dot(ref[...], weight_refs[index][:, summed])
            else:
                part = dot(ref[...], weight_refs[index][summed, :])
            total = part if total is None else total + part
        for ref in refs[len(terms) + len(weights) : -1]:
            total = total + ref[...].astype(jnp.float32)
        refs[-1][...] = total.astype(kind)

    depth = sum(value.shape[1] for value, *_ in terms)
    out = jax.ShapeDtypeStruct((count, columns), kind)
    return pl.pallas_call(
        kernel,
        grid=(columns // tile,),
        in_specs=specs,
        out_specs=pl.BlockSpec((count, tile), lambda n: (0, n)),
        out_shape=out,
        compiler_params=params(),
        cost_estimate=cost(2 * count * columns * depth, out, *weights),
        name="back_product" if transposed else "out_product",
    )(*(value for value, *_ in terms), *weights, *(add for add, _ in adds))


MLP_CUTS = (256, 512, 768)


def body(layer_input, out_cotangent, w_query, w_key, w_value, w_mlp_in, w_attn_out, w_mlp_out):
    n_gx, n_gz = lax.axis_size("gx"), lax.axis_size("gz")
    own_rows, features = layer_input.shape
    count = own_rows * lax.axis_size("gy")

    def after(value, *earlier):
        return lax.optimization_barrier((value, earlier))[0]

    def others(part):
        if n_gz == 2:
            return trade(part, "gz", 1)
        return half(lax.psum(part.astype(jnp.float32), "gz") - part.astype(jnp.float32))

    def with_x(block):
        return jnp.stack([block, trade(block, "gx", 2)])

    def over_z(pair):
        near, far = trade(pair, "gy", 1), trade(pair, "gy", 2)
        return [pair, near, far, trade(far, "gy", 1)]

    def with_core(part):
        return part, trade(part, "gx", 1)

    def swap(packed):
        swapped = lax.all_to_all(packed, "gx", split_axis=0, concat_axis=0, tiled=True)
        return swapped.reshape(n_gx * packed.shape[1], packed.shape[2])

    heads_width = w_query.shape[1] // n_gx
    packed_heads = pack((w_query, w_key, w_value), n_gx, 0, heads_width, heads_width)
    starts = [sum(MLP_CUTS[:cut]) for cut in range(len(MLP_CUTS))]
    packed_mlp = [
        pack((w_mlp_in,), n_gx, start, width, 256) for start, width in zip(starts, MLP_CUTS)
    ]

    cot_pair = with_x(out_cotangent)
    wide = layer_input.astype(jnp.float32)
    total, squares = lax.psum((jnp.sum(wide, axis=1), jnp.sum(wide * wide, axis=1)), "gz")
    center = total / D
    spread = squares / D - center * center
    inverse = lax.rsqrt(spread + EPSILON)
    normed = (wide - center[:, None]) * inverse[:, None]
    normed_pair = with_x(half(normed))

    cot_parts, normed_parts = over_z(cot_pair), over_z(normed_pair)
    waits = [(), (normed_parts[1],), (), ()]
    cot_owns, cot_gots = [], []
    for place, part in enumerate(cot_parts):
        own, other = with_core(part)
        own = after(own, *waits[place], *cot_gots[: max(place - 1, 0)])
        cot_owns.append(cot_product((own, other), w_attn_out, w_mlp_out))
        cot_gots.append(others(cot_owns[-1]))
    all_in = assemble([with_core(part) for part in normed_parts])

    in_heads = swap(after(packed_heads, normed_pair, cot_owns[0]))
    in_mlp = [swap(after(packed_mlp[0], in_heads, cot_owns[2], normed_parts[2]))]
    in_mlp.append(swap(after(packed_mlp[1], in_mlp[0], cot_owns[3])))
    heads_own = in_product(after(all_in, cot_gots[1]), in_heads)
    heads_got = others(heads_own)
    mlp_own = [in_product(after(all_in, cot_gots[2], heads_own), in_mlp[0])]
    mlp_got = [others(mlp_own[0])]
    in_mlp.append(swap(after(packed_mlp[2], in_mlp[1], heads_own)))
    mlp_own.append(in_product(after(all_in, cot_gots[3], mlp_own[0]), in_mlp[1]))
    mlp_got.append(others(mlp_own[1]))

    out_grad = add_parts(after(cot_owns, mlp_own[0]), cot_gots)
    late_owns = [in_product(after(all_in, heads_got, out_grad), in_mlp[2], 0)]
    late_gots = [others(late_owns[0])]
    late_owns.append(in_product(after(all_in, late_owns[0]), in_mlp[2], 1))
    late_gots.append(others(late_owns[1]))

    mixed, *head_grads = attend(heads_own, heads_got, out_grad)

    def mlp_terms(cut, first_row, own, got):
        pre = wide_sum(own, got)
        column = heads_width + starts[cut]
        rows = slice(first_row, first_row + own.shape[0])
        grad = gelu_back(pre, out_grad[rows, column : column + own.shape[1]])
        return half(gelu(pre)), grad

    forward_terms = [(after(mixed, late_owns), 0, 0, 0)]
    backward_terms = [
        (grad, 0, index * heads_width, 0) for index, grad in enumerate(head_grads)
    ]
    for cut in range(2):
        act, grad = mlp_terms(cut, 0, after(mlp_own[cut], mixed), mlp_got[cut])
        forward_terms.append((act, 1, starts[cut], 0))
        backward_terms.append((grad, 1 + cut, 0, 0))
    rows = 4 * count
    forward_early = product(
        forward_terms, [w_attn_out, w_mlp_out], [], 0, rows, jnp.bfloat16, False
    )
    backward_early = product(
        backward_terms, [in_heads, *in_mlp[:2]], [], 0, rows, jnp.bfloat16, True
    )
    forward_late, backward_late = [], []

    def add_late(part, *earlier):
        first_row = part * 2 * count
        own = after(late_owns[part], *earlier)
        act, grad = mlp_terms(2, first_row, own, late_gots[part])
        forward_late.append([(act, 0, 0, first_row)])
        backward_late.append([(grad, 0, 0, first_row)])

    late_rows = (starts[2] // MLP_CUTS[2], MLP_CUTS[2])

    def forward_term(start, size, adds, window=None):
        adds, terms = [(forward_early, start), *adds], forward_late[start // (2 * count)]
        return product(
            terms, [w_mlp_out], adds, start, size, jnp.bfloat16, False, window, late_rows
        )

    def backward_term(start, size, adds, window=None):
        adds, terms = [(backward_early, start), *adds], backward_late[start // (2 * count)]
        return product(terms, [in_mlp[2]], adds, start, size, jnp.bfloat16, True, window)

    def wider(value):
        return value.astype(jnp.float32)

    def over_x_z(term, from_core, window):
        from_x = trade(term(2 * count, count, [(from_core, 0)], window), "gx", 2)
        mine = wide_sum(term(3 * count, count, [(from_core, count)], window), from_x)
        mine = mine.reshape(2, 2, own_rows, window[1])
        pair = mine[:, 0] + wider(trade(half(mine[:, 1]), "gy", 1))
        return pair[0] + wider(trade(half(pair[1]), "gy", 2))

    def over_z_x(term, from_core, window):
        both = term(2 * count, 2 * count, [(from_core, 0)], window)
        both = both.reshape(2, 2, 2, own_rows, window[1])
        pair = wide_sum(both[:, :, 0], trade(both[:, :, 1], "gy", 1))
        ends = pair[:, 0] + wider(trade(half(pair[:, 1]), "gy", 2))
        return ends[1] + wider(trade(half(ends[0]), "gx", 2))

    add_late(0, forward_early, backward_early)
    forward_to_core = forward_term(0, 2 * count, [])
    (grad, *where), *_ = backward_late[0]
    backward_late[0] = [(after(grad, late_gots[1]), *where)]
    to_cores = forward_to_core, backward_term(0, 2 * count, [])
    add_late(1, *to_cores)

    def spread_rows(term, to_core, ways):
        width = features // len(ways)
        from_core = trade(to_core, "gx", 1)
        sums = [way(term, from_core, (place * width, width)) for place, way in enumerate(ways)]
        return jnp.concatenate(sums, axis=1)

    normed_grad = spread_rows(backward_term, to_cores[1], (over_x_z, over_z_x))
    layer_out = half(wide + spread_rows(forward_term, to_cores[0], (over_x_z, over_x_z)))
    first, second = lax.psum(
        (jnp.sum(normed_grad, axis=1), jnp.sum(normed_grad * normed, axis=1)), "gz"
    )
    grad_full = out_cotangent.astype(jnp.float32) + inverse[:, None] * (
        normed_grad - (first / D)[:, None] - normed * (second / D)[:, None]
    )
    return (layer_out, half(grad_full))


def solution(mesh):
    in_specs = (
        P(("gx", "gy"), "gz"),
        P(("gx", "gy"), "gz"),
        P(("gz", "gx"), "gy"),
        P(("gz", "gx"), "gy"),
        P(("gz", "gx"), "gy"),
        P(("gz", "gx"), "gy"),
        P(("gy", "gx"), "gz"),
        P(("gy", "gx"), "gz"),
    )
    out_specs = (P(("gx", "gy"), "gz"), P(("gx", "gy"), "gz"))
    return jax.shard_map(body, mesh=mesh, in_specs=in_specs, out_specs=out_specs, check_vma=False)
```

```python
import functools
import math

import jax
import jax.numpy as jnp
from jax import lax
from jax.experimental import pallas as pl
from jax.experimental.pallas import tpu as pltpu
from jax.sharding import PartitionSpec as P

D = 6144
HEAD_DIM = 128
IMG_TOK = 256


EPSILON = 1e-06
ROOT_HALF = 0.7071067811865476
ROOT_TWO_PI_INV = 0.3989422804014327


def attend_kernel(
    q_own, q_got, k_own, k_got, v_own, v_got, g_ref, mixed_ref, dq_ref, dk_ref, dv_ref, *, scale
):
    def total(own, got):
        return own[...].astype(jnp.float32) + got[...].astype(jnp.float32)

    def norm(values):
        center = values - jnp.mean(values, axis=-1, keepdims=True)
        spread = jnp.mean(center * center, axis=-1, keepdims=True)
        inverse = lax.rsqrt(spread + EPSILON)
        return center * inverse, inverse

    def norm_back(grad, normed, inverse):
        slope = inverse * (grad - normed * jnp.mean(grad * normed, axis=-1, keepdims=True))
        return (slope - jnp.mean(slope, axis=-1, keepdims=True)).astype(jnp.bfloat16)

    def contract(left, right, left_dim, right_dim):
        return lax.dot_general(
            left,
            right,
            (((left_dim,), (right_dim,)), ((), ())),
            preferred_element_type=jnp.float32,
        )

    def half(values):
        return values.astype(jnp.bfloat16)

    q_norm, q_inverse = norm(total(q_own, q_got))
    k_norm, k_inverse = norm(total(k_own, k_got))
    q_half, k_half = half(q_norm), half(k_norm)
    v_half = half(total(v_own, v_got))
    grad = g_ref[...]
    weights = jnp.exp(contract(q_half, k_half, 1, 1) * scale)
    probs = weights / jnp.sum(weights, axis=-1, keepdims=True)
    probs_half = half(probs)
    mixed_ref[...] = half(contract(probs_half, v_half, 1, 0))
    dv_ref[...] = half(contract(probs_half, grad, 0, 0))
    probs_grad = half(contract(grad, v_half, 1, 1)).astype(jnp.float32)
    inner = jnp.sum(probs_grad * probs, axis=-1, keepdims=True)
    score_grad = half(probs * (probs_grad - inner) * scale)
    q_grad = half(contract(score_grad, k_half, 1, 0)).astype(jnp.float32)
    k_grad = half(contract(score_grad, q_half, 0, 0)).astype(jnp.float32)
    dq_ref[...] = norm_back(q_grad, q_norm, q_inverse)
    dk_ref[...] = norm_back(k_grad, k_norm, k_inverse)


def attend(own, got, grad):
    rows, width = own.shape[0], own.shape[1] // 3
    heads = width // HEAD_DIM

    def block(part):
        return pl.BlockSpec((IMG_TOK, HEAD_DIM), lambda image, head: (image, part * heads + head))

    half = jax.ShapeDtypeStruct((rows, width), jnp.bfloat16)
    return pl.pallas_call(
        functools.partial(attend_kernel, scale=1.0 / math.sqrt(HEAD_DIM)),
        grid=(rows // IMG_TOK, heads),
        in_specs=[block(0), block(0), block(1), block(1), block(2), block(2), block(0)],
        out_specs=[block(0)] * 4,
        out_shape=[half] * 4,
        compiler_params=pltpu.CompilerParams(vmem_limit_bytes=32 * 1024 * 1024),
        cost_estimate=pl.CostEstimate(
            flops=rows * IMG_TOK * width // 8,
            bytes_accessed=rows * width // 4,
            transcendentals=0,
        ),
        name="attend",
    )(own, got, own, got, own, got, grad)


def gelu(pre):
    return pre * 0.5 * (1.0 + lax.erf(pre * ROOT_HALF))


def gelu_back(pre, grad_half):
    cdf = 0.5 * (1.0 + lax.erf(pre * ROOT_HALF))
    pdf = jnp.exp(-0.5 * pre * pre) * ROOT_TWO_PI_INV
    return (grad_half.astype(jnp.float32) * (cdf + pre * pdf)).astype(jnp.bfloat16)


def dot(left, right):
    return jnp.dot(left, right, preferred_element_type=jnp.float32)


def back_dot(left, right):
    return lax.dot_general(
        left, right, (((1,), (1,)), ((), ())), preferred_element_type=jnp.float32
    )


def half(values):
    return values.astype(jnp.bfloat16)


def wide_sum(own, got):
    return own.astype(jnp.float32) + got.astype(jnp.float32)


def trade(block, axis, bit):
    pairs = [(index, index ^ bit) for index in range(lax.axis_size(axis))]
    return lax.ppermute(block, axis, pairs)


VMEM_LIMIT = 48 * 1024 * 1024


def params():
    return pltpu.CompilerParams(vmem_limit_bytes=VMEM_LIMIT)


def cost(flops, *arrays):
    moved = sum(math.prod(array.shape) * array.dtype.itemsize for array in arrays)
    return pl.CostEstimate(flops=flops // 64, bytes_accessed=moved // 64, transcendentals=0)


def pack_kernel(*refs):
    out_ref, start = refs[-1], 0
    for ref in refs[:-1]:
        out_ref[0, :, start : start + ref.shape[1]] = ref[...]
        start += ref.shape[1]


def pack(weights, owners, start, width, tile):
    rows, columns = weights[0].shape
    first, blocks = start // tile, columns // owners // tile
    out = jax.ShapeDtypeStruct((owners, rows, len(weights) * width), weights[0].dtype)
    spec = pl.BlockSpec((rows, tile), lambda owner, n: (0, owner * blocks + first + n))
    return pl.pallas_call(
        pack_kernel,
        grid=(owners, width // tile),
        in_specs=[spec] * len(weights),
        out_specs=pl.BlockSpec((1, rows, len(weights) * tile), lambda owner, n: (owner, 0, n)),
        out_shape=out,
        compiler_params=params(),
        cost_estimate=cost(0, out, out),
        name="pack",
    )(*weights)


IMAGE_ORDER = ((1, 1), (0, 1), (1, 0), (0, 0))


def assemble_kernel(*refs):
    parts, out_ref = refs[:-1], refs[-1]
    rows = parts[0].shape[1]
    start = 0
    for x_bit, core_bit in IMAGE_ORDER:
        for part in range(len(parts) // 2):
            out_ref[start : start + rows, :] = parts[2 * part + core_bit][x_bit]
            start += rows


def assemble(parts):
    flat = [value for part in parts for value in part]
    _, rows, features = flat[0].shape
    tile = 768
    out = jax.ShapeDtypeStruct((len(flat) * 2 * rows, features), flat[0].dtype)
    return pl.pallas_call(
        assemble_kernel,
        grid=(features // tile,),
        in_specs=[pl.BlockSpec((2, rows, tile), lambda n: (0, 0, n))] * len(flat),
        out_specs=pl.BlockSpec((out.shape[0], tile), lambda n: (0, n)),
        out_shape=out,
        compiler_params=params(),
        cost_estimate=cost(0, out, out),
        name="assemble",
    )(*flat)


def cot_kernel(own_ref, other_ref, attn_ref, mlp_ref, out_ref, rows_ref):
    rows = own_ref.shape[1]
    step = pl.program_id(0)

    @pl.when(step == 0)
    def _():
        for place, (x_bit, core_bit) in enumerate(IMAGE_ORDER):
            part = other_ref if core_bit else own_ref
            rows_ref[place * rows : (place + 1) * rows, :] = part[x_bit]
        out_ref[...] = half(back_dot(rows_ref[...], attn_ref[...]))

    @pl.when(step > 0)
    def _():
        out_ref[...] = half(back_dot(rows_ref[...], mlp_ref[...]))


def cot_product(part, w_attn_out, w_mlp_out):
    own, other = part
    _, rows, features = own.shape
    tile = w_attn_out.shape[0]
    columns = tile + w_mlp_out.shape[0]
    count = len(IMAGE_ORDER) * rows
    out = jax.ShapeDtypeStruct((count, columns), jnp.bfloat16)
    whole = pl.BlockSpec(own.shape, lambda n: (0, 0, 0))
    return pl.pallas_call(
        cot_kernel,
        grid=(columns // tile,),
        in_specs=[
            whole,
            whole,
            pl.BlockSpec((tile, features), lambda n: (0, 0)),
            pl.BlockSpec((tile, features), lambda n: (jnp.maximum(n - 1, 0), 0)),
        ],
        out_specs=pl.BlockSpec((count, tile), lambda n: (0, n)),
        out_shape=out,
        scratch_shapes=[pltpu.VMEM((count, features), jnp.bfloat16)],
        compiler_params=params(),
        cost_estimate=cost(2 * count * columns * features, out, w_attn_out, w_mlp_out),
        name="cot_product",
    )(own, other, w_attn_out, w_mlp_out)


def add_kernel(*refs):
    terms, out_ref = refs[:-1], refs[-1]
    count = len(terms) // 2
    for part in range(count):
        out_ref[0, part] = half(wide_sum(terms[part][0], terms[count + part][0]))


def add_parts(owns, gots):
    images, parts = len(IMAGE_ORDER), len(owns)
    rows, columns = owns[0].shape[0] // images, owns[0].shape[1]
    out = jax.ShapeDtypeStruct((images, parts, rows, columns), jnp.bfloat16)
    terms = [value.reshape(images, rows, columns) for value in (*owns, *gots)]
    added = pl.pallas_call(
        add_kernel,
        grid=(images,),
        in_specs=[pl.BlockSpec((1, rows, columns), lambda image: (image, 0, 0))] * len(terms),
        out_specs=pl.BlockSpec((1, parts, rows, columns), lambda image: (image, 0, 0, 0)),
        out_shape=out,
        compiler_params=params(),
        cost_estimate=cost(0, out, out, out),
        name="add_parts",
    )(*terms)
    return added.reshape(images * parts * rows, columns)


def in_kernel(rows_ref, weight_ref, out_ref):
    out_ref[...] = half(dot(rows_ref[...], weight_ref[...]))


def in_product(rows, weight, half_index=None):
    count, features = rows.shape
    first = half_index or 0
    count = count if half_index is None else count // 2
    columns = weight.shape[1]
    tile = 384 if columns % 384 == 0 else 256
    out = jax.ShapeDtypeStruct((count, columns), jnp.bfloat16)
    return pl.pallas_call(
        in_kernel,
        grid=(columns // tile,),
        in_specs=[
            pl.BlockSpec((count, features), lambda n: (first, 0)),
            pl.BlockSpec((features, tile), lambda n: (0, n)),
        ],
        out_specs=pl.BlockSpec((count, tile), lambda n: (0, n)),
        out_shape=out,
        compiler_params=params(),
        cost_estimate=cost(2 * count * columns * features, rows, out, weight),
        name="in_product",
    )(rows, weight)


def product(terms, weights, adds, start, count, kind, transposed, window=None, rows=None):
    whole = weights[0].shape[0 if transposed else 1]
    first_column, columns = window or (0, whole)
    tile = 512 if columns % 512 == 0 else 384 if columns % 384 == 0 else 256
    skip = first_column // tile
    specs = [
        pl.BlockSpec(
            (count, value.shape[1]), lambda n, place=(start - row) // count: (place, 0)
        )
        for value, _, _, row in terms
    ]
    for weight in weights:
        if transposed:
            specs.append(pl.BlockSpec((tile, weight.shape[1]), lambda n: (n + skip, 0)))
        else:
            block, size = rows or (0, weight.shape[0])
            specs.append(pl.BlockSpec((size, tile), lambda n, block=block: (block, n + skip)))
    for _, first in adds:
        specs.append(
            pl.BlockSpec((count, tile), lambda n, place=first // count: (place, n + skip))
        )

    def kernel(*refs):
        weight_refs = refs[len(terms) : len(terms) + len(weights)]
        total = None
        for ref, (value, index, offset, _) in zip(refs, terms):
            summed = slice(offset, offset + value.shape[1])
            if transposed:
                part = back_dot(ref[...], weight_refs[index][:, summed])
            else:
                part = dot(ref[...], weight_refs[index][summed, :])
            total = part if total is None else total + part
        for ref in refs[len(terms) + len(weights) : -1]:
            total = total + ref[...].astype(jnp.float32)
        refs[-1][...] = total.astype(kind)

    depth = sum(value.shape[1] for value, *_ in terms)
    out = jax.ShapeDtypeStruct((count, columns), kind)
    return pl.pallas_call(
        kernel,
        grid=(columns // tile,),
        in_specs=specs,
        out_specs=pl.BlockSpec((count, tile), lambda n: (0, n)),
        out_shape=out,
        compiler_params=params(),
        cost_estimate=cost(2 * count * columns * depth, out, *weights),
        name="back_product" if transposed else "out_product",
    )(*(value for value, *_ in terms), *weights, *(add for add, _ in adds))


MLP_CUTS = (256, 512, 768)


def body(layer_input, out_cotangent, w_query, w_key, w_value, w_mlp_in, w_attn_out, w_mlp_out):
    n_gx, n_gz = lax.axis_size("gx"), lax.axis_size("gz")
    own_rows, features = layer_input.shape
    count = own_rows * lax.axis_size("gy")

    def after(value, *earlier):
        return lax.optimization_barrier((value, earlier))[0]

    def others(part):
        if n_gz == 2:
            return trade(part, "gz", 1)
        return half(lax.psum(part.astype(jnp.float32), "gz") - part.astype(jnp.float32))

    def with_x(block):
        return jnp.stack([block, trade(block, "gx", 2)])

    def over_z(pair):
        near, far = trade(pair, "gy", 1), trade(pair, "gy", 2)
        return [pair, near, far, trade(far, "gy", 1)]

    def with_core(part):
        return part, trade(part, "gx", 1)

    def swap(packed):
        swapped = lax.all_to_all(packed, "gx", split_axis=0, concat_axis=0, tiled=True)
        return swapped.reshape(n_gx * packed.shape[1], packed.shape[2])

    heads_width = w_query.shape[1] // n_gx
    packed_heads = pack((w_query, w_key, w_value), n_gx, 0, heads_width, heads_width)
    starts = [sum(MLP_CUTS[:cut]) for cut in range(len(MLP_CUTS))]
    packed_mlp = [
        pack((w_mlp_in,), n_gx, start, width, 256) for start, width in zip(starts, MLP_CUTS)
    ]

    cot_pair = with_x(out_cotangent)
    wide = layer_input.astype(jnp.float32)
    total, squares = lax.psum((jnp.sum(wide, axis=1), jnp.sum(wide * wide, axis=1)), "gz")
    center = total / D
    spread = squares / D - center * center
    inverse = lax.rsqrt(spread + EPSILON)
    normed = (wide - center[:, None]) * inverse[:, None]
    normed_pair = with_x(half(normed))

    cot_parts, normed_parts = over_z(cot_pair), over_z(normed_pair)
    cot_owns, cot_gots = [], []
    for place, part in enumerate(cot_parts):
        own, other = with_core(part)
        if place == 2:
            own = after(own, cot_owns[1], cot_gots[0])
        if place == 3:
            own = after(own, cot_gots[1], cot_gots[2], normed_parts[2])
        cot_owns.append(cot_product((own, other), w_attn_out, w_mlp_out))
        cot_gots.append(others(cot_owns[-1]))
    all_in = assemble([with_core(part) for part in normed_parts])

    in_heads = swap(after(packed_heads, normed_pair, cot_owns[0]))
    in_mlp = [swap(after(packed_mlp[0], in_heads, cot_owns[2], *normed_parts[1:3]))]
    in_mlp.append(swap(after(packed_mlp[1], in_mlp[0], cot_owns[3], all_in)))
    heads_own = in_product(after(all_in, cot_gots[3]), in_heads)
    heads_got = others(heads_own)
    mlp_own = [in_product(after(all_in, heads_own), in_mlp[0])]
    mlp_got = [others(mlp_own[0])]
    in_mlp.append(swap(after(packed_mlp[2], in_mlp[1], heads_own)))
    mlp_own.append(in_product(after(all_in, mlp_own[0]), in_mlp[1]))
    mlp_got.append(others(mlp_own[1]))

    out_grad = add_parts(after(cot_owns, mlp_own[0]), cot_gots)
    late_owns = [in_product(after(all_in, heads_got, out_grad), in_mlp[2], 0)]
    late_gots = [others(late_owns[0])]
    late_owns.append(in_product(after(all_in, late_owns[0]), in_mlp[2], 1))
    late_gots.append(others(late_owns[1]))

    mixed, *head_grads = attend(heads_own, heads_got, out_grad)

    def mlp_terms(cut, first_row, own, got):
        pre = wide_sum(own, got)
        column = heads_width + starts[cut]
        rows = slice(first_row, first_row + own.shape[0])
        grad = gelu_back(pre, out_grad[rows, column : column + own.shape[1]])
        return half(gelu(pre)), grad

    forward_terms = [(after(mixed, late_owns), 0, 0, 0)]
    backward_terms = [
        (grad, 0, index * heads_width, 0) for index, grad in enumerate(head_grads)
    ]
    for cut in range(2):
        act, grad = mlp_terms(cut, 0, after(mlp_own[cut], mixed), mlp_got[cut])
        forward_terms.append((act, 1, starts[cut], 0))
        backward_terms.append((grad, 1 + cut, 0, 0))
    rows = 4 * count
    forward_early = product(
        forward_terms, [w_attn_out, w_mlp_out], [], 0, rows, jnp.bfloat16, False
    )
    backward_early = product(
        backward_terms, [in_heads, *in_mlp[:2]], [], 0, rows, jnp.bfloat16, True
    )
    forward_late, backward_late = [], []

    def add_late(part, *earlier):
        first_row = part * 2 * count
        own = after(late_owns[part], *earlier)
        act, grad = mlp_terms(2, first_row, own, late_gots[part])
        forward_late.append([(act, 0, 0, first_row)])
        backward_late.append([(grad, 0, 0, first_row)])

    late_rows = (starts[2] // MLP_CUTS[2], MLP_CUTS[2])

    def forward_term(start, size, adds, window=None):
        adds, terms = [(forward_early, start), *adds], forward_late[start // (2 * count)]
        return product(
            terms, [w_mlp_out], adds, start, size, jnp.bfloat16, False, window, late_rows
        )

    def backward_term(start, size, adds, window=None):
        adds, terms = [(backward_early, start), *adds], backward_late[start // (2 * count)]
        return product(terms, [in_mlp[2]], adds, start, size, jnp.bfloat16, True, window)

    def wider(value):
        return value.astype(jnp.float32)

    def over_x_z(term, from_core, window):
        from_x = trade(term(2 * count, count, [(from_core, 0)], window), "gx", 2)
        mine = wide_sum(term(3 * count, count, [(from_core, count)], window), from_x)
        mine = mine.reshape(2, 2, own_rows, window[1])
        pair = mine[:, 0] + wider(trade(half(mine[:, 1]), "gy", 1))
        return pair[0] + wider(trade(half(pair[1]), "gy", 2))

    def over_z_x(term, from_core, window):
        both = term(2 * count, 2 * count, [(from_core, 0)], window)
        both = both.reshape(2, 2, 2, own_rows, window[1])
        pair = wide_sum(both[:, :, 0], trade(both[:, :, 1], "gy", 1))
        ends = pair[:, 0] + wider(trade(half(pair[:, 1]), "gy", 2))
        return ends[1] + wider(trade(half(ends[0]), "gx", 2))

    add_late(0, forward_early, backward_early)
    forward_to_core = forward_term(0, 2 * count, [])
    (grad, *where), *_ = backward_late[0]
    backward_late[0] = [(after(grad, late_gots[1]), *where)]
    to_cores = forward_to_core, backward_term(0, 2 * count, [])
    add_late(1, *to_cores)

    def spread_rows(term, to_core, ways):
        width = features // len(ways)
        from_core = trade(to_core, "gx", 1)
        sums = [way(term, from_core, (place * width, width)) for place, way in enumerate(ways)]
        return jnp.concatenate(sums, axis=1)

    normed_grad = spread_rows(backward_term, to_cores[1], (over_x_z, over_z_x))
    layer_out = half(wide + spread_rows(forward_term, to_cores[0], (over_x_z, over_x_z)))
    first, second = lax.psum(
        (jnp.sum(normed_grad, axis=1), jnp.sum(normed_grad * normed, axis=1)), "gz"
    )
    grad_full = out_cotangent.astype(jnp.float32) + inverse[:, None] * (
        normed_grad - (first / D)[:, None] - normed * (second / D)[:, None]
    )
    return (layer_out, half(grad_full))


def solution(mesh):
    in_specs = (
        P(("gx", "gy"), "gz"),
        P(("gx", "gy"), "gz"),
        P(("gz", "gx"), "gy"),
        P(("gz", "gx"), "gy"),
        P(("gz", "gx"), "gy"),
        P(("gz", "gx"), "gy"),
        P(("gy", "gx"), "gz"),
        P(("gy", "gx"), "gz"),
    )
    out_specs = (P(("gx", "gy"), "gz"), P(("gx", "gy"), "gz"))
    return jax.shard_map(body, mesh=mesh, in_specs=in_specs, out_specs=out_specs, check_vma=False)
```

```python
import functools
import math

import jax
import jax.numpy as jnp
from jax import lax
from jax.experimental import pallas as pl
from jax.experimental.pallas import tpu as pltpu
from jax.sharding import PartitionSpec as P

D = 6144
HEAD_DIM = 128
IMG_TOK = 256


EPSILON = 1e-06
ROOT_HALF = 0.7071067811865476
ROOT_TWO_PI_INV = 0.3989422804014327


def attend_kernel(
    q_own, q_got, k_own, k_got, v_own, v_got, g_ref, mixed_ref, dq_ref, dk_ref, dv_ref, *, scale
):
    def total(own, got):
        return own[...].astype(jnp.float32) + got[...].astype(jnp.float32)

    def norm(values):
        center = values - jnp.mean(values, axis=-1, keepdims=True)
        spread = jnp.mean(center * center, axis=-1, keepdims=True)
        inverse = lax.rsqrt(spread + EPSILON)
        return center * inverse, inverse

    def norm_back(grad, normed, inverse):
        slope = inverse * (grad - normed * jnp.mean(grad * normed, axis=-1, keepdims=True))
        return (slope - jnp.mean(slope, axis=-1, keepdims=True)).astype(jnp.bfloat16)

    def contract(left, right, left_dim, right_dim):
        return lax.dot_general(
            left,
            right,
            (((left_dim,), (right_dim,)), ((), ())),
            preferred_element_type=jnp.float32,
        )

    def half(values):
        return values.astype(jnp.bfloat16)

    q_norm, q_inverse = norm(total(q_own, q_got))
    k_norm, k_inverse = norm(total(k_own, k_got))
    q_half, k_half = half(q_norm), half(k_norm)
    v_half = half(total(v_own, v_got))
    grad = g_ref[...]
    weights = jnp.exp(contract(q_half, k_half, 1, 1) * scale)
    probs = weights / jnp.sum(weights, axis=-1, keepdims=True)
    probs_half = half(probs)
    mixed_ref[...] = half(contract(probs_half, v_half, 1, 0))
    dv_ref[...] = half(contract(probs_half, grad, 0, 0))
    probs_grad = half(contract(grad, v_half, 1, 1)).astype(jnp.float32)
    inner = jnp.sum(probs_grad * probs, axis=-1, keepdims=True)
    score_grad = half(probs * (probs_grad - inner) * scale)
    q_grad = half(contract(score_grad, k_half, 1, 0)).astype(jnp.float32)
    k_grad = half(contract(score_grad, q_half, 0, 0)).astype(jnp.float32)
    dq_ref[...] = norm_back(q_grad, q_norm, q_inverse)
    dk_ref[...] = norm_back(k_grad, k_norm, k_inverse)


def attend(own, got, grad):
    rows, width = own.shape[0], own.shape[1] // 3
    heads = width // HEAD_DIM

    def block(part):
        return pl.BlockSpec((IMG_TOK, HEAD_DIM), lambda image, head: (image, part * heads + head))

    half = jax.ShapeDtypeStruct((rows, width), jnp.bfloat16)
    return pl.pallas_call(
        functools.partial(attend_kernel, scale=1.0 / math.sqrt(HEAD_DIM)),
        grid=(rows // IMG_TOK, heads),
        in_specs=[block(0), block(0), block(1), block(1), block(2), block(2), block(0)],
        out_specs=[block(0)] * 4,
        out_shape=[half] * 4,
        compiler_params=pltpu.CompilerParams(vmem_limit_bytes=32 * 1024 * 1024),
        cost_estimate=pl.CostEstimate(
            flops=rows * IMG_TOK * width // 8,
            bytes_accessed=rows * width // 4,
            transcendentals=0,
        ),
        name="attend",
    )(own, got, own, got, own, got, grad)


def gelu(pre):
    return pre * 0.5 * (1.0 + lax.erf(pre * ROOT_HALF))


def gelu_back(pre, grad_half):
    cdf = 0.5 * (1.0 + lax.erf(pre * ROOT_HALF))
    pdf = jnp.exp(-0.5 * pre * pre) * ROOT_TWO_PI_INV
    return (grad_half.astype(jnp.float32) * (cdf + pre * pdf)).astype(jnp.bfloat16)


def dot(left, right):
    return jnp.dot(left, right, preferred_element_type=jnp.float32)


def back_dot(left, right):
    return lax.dot_general(
        left, right, (((1,), (1,)), ((), ())), preferred_element_type=jnp.float32
    )


def half(values):
    return values.astype(jnp.bfloat16)


def wide_sum(own, got):
    return own.astype(jnp.float32) + got.astype(jnp.float32)


def trade(block, axis, bit):
    pairs = [(index, index ^ bit) for index in range(lax.axis_size(axis))]
    return lax.ppermute(block, axis, pairs)


VMEM_LIMIT = 48 * 1024 * 1024


def params():
    return pltpu.CompilerParams(vmem_limit_bytes=VMEM_LIMIT)


def cost(flops, *arrays):
    moved = sum(math.prod(array.shape) * array.dtype.itemsize for array in arrays)
    return pl.CostEstimate(flops=flops // 64, bytes_accessed=moved // 64, transcendentals=0)


def pack_kernel(*refs):
    out_ref, start = refs[-1], 0
    for ref in refs[:-1]:
        out_ref[0, :, start : start + ref.shape[1]] = ref[...]
        start += ref.shape[1]


def pack(weights, owners, start, width, tile):
    rows, columns = weights[0].shape
    first, blocks = start // tile, columns // owners // tile
    out = jax.ShapeDtypeStruct((owners, rows, len(weights) * width), weights[0].dtype)
    spec = pl.BlockSpec((rows, tile), lambda owner, n: (0, owner * blocks + first + n))
    return pl.pallas_call(
        pack_kernel,
        grid=(owners, width // tile),
        in_specs=[spec] * len(weights),
        out_specs=pl.BlockSpec((1, rows, len(weights) * tile), lambda owner, n: (owner, 0, n)),
        out_shape=out,
        compiler_params=params(),
        cost_estimate=cost(0, out, out),
        name="pack",
    )(*weights)


IMAGE_ORDER = ((1, 1), (0, 1), (1, 0), (0, 0))


def assemble_kernel(*refs):
    parts, out_ref = refs[:-1], refs[-1]
    rows = parts[0].shape[1]
    start = 0
    for x_bit, core_bit in IMAGE_ORDER:
        for part in range(len(parts) // 2):
            out_ref[start : start + rows, :] = parts[2 * part + core_bit][x_bit]
            start += rows


def assemble(parts):
    flat = [value for part in parts for value in part]
    _, rows, features = flat[0].shape
    tile = 768
    out = jax.ShapeDtypeStruct((len(flat) * 2 * rows, features), flat[0].dtype)
    return pl.pallas_call(
        assemble_kernel,
        grid=(features // tile,),
        in_specs=[pl.BlockSpec((2, rows, tile), lambda n: (0, 0, n))] * len(flat),
        out_specs=pl.BlockSpec((out.shape[0], tile), lambda n: (0, n)),
        out_shape=out,
        compiler_params=params(),
        cost_estimate=cost(0, out, out),
        name="assemble",
    )(*flat)


def cot_kernel(own_ref, other_ref, attn_ref, mlp_ref, out_ref, rows_ref):
    rows = own_ref.shape[1]
    step = pl.program_id(0)

    @pl.when(step == 0)
    def _():
        for place, (x_bit, core_bit) in enumerate(IMAGE_ORDER):
            part = other_ref if core_bit else own_ref
            rows_ref[place * rows : (place + 1) * rows, :] = part[x_bit]
        out_ref[...] = half(back_dot(rows_ref[...], attn_ref[...]))

    @pl.when(step > 0)
    def _():
        out_ref[...] = half(back_dot(rows_ref[...], mlp_ref[...]))


def cot_product(part, w_attn_out, w_mlp_out):
    own, other = part
    _, rows, features = own.shape
    tile = w_attn_out.shape[0]
    columns = tile + w_mlp_out.shape[0]
    count = len(IMAGE_ORDER) * rows
    out = jax.ShapeDtypeStruct((count, columns), jnp.bfloat16)
    whole = pl.BlockSpec(own.shape, lambda n: (0, 0, 0))
    return pl.pallas_call(
        cot_kernel,
        grid=(columns // tile,),
        in_specs=[
            whole,
            whole,
            pl.BlockSpec((tile, features), lambda n: (0, 0)),
            pl.BlockSpec((tile, features), lambda n: (jnp.maximum(n - 1, 0), 0)),
        ],
        out_specs=pl.BlockSpec((count, tile), lambda n: (0, n)),
        out_shape=out,
        scratch_shapes=[pltpu.VMEM((count, features), jnp.bfloat16)],
        compiler_params=params(),
        cost_estimate=cost(2 * count * columns * features, out, w_attn_out, w_mlp_out),
        name="cot_product",
    )(own, other, w_attn_out, w_mlp_out)


def add_kernel(*refs):
    terms, out_ref = refs[:-1], refs[-1]
    count = len(terms) // 2
    for part in range(count):
        out_ref[0, part] = half(wide_sum(terms[part][0], terms[count + part][0]))


def add_parts(owns, gots):
    images, parts = len(IMAGE_ORDER), len(owns)
    rows, columns = owns[0].shape[0] // images, owns[0].shape[1]
    out = jax.ShapeDtypeStruct((images, parts, rows, columns), jnp.bfloat16)
    terms = [value.reshape(images, rows, columns) for value in (*owns, *gots)]
    added = pl.pallas_call(
        add_kernel,
        grid=(images,),
        in_specs=[pl.BlockSpec((1, rows, columns), lambda image: (image, 0, 0))] * len(terms),
        out_specs=pl.BlockSpec((1, parts, rows, columns), lambda image: (image, 0, 0, 0)),
        out_shape=out,
        compiler_params=params(),
        cost_estimate=cost(0, out, out, out),
        name="add_parts",
    )(*terms)
    return added.reshape(images * parts * rows, columns)


def in_kernel(rows_ref, weight_ref, out_ref):
    out_ref[...] = half(dot(rows_ref[...], weight_ref[...]))


def in_product(rows, weight, half_index=None):
    count, features = rows.shape
    first = half_index or 0
    count = count if half_index is None else count // 2
    columns = weight.shape[1]
    tile = 384 if columns % 384 == 0 else 256
    out = jax.ShapeDtypeStruct((count, columns), jnp.bfloat16)
    return pl.pallas_call(
        in_kernel,
        grid=(columns // tile,),
        in_specs=[
            pl.BlockSpec((count, features), lambda n: (first, 0)),
            pl.BlockSpec((features, tile), lambda n: (0, n)),
        ],
        out_specs=pl.BlockSpec((count, tile), lambda n: (0, n)),
        out_shape=out,
        compiler_params=params(),
        cost_estimate=cost(2 * count * columns * features, rows, out, weight),
        name="in_product",
    )(rows, weight)


def product(terms, weights, adds, start, count, kind, transposed, window=None, rows=None):
    whole = weights[0].shape[0 if transposed else 1]
    first_column, columns = window or (0, whole)
    tile = 512 if columns % 512 == 0 else 384 if columns % 384 == 0 else 256
    skip = first_column // tile
    specs = [
        pl.BlockSpec(
            (count, value.shape[1]), lambda n, place=(start - row) // count: (place, 0)
        )
        for value, _, _, row in terms
    ]
    for weight in weights:
        if transposed:
            specs.append(pl.BlockSpec((tile, weight.shape[1]), lambda n: (n + skip, 0)))
        else:
            block, size = rows or (0, weight.shape[0])
            specs.append(pl.BlockSpec((size, tile), lambda n, block=block: (block, n + skip)))
    for _, first in adds:
        specs.append(
            pl.BlockSpec((count, tile), lambda n, place=first // count: (place, n + skip))
        )

    def kernel(*refs):
        weight_refs = refs[len(terms) : len(terms) + len(weights)]
        total = None
        for ref, (value, index, offset, _) in zip(refs, terms):
            summed = slice(offset, offset + value.shape[1])
            if transposed:
                part = back_dot(ref[...], weight_refs[index][:, summed])
            else:
                part = dot(ref[...], weight_refs[index][summed, :])
            total = part if total is None else total + part
        for ref in refs[len(terms) + len(weights) : -1]:
            total = total + ref[...].astype(jnp.float32)
        refs[-1][...] = total.astype(kind)

    depth = sum(value.shape[1] for value, *_ in terms)
    out = jax.ShapeDtypeStruct((count, columns), kind)
    return pl.pallas_call(
        kernel,
        grid=(columns // tile,),
        in_specs=specs,
        out_specs=pl.BlockSpec((count, tile), lambda n: (0, n)),
        out_shape=out,
        compiler_params=params(),
        cost_estimate=cost(2 * count * columns * depth, out, *weights),
        name="back_product" if transposed else "out_product",
    )(*(value for value, *_ in terms), *weights, *(add for add, _ in adds))


MLP_CUTS = (512, 256, 768)


def body(layer_input, out_cotangent, w_query, w_key, w_value, w_mlp_in, w_attn_out, w_mlp_out):
    n_gx, n_gz = lax.axis_size("gx"), lax.axis_size("gz")
    own_rows, features = layer_input.shape
    count = own_rows * lax.axis_size("gy")

    def after(value, *earlier):
        return lax.optimization_barrier((value, earlier))[0]

    def others(part):
        if n_gz == 2:
            return trade(part, "gz", 1)
        return half(lax.psum(part.astype(jnp.float32), "gz") - part.astype(jnp.float32))

    def with_x(block):
        return jnp.stack([block, trade(block, "gx", 2)])

    def over_z(pair):
        return [pair, trade(pair, "gy", 1), trade(pair, "gy", 2)]

    def with_core(part):
        return part, trade(part, "gx", 1)

    def swap(packed):
        swapped = lax.all_to_all(packed, "gx", split_axis=0, concat_axis=0, tiled=True)
        return swapped.reshape(n_gx * packed.shape[1], packed.shape[2])

    heads_width = w_query.shape[1] // n_gx
    packed_heads = pack((w_query, w_key, w_value), n_gx, 0, heads_width, heads_width)
    starts = [sum(MLP_CUTS[:cut]) for cut in range(len(MLP_CUTS))]
    packed_mlp = [
        pack((w_mlp_in,), n_gx, start, width, 256) for start, width in zip(starts, MLP_CUTS)
    ]

    cot_pair = with_x(out_cotangent)
    wide = layer_input.astype(jnp.float32)
    total, squares = lax.psum((jnp.sum(wide, axis=1), jnp.sum(wide * wide, axis=1)), "gz")
    center = total / D
    spread = squares / D - center * center
    inverse = lax.rsqrt(spread + EPSILON)
    normed = (wide - center[:, None]) * inverse[:, None]
    normed_pair = with_x(half(normed))

    cot_parts, normed_parts = over_z(cot_pair), over_z(normed_pair)
    cot_parts.append(trade(cot_parts[2], "gy", 1))
    cot_owns, cot_gots = [], []
    for place, part in enumerate(cot_parts):
        own, other = with_core(part)
        if place == 2:
            own = after(own, cot_owns[1], cot_gots[0])
        if place == 3:
            own = after(own, cot_gots[1], cot_gots[2])
        cot_owns.append(cot_product((own, other), w_attn_out, w_mlp_out))
        cot_gots.append(others(cot_owns[-1]))
    normed_parts.append(trade(after(normed_parts[2], *cot_owns[1:3]), "gy", 1))
    normed_parts = [with_core(part) for part in normed_parts]
    normed_parts[0] = after(normed_parts[0], cot_owns[3])
    all_in = assemble(normed_parts)

    in_heads = swap(after(packed_heads, normed_pair, cot_owns[0]))
    in_mlp = [swap(after(packed_mlp[0], in_heads, cot_owns[2]))]
    in_mlp.append(swap(after(packed_mlp[1], in_mlp[0], all_in)))
    heads_own = in_product(after(all_in, cot_gots[3]), in_heads)
    heads_got = others(heads_own)
    mlp_own = [in_product(after(all_in, heads_own, in_mlp[1]), in_mlp[0])]
    mlp_got = [others(mlp_own[0])]
    in_mlp.append(swap(after(packed_mlp[2], in_mlp[1], heads_own)))
    mlp_own.append(in_product(after(all_in, mlp_own[0]), in_mlp[1]))
    mlp_got.append(others(mlp_own[1]))

    out_grad = add_parts(after(cot_owns, mlp_own[0]), cot_gots)
    late_owns = [in_product(after(all_in, heads_got, out_grad), in_mlp[2], 0)]
    late_gots = [others(late_owns[0])]
    late_owns.append(in_product(after(all_in, late_owns[0]), in_mlp[2], 1))
    late_gots.append(others(late_owns[1]))

    mixed, *head_grads = attend(heads_own, heads_got, out_grad)

    def mlp_terms(cut, first_row, own, got):
        pre = wide_sum(own, got)
        column = heads_width + starts[cut]
        rows = slice(first_row, first_row + own.shape[0])
        grad = gelu_back(pre, out_grad[rows, column : column + own.shape[1]])
        return half(gelu(pre)), grad

    forward_terms = [(after(mixed, late_owns), 0, 0, 0)]
    backward_terms = [
        (grad, 0, index * heads_width, 0) for index, grad in enumerate(head_grads)
    ]
    for cut in range(2):
        act, grad = mlp_terms(cut, 0, after(mlp_own[cut], mixed), mlp_got[cut])
        forward_terms.append((act, 1, starts[cut], 0))
        backward_terms.append((grad, 1 + cut, 0, 0))
    rows = 4 * count
    forward_early = product(
        forward_terms, [w_attn_out, w_mlp_out], [], 0, rows, jnp.bfloat16, False
    )
    backward_early = product(
        backward_terms, [in_heads, *in_mlp[:2]], [], 0, rows, jnp.bfloat16, True
    )
    forward_late, backward_late = [], []

    def add_late(part, *earlier):
        first_row = part * 2 * count
        own = after(late_owns[part], *earlier)
        act, grad = mlp_terms(2, first_row, own, late_gots[part])
        forward_late.append([(act, 0, 0, first_row)])
        backward_late.append([(grad, 0, 0, first_row)])

    late_rows = (starts[2] // MLP_CUTS[2], MLP_CUTS[2])

    def forward_term(start, size, adds, window=None):
        adds, terms = [(forward_early, start), *adds], forward_late[start // (2 * count)]
        return product(
            terms, [w_mlp_out], adds, start, size, jnp.bfloat16, False, window, late_rows
        )

    def backward_term(start, size, adds, window=None):
        adds, terms = [(backward_early, start), *adds], backward_late[start // (2 * count)]
        return product(terms, [in_mlp[2]], adds, start, size, jnp.bfloat16, True, window)

    def wider(value):
        return value.astype(jnp.float32)

    def over_x_z(term, from_core, window):
        from_x = trade(term(2 * count, count, [(from_core, 0)], window), "gx", 2)
        mine = wide_sum(term(3 * count, count, [(from_core, count)], window), from_x)
        mine = mine.reshape(2, 2, own_rows, window[1])
        pair = mine[:, 0] + wider(trade(half(mine[:, 1]), "gy", 1))
        return pair[0] + wider(trade(half(pair[1]), "gy", 2))

    def over_z_x(term, from_core, window):
        both = term(2 * count, 2 * count, [(from_core, 0)], window)
        both = both.reshape(2, 2, 2, own_rows, window[1])
        pair = wide_sum(both[:, :, 0], trade(both[:, :, 1], "gy", 1))
        ends = pair[:, 0] + wider(trade(half(pair[:, 1]), "gy", 2))
        return ends[1] + wider(trade(half(ends[0]), "gx", 2))

    add_late(0, forward_early, backward_early)
    forward_to_core = forward_term(0, 2 * count, [])
    (grad, *where), *_ = backward_late[0]
    backward_late[0] = [(after(grad, late_gots[1]), *where)]
    to_cores = forward_to_core, backward_term(0, 2 * count, [])
    add_late(1, *to_cores)

    def spread_rows(term, to_core, ways):
        width = features // len(ways)
        from_core = trade(to_core, "gx", 1)
        sums = [way(term, from_core, (place * width, width)) for place, way in enumerate(ways)]
        return jnp.concatenate(sums, axis=1)

    normed_grad = spread_rows(backward_term, to_cores[1], (over_x_z, over_z_x))
    layer_out = half(wide + spread_rows(forward_term, to_cores[0], (over_x_z, over_x_z)))
    first, second = lax.psum(
        (jnp.sum(normed_grad, axis=1), jnp.sum(normed_grad * normed, axis=1)), "gz"
    )
    grad_full = out_cotangent.astype(jnp.float32) + inverse[:, None] * (
        normed_grad - (first / D)[:, None] - normed * (second / D)[:, None]
    )
    return (layer_out, half(grad_full))


def solution(mesh):
    in_specs = (
        P(("gx", "gy"), "gz"),
        P(("gx", "gy"), "gz"),
        P(("gz", "gx"), "gy"),
        P(("gz", "gx"), "gy"),
        P(("gz", "gx"), "gy"),
        P(("gz", "gx"), "gy"),
        P(("gy", "gx"), "gz"),
        P(("gy", "gx"), "gz"),
    )
    out_specs = (P(("gx", "gy"), "gz"), P(("gx", "gy"), "gz"))
    return jax.shard_map(body, mesh=mesh, in_specs=in_specs, out_specs=out_specs, check_vma=False)
```

```python
import functools
import math

import jax
import jax.numpy as jnp
from jax import lax
from jax.experimental import pallas as pl
from jax.experimental.pallas import tpu as pltpu
from jax.sharding import PartitionSpec as P

D = 6144
HEAD_DIM = 128
IMG_TOK = 256


EPSILON = 1e-06
ROOT_HALF = 0.7071067811865476
ROOT_TWO_PI_INV = 0.3989422804014327


def attend_kernel(
    q_own, q_got, k_own, k_got, v_own, v_got, g_ref, mixed_ref, dq_ref, dk_ref, dv_ref, *, scale
):
    def total(own, got):
        return own[...].astype(jnp.float32) + got[...].astype(jnp.float32)

    def norm(values):
        center = values - jnp.mean(values, axis=-1, keepdims=True)
        spread = jnp.mean(center * center, axis=-1, keepdims=True)
        inverse = lax.rsqrt(spread + EPSILON)
        return center * inverse, inverse

    def norm_back(grad, normed, inverse):
        slope = inverse * (grad - normed * jnp.mean(grad * normed, axis=-1, keepdims=True))
        return (slope - jnp.mean(slope, axis=-1, keepdims=True)).astype(jnp.bfloat16)

    def contract(left, right, left_dim, right_dim):
        return lax.dot_general(
            left,
            right,
            (((left_dim,), (right_dim,)), ((), ())),
            preferred_element_type=jnp.float32,
        )

    def half(values):
        return values.astype(jnp.bfloat16)

    q_norm, q_inverse = norm(total(q_own, q_got))
    k_norm, k_inverse = norm(total(k_own, k_got))
    q_half, k_half = half(q_norm), half(k_norm)
    v_half = half(total(v_own, v_got))
    grad = g_ref[...]
    weights = jnp.exp(contract(q_half, k_half, 1, 1) * scale)
    probs = weights / jnp.sum(weights, axis=-1, keepdims=True)
    probs_half = half(probs)
    mixed_ref[...] = half(contract(probs_half, v_half, 1, 0))
    dv_ref[...] = half(contract(probs_half, grad, 0, 0))
    probs_grad = half(contract(grad, v_half, 1, 1)).astype(jnp.float32)
    inner = jnp.sum(probs_grad * probs, axis=-1, keepdims=True)
    score_grad = half(probs * (probs_grad - inner) * scale)
    q_grad = half(contract(score_grad, k_half, 1, 0)).astype(jnp.float32)
    k_grad = half(contract(score_grad, q_half, 0, 0)).astype(jnp.float32)
    dq_ref[...] = norm_back(q_grad, q_norm, q_inverse)
    dk_ref[...] = norm_back(k_grad, k_norm, k_inverse)


def attend(own, got, grad):
    rows, width = own.shape[0], own.shape[1] // 3
    heads = width // HEAD_DIM

    def block(part):
        return pl.BlockSpec((IMG_TOK, HEAD_DIM), lambda image, head: (image, part * heads + head))

    half = jax.ShapeDtypeStruct((rows, width), jnp.bfloat16)
    return pl.pallas_call(
        functools.partial(attend_kernel, scale=1.0 / math.sqrt(HEAD_DIM)),
        grid=(rows // IMG_TOK, heads),
        in_specs=[block(0), block(0), block(1), block(1), block(2), block(2), block(0)],
        out_specs=[block(0)] * 4,
        out_shape=[half] * 4,
        compiler_params=pltpu.CompilerParams(vmem_limit_bytes=32 * 1024 * 1024),
        cost_estimate=pl.CostEstimate(
            flops=rows * IMG_TOK * width // 8,
            bytes_accessed=rows * width // 4,
            transcendentals=0,
        ),
        name="attend",
    )(own, got, own, got, own, got, grad)


def gelu(pre):
    return pre * 0.5 * (1.0 + lax.erf(pre * ROOT_HALF))


def gelu_back(pre, grad_half):
    cdf = 0.5 * (1.0 + lax.erf(pre * ROOT_HALF))
    pdf = jnp.exp(-0.5 * pre * pre) * ROOT_TWO_PI_INV
    return (grad_half.astype(jnp.float32) * (cdf + pre * pdf)).astype(jnp.bfloat16)


def dot(left, right):
    return jnp.dot(left, right, preferred_element_type=jnp.float32)


def back_dot(left, right):
    return lax.dot_general(
        left, right, (((1,), (1,)), ((), ())), preferred_element_type=jnp.float32
    )


def half(values):
    return values.astype(jnp.bfloat16)


def wide_sum(own, got):
    return own.astype(jnp.float32) + got.astype(jnp.float32)


def trade(block, axis, bit):
    pairs = [(index, index ^ bit) for index in range(lax.axis_size(axis))]
    return lax.ppermute(block, axis, pairs)


VMEM_LIMIT = 48 * 1024 * 1024


def params():
    return pltpu.CompilerParams(vmem_limit_bytes=VMEM_LIMIT)


def cost(flops, *arrays):
    moved = sum(math.prod(array.shape) * array.dtype.itemsize for array in arrays)
    return pl.CostEstimate(flops=flops // 64, bytes_accessed=moved // 64, transcendentals=0)


def pack_kernel(*refs):
    out_ref, start = refs[-1], 0
    for ref in refs[:-1]:
        out_ref[0, :, start : start + ref.shape[1]] = ref[...]
        start += ref.shape[1]


def pack(weights, owners, start, width, tile):
    rows, columns = weights[0].shape
    first, blocks = start // tile, columns // owners // tile
    out = jax.ShapeDtypeStruct((owners, rows, len(weights) * width), weights[0].dtype)
    spec = pl.BlockSpec((rows, tile), lambda owner, n: (0, owner * blocks + first + n))
    return pl.pallas_call(
        pack_kernel,
        grid=(owners, width // tile),
        in_specs=[spec] * len(weights),
        out_specs=pl.BlockSpec((1, rows, len(weights) * tile), lambda owner, n: (owner, 0, n)),
        out_shape=out,
        compiler_params=params(),
        cost_estimate=cost(0, out, out),
        name="pack",
    )(*weights)


IMAGE_ORDER = ((1, 1), (0, 1), (1, 0), (0, 0))


def assemble_kernel(*refs):
    parts, out_ref = refs[:-1], refs[-1]
    rows = parts[0].shape[1]
    start = 0
    for x_bit, core_bit in IMAGE_ORDER:
        for part in range(len(parts) // 2):
            out_ref[start : start + rows, :] = parts[2 * part + core_bit][x_bit]
            start += rows


def assemble(parts):
    flat = [value for part in parts for value in part]
    _, rows, features = flat[0].shape
    tile = 768
    out = jax.ShapeDtypeStruct((len(flat) * 2 * rows, features), flat[0].dtype)
    return pl.pallas_call(
        assemble_kernel,
        grid=(features // tile,),
        in_specs=[pl.BlockSpec((2, rows, tile), lambda n: (0, 0, n))] * len(flat),
        out_specs=pl.BlockSpec((out.shape[0], tile), lambda n: (0, n)),
        out_shape=out,
        compiler_params=params(),
        cost_estimate=cost(0, out, out),
        name="assemble",
    )(*flat)


def cot_kernel(own_ref, other_ref, attn_ref, mlp_ref, out_ref, rows_ref):
    rows = own_ref.shape[1]
    step = pl.program_id(0)

    @pl.when(step == 0)
    def _():
        for place, (x_bit, core_bit) in enumerate(IMAGE_ORDER):
            part = other_ref if core_bit else own_ref
            rows_ref[place * rows : (place + 1) * rows, :] = part[x_bit]
        out_ref[...] = half(back_dot(rows_ref[...], attn_ref[...]))

    @pl.when(step > 0)
    def _():
        out_ref[...] = half(back_dot(rows_ref[...], mlp_ref[...]))


def cot_product(part, w_attn_out, w_mlp_out):
    own, other = part
    _, rows, features = own.shape
    tile = w_attn_out.shape[0]
    columns = tile + w_mlp_out.shape[0]
    count = len(IMAGE_ORDER) * rows
    out = jax.ShapeDtypeStruct((count, columns), jnp.bfloat16)
    whole = pl.BlockSpec(own.shape, lambda n: (0, 0, 0))
    return pl.pallas_call(
        cot_kernel,
        grid=(columns // tile,),
        in_specs=[
            whole,
            whole,
            pl.BlockSpec((tile, features), lambda n: (0, 0)),
            pl.BlockSpec((tile, features), lambda n: (jnp.maximum(n - 1, 0), 0)),
        ],
        out_specs=pl.BlockSpec((count, tile), lambda n: (0, n)),
        out_shape=out,
        scratch_shapes=[pltpu.VMEM((count, features), jnp.bfloat16)],
        compiler_params=params(),
        cost_estimate=cost(2 * count * columns * features, out, w_attn_out, w_mlp_out),
        name="cot_product",
    )(own, other, w_attn_out, w_mlp_out)


def add_kernel(*refs):
    terms, out_ref = refs[:-1], refs[-1]
    count = len(terms) // 2
    for part in range(count):
        out_ref[0, part] = half(wide_sum(terms[part][0], terms[count + part][0]))


def add_parts(owns, gots):
    images, parts = len(IMAGE_ORDER), len(owns)
    rows, columns = owns[0].shape[0] // images, owns[0].shape[1]
    out = jax.ShapeDtypeStruct((images, parts, rows, columns), jnp.bfloat16)
    terms = [value.reshape(images, rows, columns) for value in (*owns, *gots)]
    added = pl.pallas_call(
        add_kernel,
        grid=(images,),
        in_specs=[pl.BlockSpec((1, rows, columns), lambda image: (image, 0, 0))] * len(terms),
        out_specs=pl.BlockSpec((1, parts, rows, columns), lambda image: (image, 0, 0, 0)),
        out_shape=out,
        compiler_params=params(),
        cost_estimate=cost(0, out, out, out),
        name="add_parts",
    )(*terms)
    return added.reshape(images * parts * rows, columns)


def in_kernel(rows_ref, weight_ref, out_ref):
    out_ref[...] = half(dot(rows_ref[...], weight_ref[...]))


def in_product(rows, weight, half_index=None):
    count, features = rows.shape
    first = half_index or 0
    count = count if half_index is None else count // 2
    columns = weight.shape[1]
    tile = 384 if columns % 384 == 0 else 256
    out = jax.ShapeDtypeStruct((count, columns), jnp.bfloat16)
    return pl.pallas_call(
        in_kernel,
        grid=(columns // tile,),
        in_specs=[
            pl.BlockSpec((count, features), lambda n: (first, 0)),
            pl.BlockSpec((features, tile), lambda n: (0, n)),
        ],
        out_specs=pl.BlockSpec((count, tile), lambda n: (0, n)),
        out_shape=out,
        compiler_params=params(),
        cost_estimate=cost(2 * count * columns * features, rows, out, weight),
        name="in_product",
    )(rows, weight)


def product(terms, weights, adds, start, count, kind, transposed, window=None, rows=None):
    whole = weights[0].shape[0 if transposed else 1]
    first_column, columns = window or (0, whole)
    tile = 512 if columns % 512 == 0 else 384 if columns % 384 == 0 else 256
    skip = first_column // tile
    specs = [
        pl.BlockSpec(
            (count, value.shape[1]), lambda n, place=(start - row) // count: (place, 0)
        )
        for value, _, _, row in terms
    ]
    for weight in weights:
        if transposed:
            specs.append(pl.BlockSpec((tile, weight.shape[1]), lambda n: (n + skip, 0)))
        else:
            block, size = rows or (0, weight.shape[0])
            specs.append(pl.BlockSpec((size, tile), lambda n, block=block: (block, n + skip)))
    for _, first in adds:
        specs.append(
            pl.BlockSpec((count, tile), lambda n, place=first // count: (place, n + skip))
        )

    def kernel(*refs):
        weight_refs = refs[len(terms) : len(terms) + len(weights)]
        total = None
        for ref, (value, index, offset, _) in zip(refs, terms):
            summed = slice(offset, offset + value.shape[1])
            if transposed:
                part = back_dot(ref[...], weight_refs[index][:, summed])
            else:
                part = dot(ref[...], weight_refs[index][summed, :])
            total = part if total is None else total + part
        for ref in refs[len(terms) + len(weights) : -1]:
            total = total + ref[...].astype(jnp.float32)
        refs[-1][...] = total.astype(kind)

    depth = sum(value.shape[1] for value, *_ in terms)
    out = jax.ShapeDtypeStruct((count, columns), kind)
    return pl.pallas_call(
        kernel,
        grid=(columns // tile,),
        in_specs=specs,
        out_specs=pl.BlockSpec((count, tile), lambda n: (0, n)),
        out_shape=out,
        compiler_params=params(),
        cost_estimate=cost(2 * count * columns * depth, out, *weights),
        name="back_product" if transposed else "out_product",
    )(*(value for value, *_ in terms), *weights, *(add for add, _ in adds))


MLP_CUTS = (512, 256, 768)


def body(layer_input, out_cotangent, w_query, w_key, w_value, w_mlp_in, w_attn_out, w_mlp_out):
    n_gx, n_gz = lax.axis_size("gx"), lax.axis_size("gz")
    own_rows, features = layer_input.shape
    count = own_rows * lax.axis_size("gy")

    def after(value, *earlier):
        return lax.optimization_barrier((value, earlier))[0]

    def others(part):
        if n_gz == 2:
            return trade(part, "gz", 1)
        return half(lax.psum(part.astype(jnp.float32), "gz") - part.astype(jnp.float32))

    def with_x(block):
        return jnp.stack([block, trade(block, "gx", 2)])

    def over_z(pair):
        return [pair, trade(pair, "gy", 1), trade(pair, "gy", 2)]

    def with_core(part):
        return part, trade(part, "gx", 1)

    def swap(packed):
        swapped = lax.all_to_all(packed, "gx", split_axis=0, concat_axis=0, tiled=True)
        return swapped.reshape(n_gx * packed.shape[1], packed.shape[2])

    heads_width = w_query.shape[1] // n_gx
    packed_heads = pack((w_query, w_key, w_value), n_gx, 0, heads_width, heads_width)
    starts = [sum(MLP_CUTS[:cut]) for cut in range(len(MLP_CUTS))]
    packed_mlp = [
        pack((w_mlp_in,), n_gx, start, width, 256) for start, width in zip(starts, MLP_CUTS)
    ]

    cot_pair = with_x(out_cotangent)
    wide = layer_input.astype(jnp.float32)
    total, squares = lax.psum((jnp.sum(wide, axis=1), jnp.sum(wide * wide, axis=1)), "gz")
    center = total / D
    spread = squares / D - center * center
    inverse = lax.rsqrt(spread + EPSILON)
    normed = (wide - center[:, None]) * inverse[:, None]
    normed_pair = with_x(half(normed))

    cot_parts, normed_parts = over_z(cot_pair), over_z(normed_pair)
    cot_parts.append(trade(cot_parts[2], "gy", 1))
    cot_owns, cot_gots = [], []
    for place, part in enumerate(cot_parts):
        own, other = with_core(part)
        if place == 2:
            own = after(own, cot_owns[1], cot_gots[0], normed_parts[1])
        if place == 3:
            own = after(own, cot_gots[1])
        cot_owns.append(cot_product((own, other), w_attn_out, w_mlp_out))
        cot_gots.append(others(cot_owns[-1]))
    normed_parts.append(trade(after(normed_parts[2], *cot_owns[1:3]), "gy", 1))
    normed_parts = [with_core(part) for part in normed_parts]
    normed_parts[0] = after(normed_parts[0], cot_owns[3], cot_gots[2])
    all_in = assemble(normed_parts)

    in_heads = swap(after(packed_heads, normed_pair, cot_owns[0]))
    early = (cot_owns[2], cot_gots[1], cot_parts[3])
    in_mlp = [swap(after(packed_mlp[0], in_heads, *early))]
    in_mlp.append(swap(after(packed_mlp[1], in_mlp[0], all_in)))
    heads_own = in_product(after(all_in, cot_gots[3]), in_heads)
    heads_got = others(heads_own)
    mlp_own = [in_product(after(all_in, heads_own, in_mlp[1]), in_mlp[0])]
    mlp_got = [others(mlp_own[0])]
    in_mlp.append(swap(after(packed_mlp[2], in_mlp[1], heads_own)))
    mlp_own.append(in_product(after(all_in, mlp_own[0]), in_mlp[1]))
    mlp_got.append(others(mlp_own[1]))

    out_grad = add_parts(after(cot_owns, mlp_own[0]), cot_gots)
    late_owns = [in_product(after(all_in, heads_got, out_grad), in_mlp[2], 0)]
    late_gots = [others(late_owns[0])]
    late_owns.append(in_product(after(all_in, late_owns[0]), in_mlp[2], 1))
    late_gots.append(others(late_owns[1]))

    mixed, *head_grads = attend(heads_own, heads_got, out_grad)

    def mlp_terms(cut, first_row, own, got):
        pre = wide_sum(own, got)
        column = heads_width + starts[cut]
        rows = slice(first_row, first_row + own.shape[0])
        grad = gelu_back(pre, out_grad[rows, column : column + own.shape[1]])
        return half(gelu(pre)), grad

    forward_terms = [(after(mixed, late_owns), 0, 0, 0)]
    backward_terms = [
        (grad, 0, index * heads_width, 0) for index, grad in enumerate(head_grads)
    ]
    for cut in range(2):
        act, grad = mlp_terms(cut, 0, after(mlp_own[cut], mixed), mlp_got[cut])
        forward_terms.append((act, 1, starts[cut], 0))
        backward_terms.append((grad, 1 + cut, 0, 0))
    rows = 4 * count
    forward_early = product(
        forward_terms, [w_attn_out, w_mlp_out], [], 0, rows, jnp.bfloat16, False
    )
    backward_early = product(
        backward_terms, [in_heads, *in_mlp[:2]], [], 0, rows, jnp.bfloat16, True
    )
    forward_late, backward_late = [], []

    def add_late(part, *earlier):
        first_row = part * 2 * count
        own = after(late_owns[part], *earlier)
        act, grad = mlp_terms(2, first_row, own, late_gots[part])
        forward_late.append([(act, 0, 0, first_row)])
        backward_late.append([(grad, 0, 0, first_row)])

    late_rows = (starts[2] // MLP_CUTS[2], MLP_CUTS[2])

    def forward_term(start, size, adds, window=None):
        adds, terms = [(forward_early, start), *adds], forward_late[start // (2 * count)]
        return product(
            terms, [w_mlp_out], adds, start, size, jnp.bfloat16, False, window, late_rows
        )

    def backward_term(start, size, adds, window=None):
        adds, terms = [(backward_early, start), *adds], backward_late[start // (2 * count)]
        return product(terms, [in_mlp[2]], adds, start, size, jnp.bfloat16, True, window)

    def wider(value):
        return value.astype(jnp.float32)

    def over_x_z(term, from_core, window):
        from_x = trade(term(2 * count, count, [(from_core, 0)], window), "gx", 2)
        mine = wide_sum(term(3 * count, count, [(from_core, count)], window), from_x)
        mine = mine.reshape(2, 2, own_rows, window[1])
        pair = mine[:, 0] + wider(trade(half(mine[:, 1]), "gy", 1))
        return pair[0] + wider(trade(half(pair[1]), "gy", 2))

    def over_z_x(term, from_core, window):
        both = term(2 * count, 2 * count, [(from_core, 0)], window)
        both = both.reshape(2, 2, 2, own_rows, window[1])
        pair = wide_sum(both[:, :, 0], trade(both[:, :, 1], "gy", 1))
        ends = pair[:, 0] + wider(trade(half(pair[:, 1]), "gy", 2))
        return ends[1] + wider(trade(half(ends[0]), "gx", 2))

    add_late(0, forward_early, backward_early)
    forward_to_core = forward_term(0, 2 * count, [])
    (grad, *where), *_ = backward_late[0]
    backward_late[0] = [(after(grad, late_gots[1]), *where)]
    to_cores = forward_to_core, backward_term(0, 2 * count, [])
    add_late(1, *to_cores)

    def spread_rows(term, to_core, ways):
        width = features // len(ways)
        from_core = trade(to_core, "gx", 1)
        sums = [way(term, from_core, (place * width, width)) for place, way in enumerate(ways)]
        return jnp.concatenate(sums, axis=1)

    normed_grad = spread_rows(backward_term, to_cores[1], (over_x_z, over_z_x))
    layer_out = half(wide + spread_rows(forward_term, to_cores[0], (over_x_z, over_x_z)))
    first, second = lax.psum(
        (jnp.sum(normed_grad, axis=1), jnp.sum(normed_grad * normed, axis=1)), "gz"
    )
    grad_full = out_cotangent.astype(jnp.float32) + inverse[:, None] * (
        normed_grad - (first / D)[:, None] - normed * (second / D)[:, None]
    )
    return (layer_out, half(grad_full))


def solution(mesh):
    in_specs = (
        P(("gx", "gy"), "gz"),
        P(("gx", "gy"), "gz"),
        P(("gz", "gx"), "gy"),
        P(("gz", "gx"), "gy"),
        P(("gz", "gx"), "gy"),
        P(("gz", "gx"), "gy"),
        P(("gy", "gx"), "gz"),
        P(("gy", "gx"), "gz"),
    )
    out_specs = (P(("gx", "gy"), "gz"), P(("gx", "gy"), "gz"))
    return jax.shard_map(body, mesh=mesh, in_specs=in_specs, out_specs=out_specs, check_vma=False)
```

```python
import functools
import math

import jax
import jax.numpy as jnp
from jax import lax
from jax.experimental import pallas as pl
from jax.experimental.pallas import tpu as pltpu
from jax.sharding import PartitionSpec as P

D = 6144
HEAD_DIM = 128
IMG_TOK = 256


EPSILON = 1e-06
ROOT_HALF = 0.7071067811865476
ROOT_TWO_PI_INV = 0.3989422804014327


def attend_kernel(
    q_own, q_got, k_own, k_got, v_own, v_got, g_ref, mixed_ref, dq_ref, dk_ref, dv_ref, *, scale
):
    def total(own, got):
        return own[...].astype(jnp.float32) + got[...].astype(jnp.float32)

    def norm(values):
        center = values - jnp.mean(values, axis=-1, keepdims=True)
        spread = jnp.mean(center * center, axis=-1, keepdims=True)
        inverse = lax.rsqrt(spread + EPSILON)
        return center * inverse, inverse

    def norm_back(grad, normed, inverse):
        slope = inverse * (grad - normed * jnp.mean(grad * normed, axis=-1, keepdims=True))
        return (slope - jnp.mean(slope, axis=-1, keepdims=True)).astype(jnp.bfloat16)

    def contract(left, right, left_dim, right_dim):
        return lax.dot_general(
            left,
            right,
            (((left_dim,), (right_dim,)), ((), ())),
            preferred_element_type=jnp.float32,
        )

    def half(values):
        return values.astype(jnp.bfloat16)

    q_norm, q_inverse = norm(total(q_own, q_got))
    k_norm, k_inverse = norm(total(k_own, k_got))
    q_half, k_half = half(q_norm), half(k_norm)
    v_half = half(total(v_own, v_got))
    grad = g_ref[...]
    weights = jnp.exp(contract(q_half, k_half, 1, 1) * scale)
    probs = weights / jnp.sum(weights, axis=-1, keepdims=True)
    probs_half = half(probs)
    mixed_ref[...] = half(contract(probs_half, v_half, 1, 0))
    dv_ref[...] = half(contract(probs_half, grad, 0, 0))
    probs_grad = half(contract(grad, v_half, 1, 1)).astype(jnp.float32)
    inner = jnp.sum(probs_grad * probs, axis=-1, keepdims=True)
    score_grad = half(probs * (probs_grad - inner) * scale)
    q_grad = half(contract(score_grad, k_half, 1, 0)).astype(jnp.float32)
    k_grad = half(contract(score_grad, q_half, 0, 0)).astype(jnp.float32)
    dq_ref[...] = norm_back(q_grad, q_norm, q_inverse)
    dk_ref[...] = norm_back(k_grad, k_norm, k_inverse)


def attend(own, got, grad):
    rows, width = own.shape[0], own.shape[1] // 3
    heads = width // HEAD_DIM

    def block(part):
        return pl.BlockSpec((IMG_TOK, HEAD_DIM), lambda image, head: (image, part * heads + head))

    half = jax.ShapeDtypeStruct((rows, width), jnp.bfloat16)
    return pl.pallas_call(
        functools.partial(attend_kernel, scale=1.0 / math.sqrt(HEAD_DIM)),
        grid=(rows // IMG_TOK, heads),
        in_specs=[block(0), block(0), block(1), block(1), block(2), block(2), block(0)],
        out_specs=[block(0)] * 4,
        out_shape=[half] * 4,
        compiler_params=pltpu.CompilerParams(vmem_limit_bytes=32 * 1024 * 1024),
        cost_estimate=pl.CostEstimate(
            flops=rows * IMG_TOK * width // 8,
            bytes_accessed=rows * width // 4,
            transcendentals=0,
        ),
        name="attend",
    )(own, got, own, got, own, got, grad)


def gelu(pre):
    return pre * 0.5 * (1.0 + lax.erf(pre * ROOT_HALF))


def gelu_back(pre, grad_half):
    cdf = 0.5 * (1.0 + lax.erf(pre * ROOT_HALF))
    pdf = jnp.exp(-0.5 * pre * pre) * ROOT_TWO_PI_INV
    return (grad_half.astype(jnp.float32) * (cdf + pre * pdf)).astype(jnp.bfloat16)


def dot(left, right):
    return jnp.dot(left, right, preferred_element_type=jnp.float32)


def back_dot(left, right):
    return lax.dot_general(
        left, right, (((1,), (1,)), ((), ())), preferred_element_type=jnp.float32
    )


def half(values):
    return values.astype(jnp.bfloat16)


def wide_sum(own, got):
    return own.astype(jnp.float32) + got.astype(jnp.float32)


def trade(block, axis, bit):
    pairs = [(index, index ^ bit) for index in range(lax.axis_size(axis))]
    return lax.ppermute(block, axis, pairs)


VMEM_LIMIT = 48 * 1024 * 1024


def params():
    return pltpu.CompilerParams(vmem_limit_bytes=VMEM_LIMIT)


def cost(flops, *arrays):
    moved = sum(math.prod(array.shape) * array.dtype.itemsize for array in arrays)
    return pl.CostEstimate(flops=flops // 64, bytes_accessed=moved // 64, transcendentals=0)


def pack_kernel(*refs):
    out_ref, start = refs[-1], 0
    for ref in refs[:-1]:
        out_ref[0, :, start : start + ref.shape[1]] = ref[...]
        start += ref.shape[1]


def pack(weights, owners, start, width, tile):
    rows, columns = weights[0].shape
    first, blocks = start // tile, columns // owners // tile
    out = jax.ShapeDtypeStruct((owners, rows, len(weights) * width), weights[0].dtype)
    spec = pl.BlockSpec((rows, tile), lambda owner, n: (0, owner * blocks + first + n))
    return pl.pallas_call(
        pack_kernel,
        grid=(owners, width // tile),
        in_specs=[spec] * len(weights),
        out_specs=pl.BlockSpec((1, rows, len(weights) * tile), lambda owner, n: (owner, 0, n)),
        out_shape=out,
        compiler_params=params(),
        cost_estimate=cost(0, out, out),
        name="pack",
    )(*weights)


IMAGE_ORDER = ((1, 1), (0, 1), (1, 0), (0, 0))


def assemble_kernel(*refs):
    parts, out_ref = refs[:-1], refs[-1]
    rows = parts[0].shape[1]
    start = 0
    for x_bit, core_bit in IMAGE_ORDER:
        for part in range(len(parts) // 2):
            out_ref[start : start + rows, :] = parts[2 * part + core_bit][x_bit]
            start += rows


def assemble(parts):
    flat = [value for part in parts for value in part]
    _, rows, features = flat[0].shape
    tile = 768
    out = jax.ShapeDtypeStruct((len(flat) * 2 * rows, features), flat[0].dtype)
    return pl.pallas_call(
        assemble_kernel,
        grid=(features // tile,),
        in_specs=[pl.BlockSpec((2, rows, tile), lambda n: (0, 0, n))] * len(flat),
        out_specs=pl.BlockSpec((out.shape[0], tile), lambda n: (0, n)),
        out_shape=out,
        compiler_params=params(),
        cost_estimate=cost(0, out, out),
        name="assemble",
    )(*flat)


def cot_kernel(own_ref, other_ref, attn_ref, mlp_ref, out_ref, rows_ref):
    rows = own_ref.shape[1]
    step = pl.program_id(0)

    @pl.when(step == 0)
    def _():
        for place, (x_bit, core_bit) in enumerate(IMAGE_ORDER):
            part = other_ref if core_bit else own_ref
            rows_ref[place * rows : (place + 1) * rows, :] = part[x_bit]
        out_ref[...] = half(back_dot(rows_ref[...], attn_ref[...]))

    @pl.when(step > 0)
    def _():
        out_ref[...] = half(back_dot(rows_ref[...], mlp_ref[...]))


def cot_product(part, w_attn_out, w_mlp_out):
    own, other = part
    _, rows, features = own.shape
    tile = w_attn_out.shape[0]
    columns = tile + w_mlp_out.shape[0]
    count = len(IMAGE_ORDER) * rows
    out = jax.ShapeDtypeStruct((count, columns), jnp.bfloat16)
    whole = pl.BlockSpec(own.shape, lambda n: (0, 0, 0))
    return pl.pallas_call(
        cot_kernel,
        grid=(columns // tile,),
        in_specs=[
            whole,
            whole,
            pl.BlockSpec((tile, features), lambda n: (0, 0)),
            pl.BlockSpec((tile, features), lambda n: (jnp.maximum(n - 1, 0), 0)),
        ],
        out_specs=pl.BlockSpec((count, tile), lambda n: (0, n)),
        out_shape=out,
        scratch_shapes=[pltpu.VMEM((count, features), jnp.bfloat16)],
        compiler_params=params(),
        cost_estimate=cost(2 * count * columns * features, out, w_attn_out, w_mlp_out),
        name="cot_product",
    )(own, other, w_attn_out, w_mlp_out)


def add_kernel(*refs):
    terms, out_ref = refs[:-1], refs[-1]
    count = len(terms) // 2
    for part in range(count):
        out_ref[0, part] = half(wide_sum(terms[part][0], terms[count + part][0]))


def add_parts(owns, gots):
    images, parts = len(IMAGE_ORDER), len(owns)
    rows, columns = owns[0].shape[0] // images, owns[0].shape[1]
    out = jax.ShapeDtypeStruct((images, parts, rows, columns), jnp.bfloat16)
    terms = [value.reshape(images, rows, columns) for value in (*owns, *gots)]
    added = pl.pallas_call(
        add_kernel,
        grid=(images,),
        in_specs=[pl.BlockSpec((1, rows, columns), lambda image: (image, 0, 0))] * len(terms),
        out_specs=pl.BlockSpec((1, parts, rows, columns), lambda image: (image, 0, 0, 0)),
        out_shape=out,
        compiler_params=params(),
        cost_estimate=cost(0, out, out, out),
        name="add_parts",
    )(*terms)
    return added.reshape(images * parts * rows, columns)


def in_kernel(rows_ref, weight_ref, out_ref):
    out_ref[...] = half(dot(rows_ref[...], weight_ref[...]))


def in_product(rows, weight, half_index=None):
    count, features = rows.shape
    first = half_index or 0
    count = count if half_index is None else count // 2
    columns = weight.shape[1]
    tile = 384 if columns % 384 == 0 else 256
    out = jax.ShapeDtypeStruct((count, columns), jnp.bfloat16)
    return pl.pallas_call(
        in_kernel,
        grid=(columns // tile,),
        in_specs=[
            pl.BlockSpec((count, features), lambda n: (first, 0)),
            pl.BlockSpec((features, tile), lambda n: (0, n)),
        ],
        out_specs=pl.BlockSpec((count, tile), lambda n: (0, n)),
        out_shape=out,
        compiler_params=params(),
        cost_estimate=cost(2 * count * columns * features, rows, out, weight),
        name="in_product",
    )(rows, weight)


def product(terms, weights, adds, start, count, kind, transposed, window=None, rows=None):
    whole = weights[0].shape[0 if transposed else 1]
    first_column, columns = window or (0, whole)
    tile = 512 if columns % 512 == 0 else 384 if columns % 384 == 0 else 256
    skip = first_column // tile
    specs = [
        pl.BlockSpec(
            (count, value.shape[1]), lambda n, place=(start - row) // count: (place, 0)
        )
        for value, _, _, row in terms
    ]
    for weight in weights:
        if transposed:
            specs.append(pl.BlockSpec((tile, weight.shape[1]), lambda n: (n + skip, 0)))
        else:
            block, size = rows or (0, weight.shape[0])
            specs.append(pl.BlockSpec((size, tile), lambda n, block=block: (block, n + skip)))
    for _, first in adds:
        specs.append(
            pl.BlockSpec((count, tile), lambda n, place=first // count: (place, n + skip))
        )

    def kernel(*refs):
        weight_refs = refs[len(terms) : len(terms) + len(weights)]
        total = None
        for ref, (value, index, offset, _) in zip(refs, terms):
            summed = slice(offset, offset + value.shape[1])
            if transposed:
                part = back_dot(ref[...], weight_refs[index][:, summed])
            else:
                part = dot(ref[...], weight_refs[index][summed, :])
            total = part if total is None else total + part
        for ref in refs[len(terms) + len(weights) : -1]:
            total = total + ref[...].astype(jnp.float32)
        refs[-1][...] = total.astype(kind)

    depth = sum(value.shape[1] for value, *_ in terms)
    out = jax.ShapeDtypeStruct((count, columns), kind)
    return pl.pallas_call(
        kernel,
        grid=(columns // tile,),
        in_specs=specs,
        out_specs=pl.BlockSpec((count, tile), lambda n: (0, n)),
        out_shape=out,
        compiler_params=params(),
        cost_estimate=cost(2 * count * columns * depth, out, *weights),
        name="back_product" if transposed else "out_product",
    )(*(value for value, *_ in terms), *weights, *(add for add, _ in adds))


MLP_CUTS = (512, 256, 768)


def body(layer_input, out_cotangent, w_query, w_key, w_value, w_mlp_in, w_attn_out, w_mlp_out):
    n_gx, n_gz = lax.axis_size("gx"), lax.axis_size("gz")
    own_rows, features = layer_input.shape
    count = own_rows * lax.axis_size("gy")

    def after(value, *earlier):
        return lax.optimization_barrier((value, earlier))[0]

    def others(part):
        if n_gz == 2:
            return trade(part, "gz", 1)
        return half(lax.psum(part.astype(jnp.float32), "gz") - part.astype(jnp.float32))

    def with_x(block):
        return jnp.stack([block, trade(block, "gx", 2)])

    def over_z(pair):
        return [pair, trade(pair, "gy", 1), trade(pair, "gy", 2)]

    def with_core(part):
        return part, trade(part, "gx", 1)

    def swap(packed):
        swapped = lax.all_to_all(packed, "gx", split_axis=0, concat_axis=0, tiled=True)
        return swapped.reshape(n_gx * packed.shape[1], packed.shape[2])

    heads_width = w_query.shape[1] // n_gx
    packed_heads = pack((w_query, w_key, w_value), n_gx, 0, heads_width, heads_width)
    starts = [sum(MLP_CUTS[:cut]) for cut in range(len(MLP_CUTS))]
    packed_mlp = [
        pack((w_mlp_in,), n_gx, start, width, 256) for start, width in zip(starts, MLP_CUTS)
    ]

    cot_pair = with_x(out_cotangent)
    wide = layer_input.astype(jnp.float32)
    total, squares = lax.psum((jnp.sum(wide, axis=1), jnp.sum(wide * wide, axis=1)), "gz")
    center = total / D
    spread = squares / D - center * center
    inverse = lax.rsqrt(spread + EPSILON)
    normed = (wide - center[:, None]) * inverse[:, None]
    normed_pair = with_x(half(normed))

    cot_parts, normed_parts = over_z(cot_pair), over_z(normed_pair)
    cot_parts.append(trade(cot_parts[2], "gy", 1))
    cot_owns, cot_gots = [], []
    for place, part in enumerate(cot_parts):
        own, other = with_core(part)
        if place == 2:
            own = after(own, cot_owns[1], cot_gots[0], normed_parts[1])
        if place == 3:
            own = after(own, cot_gots[1])
        cot_owns.append(cot_product((own, other), w_attn_out, w_mlp_out))
        cot_gots.append(others(cot_owns[-1]))
    normed_parts.append(trade(after(normed_parts[2], *cot_owns[1:3]), "gy", 1))
    normed_parts = [with_core(part) for part in normed_parts]
    normed_parts[0] = after(normed_parts[0], cot_owns[3], cot_gots[2])
    all_in = assemble(normed_parts)

    in_heads = swap(after(packed_heads, normed_pair, cot_owns[0]))
    early = (cot_owns[2], cot_gots[1], cot_parts[3])
    in_mlp = [swap(after(packed_mlp[0], in_heads, *early))]
    in_mlp.append(swap(after(packed_mlp[1], in_mlp[0], all_in)))
    heads_own = in_product(after(all_in, cot_owns[3]), in_heads)
    heads_got = others(heads_own)
    mlp_own = [in_product(after(all_in, heads_own, in_mlp[1]), in_mlp[0])]
    mlp_got = [others(mlp_own[0])]
    in_mlp.append(swap(after(packed_mlp[2], in_mlp[1], heads_own)))
    mlp_own.append(in_product(after(all_in, mlp_own[0]), in_mlp[1]))
    mlp_got.append(others(mlp_own[1]))

    out_grad = add_parts(after(cot_owns, mlp_own[0]), cot_gots)
    late_owns = [in_product(after(all_in, heads_got, out_grad), in_mlp[2], 0)]
    late_gots = [others(late_owns[0])]
    late_owns.append(in_product(after(all_in, late_owns[0]), in_mlp[2], 1))
    late_gots.append(others(late_owns[1]))

    mixed, *head_grads = attend(heads_own, heads_got, out_grad)

    def mlp_terms(cut, first_row, own, got):
        pre = wide_sum(own, got)
        column = heads_width + starts[cut]
        rows = slice(first_row, first_row + own.shape[0])
        grad = gelu_back(pre, out_grad[rows, column : column + own.shape[1]])
        return half(gelu(pre)), grad

    forward_terms = [(after(mixed, late_owns), 0, 0, 0)]
    backward_terms = [
        (grad, 0, index * heads_width, 0) for index, grad in enumerate(head_grads)
    ]
    for cut in range(2):
        act, grad = mlp_terms(cut, 0, after(mlp_own[cut], mixed), mlp_got[cut])
        forward_terms.append((act, 1, starts[cut], 0))
        backward_terms.append((grad, 1 + cut, 0, 0))
    rows = 4 * count
    forward_early = product(
        forward_terms, [w_attn_out, w_mlp_out], [], 0, rows, jnp.bfloat16, False
    )
    backward_early = product(
        backward_terms, [in_heads, *in_mlp[:2]], [], 0, rows, jnp.bfloat16, True
    )
    forward_late, backward_late = [], []

    def add_late(part, *earlier):
        first_row = part * 2 * count
        own = after(late_owns[part], *earlier)
        act, grad = mlp_terms(2, first_row, own, late_gots[part])
        forward_late.append([(act, 0, 0, first_row)])
        backward_late.append([(grad, 0, 0, first_row)])

    late_rows = (starts[2] // MLP_CUTS[2], MLP_CUTS[2])

    def forward_term(start, size, adds, window=None):
        adds, terms = [(forward_early, start), *adds], forward_late[start // (2 * count)]
        return product(
            terms, [w_mlp_out], adds, start, size, jnp.bfloat16, False, window, late_rows
        )

    def backward_term(start, size, adds, window=None):
        adds, terms = [(backward_early, start), *adds], backward_late[start // (2 * count)]
        return product(terms, [in_mlp[2]], adds, start, size, jnp.bfloat16, True, window)

    def wider(value):
        return value.astype(jnp.float32)

    def over_x_z(term, from_core, window):
        from_x = trade(term(2 * count, count, [(from_core, 0)], window), "gx", 2)
        mine = wide_sum(term(3 * count, count, [(from_core, count)], window), from_x)
        mine = mine.reshape(2, 2, own_rows, window[1])
        pair = mine[:, 0] + wider(trade(half(mine[:, 1]), "gy", 1))
        return pair[0] + wider(trade(half(pair[1]), "gy", 2))

    def over_z_x(term, from_core, window):
        both = term(2 * count, 2 * count, [(from_core, 0)], window)
        both = both.reshape(2, 2, 2, own_rows, window[1])
        pair = wide_sum(both[:, :, 0], trade(both[:, :, 1], "gy", 1))
        ends = pair[:, 0] + wider(trade(half(pair[:, 1]), "gy", 2))
        return ends[1] + wider(trade(half(ends[0]), "gx", 2))

    add_late(0, forward_early, backward_early)
    forward_to_core = forward_term(0, 2 * count, [])
    (grad, *where), *_ = backward_late[0]
    backward_late[0] = [(after(grad, late_gots[1]), *where)]
    to_cores = forward_to_core, backward_term(0, 2 * count, [])
    add_late(1, *to_cores)

    def spread_rows(term, to_core, ways):
        width = features // len(ways)
        from_core = trade(to_core, "gx", 1)
        sums = [way(term, from_core, (place * width, width)) for place, way in enumerate(ways)]
        return jnp.concatenate(sums, axis=1)

    normed_grad = spread_rows(backward_term, to_cores[1], (over_x_z, over_z_x))
    layer_out = half(wide + spread_rows(forward_term, to_cores[0], (over_x_z, over_x_z)))
    first, second = lax.psum(
        (jnp.sum(normed_grad, axis=1), jnp.sum(normed_grad * normed, axis=1)), "gz"
    )
    grad_full = out_cotangent.astype(jnp.float32) + inverse[:, None] * (
        normed_grad - (first / D)[:, None] - normed * (second / D)[:, None]
    )
    return (layer_out, half(grad_full))


def solution(mesh):
    in_specs = (
        P(("gx", "gy"), "gz"),
        P(("gx", "gy"), "gz"),
        P(("gz", "gx"), "gy"),
        P(("gz", "gx"), "gy"),
        P(("gz", "gx"), "gy"),
        P(("gz", "gx"), "gy"),
        P(("gy", "gx"), "gz"),
        P(("gy", "gx"), "gz"),
    )
    out_specs = (P(("gx", "gy"), "gz"), P(("gx", "gy"), "gz"))
    return jax.shard_map(body, mesh=mesh, in_specs=in_specs, out_specs=out_specs, check_vma=False)
```

```python
import functools
import math

import jax
import jax.numpy as jnp
from jax import lax
from jax.experimental import pallas as pl
from jax.experimental.pallas import tpu as pltpu
from jax.sharding import PartitionSpec as P

D = 6144
HEAD_DIM = 128
IMG_TOK = 256


EPSILON = 1e-06
ROOT_HALF = 0.7071067811865476
ROOT_TWO_PI_INV = 0.3989422804014327


def attend_kernel(
    q_own, q_got, k_own, k_got, v_own, v_got, g_ref, mixed_ref, dq_ref, dk_ref, dv_ref, *, scale
):
    def total(own, got):
        return own[...].astype(jnp.float32) + got[...].astype(jnp.float32)

    def norm(values):
        center = values - jnp.mean(values, axis=-1, keepdims=True)
        spread = jnp.mean(center * center, axis=-1, keepdims=True)
        inverse = lax.rsqrt(spread + EPSILON)
        return center * inverse, inverse

    def norm_back(grad, normed, inverse):
        slope = inverse * (grad - normed * jnp.mean(grad * normed, axis=-1, keepdims=True))
        return (slope - jnp.mean(slope, axis=-1, keepdims=True)).astype(jnp.bfloat16)

    def contract(left, right, left_dim, right_dim):
        return lax.dot_general(
            left,
            right,
            (((left_dim,), (right_dim,)), ((), ())),
            preferred_element_type=jnp.float32,
        )

    def half(values):
        return values.astype(jnp.bfloat16)

    q_norm, q_inverse = norm(total(q_own, q_got))
    k_norm, k_inverse = norm(total(k_own, k_got))
    q_half, k_half = half(q_norm), half(k_norm)
    v_half = half(total(v_own, v_got))
    grad = g_ref[...]
    weights = jnp.exp(contract(q_half, k_half, 1, 1) * scale)
    probs = weights / jnp.sum(weights, axis=-1, keepdims=True)
    probs_half = half(probs)
    mixed_ref[...] = half(contract(probs_half, v_half, 1, 0))
    dv_ref[...] = half(contract(probs_half, grad, 0, 0))
    probs_grad = half(contract(grad, v_half, 1, 1)).astype(jnp.float32)
    inner = jnp.sum(probs_grad * probs, axis=-1, keepdims=True)
    score_grad = half(probs * (probs_grad - inner) * scale)
    q_grad = half(contract(score_grad, k_half, 1, 0)).astype(jnp.float32)
    k_grad = half(contract(score_grad, q_half, 0, 0)).astype(jnp.float32)
    dq_ref[...] = norm_back(q_grad, q_norm, q_inverse)
    dk_ref[...] = norm_back(k_grad, k_norm, k_inverse)


def attend(own, got, grad):
    rows, width = own.shape[0], own.shape[1] // 3
    heads = width // HEAD_DIM

    def block(part):
        return pl.BlockSpec((IMG_TOK, HEAD_DIM), lambda image, head: (image, part * heads + head))

    half = jax.ShapeDtypeStruct((rows, width), jnp.bfloat16)
    return pl.pallas_call(
        functools.partial(attend_kernel, scale=1.0 / math.sqrt(HEAD_DIM)),
        grid=(rows // IMG_TOK, heads),
        in_specs=[block(0), block(0), block(1), block(1), block(2), block(2), block(0)],
        out_specs=[block(0)] * 4,
        out_shape=[half] * 4,
        compiler_params=pltpu.CompilerParams(vmem_limit_bytes=32 * 1024 * 1024),
        cost_estimate=pl.CostEstimate(
            flops=rows * IMG_TOK * width // 8,
            bytes_accessed=rows * width // 4,
            transcendentals=0,
        ),
        name="attend",
    )(own, got, own, got, own, got, grad)


def gelu(pre):
    return pre * 0.5 * (1.0 + lax.erf(pre * ROOT_HALF))


def gelu_back(pre, grad_half):
    cdf = 0.5 * (1.0 + lax.erf(pre * ROOT_HALF))
    pdf = jnp.exp(-0.5 * pre * pre) * ROOT_TWO_PI_INV
    return (grad_half.astype(jnp.float32) * (cdf + pre * pdf)).astype(jnp.bfloat16)


def dot(left, right):
    return jnp.dot(left, right, preferred_element_type=jnp.float32)


def back_dot(left, right):
    return lax.dot_general(
        left, right, (((1,), (1,)), ((), ())), preferred_element_type=jnp.float32
    )


def half(values):
    return values.astype(jnp.bfloat16)


def wide_sum(own, got):
    return own.astype(jnp.float32) + got.astype(jnp.float32)


def trade(block, axis, bit):
    pairs = [(index, index ^ bit) for index in range(lax.axis_size(axis))]
    return lax.ppermute(block, axis, pairs)


VMEM_LIMIT = 48 * 1024 * 1024


def params():
    return pltpu.CompilerParams(vmem_limit_bytes=VMEM_LIMIT)


def cost(flops, *arrays):
    moved = sum(math.prod(array.shape) * array.dtype.itemsize for array in arrays)
    return pl.CostEstimate(flops=flops // 64, bytes_accessed=moved // 64, transcendentals=0)


def pack_kernel(*refs):
    out_ref, start = refs[-1], 0
    for ref in refs[:-1]:
        out_ref[0, :, start : start + ref.shape[1]] = ref[...]
        start += ref.shape[1]


def pack(weights, owners, start, width, tile):
    rows, columns = weights[0].shape
    first, blocks = start // tile, columns // owners // tile
    out = jax.ShapeDtypeStruct((owners, rows, len(weights) * width), weights[0].dtype)
    spec = pl.BlockSpec((rows, tile), lambda owner, n: (0, owner * blocks + first + n))
    return pl.pallas_call(
        pack_kernel,
        grid=(owners, width // tile),
        in_specs=[spec] * len(weights),
        out_specs=pl.BlockSpec((1, rows, len(weights) * tile), lambda owner, n: (owner, 0, n)),
        out_shape=out,
        compiler_params=params(),
        cost_estimate=cost(0, out, out),
        name="pack",
    )(*weights)


IMAGE_ORDER = ((1, 1), (0, 1), (1, 0), (0, 0))


def assemble_kernel(*refs):
    parts, out_ref = refs[:-1], refs[-1]
    rows = parts[0].shape[1]
    start = 0
    for x_bit, core_bit in IMAGE_ORDER:
        for part in range(len(parts) // 2):
            out_ref[start : start + rows, :] = parts[2 * part + core_bit][x_bit]
            start += rows


def assemble(parts):
    flat = [value for part in parts for value in part]
    _, rows, features = flat[0].shape
    tile = 768
    out = jax.ShapeDtypeStruct((len(flat) * 2 * rows, features), flat[0].dtype)
    return pl.pallas_call(
        assemble_kernel,
        grid=(features // tile,),
        in_specs=[pl.BlockSpec((2, rows, tile), lambda n: (0, 0, n))] * len(flat),
        out_specs=pl.BlockSpec((out.shape[0], tile), lambda n: (0, n)),
        out_shape=out,
        compiler_params=params(),
        cost_estimate=cost(0, out, out),
        name="assemble",
    )(*flat)


def cot_kernel(own_ref, other_ref, attn_ref, mlp_ref, out_ref, rows_ref):
    rows = own_ref.shape[1]
    step = pl.program_id(0)

    @pl.when(step == 0)
    def _():
        for place, (x_bit, core_bit) in enumerate(IMAGE_ORDER):
            part = other_ref if core_bit else own_ref
            rows_ref[place * rows : (place + 1) * rows, :] = part[x_bit]
        out_ref[...] = half(back_dot(rows_ref[...], attn_ref[...]))

    @pl.when(step > 0)
    def _():
        out_ref[...] = half(back_dot(rows_ref[...], mlp_ref[...]))


def cot_product(part, w_attn_out, w_mlp_out):
    own, other = part
    _, rows, features = own.shape
    tile = w_attn_out.shape[0]
    columns = tile + w_mlp_out.shape[0]
    count = len(IMAGE_ORDER) * rows
    out = jax.ShapeDtypeStruct((count, columns), jnp.bfloat16)
    whole = pl.BlockSpec(own.shape, lambda n: (0, 0, 0))
    return pl.pallas_call(
        cot_kernel,
        grid=(columns // tile,),
        in_specs=[
            whole,
            whole,
            pl.BlockSpec((tile, features), lambda n: (0, 0)),
            pl.BlockSpec((tile, features), lambda n: (jnp.maximum(n - 1, 0), 0)),
        ],
        out_specs=pl.BlockSpec((count, tile), lambda n: (0, n)),
        out_shape=out,
        scratch_shapes=[pltpu.VMEM((count, features), jnp.bfloat16)],
        compiler_params=params(),
        cost_estimate=cost(2 * count * columns * features, out, w_attn_out, w_mlp_out),
        name="cot_product",
    )(own, other, w_attn_out, w_mlp_out)


def add_kernel(*refs):
    terms, out_ref = refs[:-1], refs[-1]
    count = len(terms) // 2
    for part in range(count):
        out_ref[0, part] = half(wide_sum(terms[part][0], terms[count + part][0]))


def add_parts(owns, gots):
    images, parts = len(IMAGE_ORDER), len(owns)
    rows, columns = owns[0].shape[0] // images, owns[0].shape[1]
    out = jax.ShapeDtypeStruct((images, parts, rows, columns), jnp.bfloat16)
    terms = [value.reshape(images, rows, columns) for value in (*owns, *gots)]
    added = pl.pallas_call(
        add_kernel,
        grid=(images,),
        in_specs=[pl.BlockSpec((1, rows, columns), lambda image: (image, 0, 0))] * len(terms),
        out_specs=pl.BlockSpec((1, parts, rows, columns), lambda image: (image, 0, 0, 0)),
        out_shape=out,
        compiler_params=params(),
        cost_estimate=cost(0, out, out, out),
        name="add_parts",
    )(*terms)
    return added.reshape(images * parts * rows, columns)


def in_kernel(rows_ref, weight_ref, out_ref):
    out_ref[...] = half(dot(rows_ref[...], weight_ref[...]))


def in_product(rows, weight, half_index=None):
    count, features = rows.shape
    first = half_index or 0
    count = count if half_index is None else count // 2
    columns = weight.shape[1]
    tile = 384 if columns % 384 == 0 else 256
    out = jax.ShapeDtypeStruct((count, columns), jnp.bfloat16)
    return pl.pallas_call(
        in_kernel,
        grid=(columns // tile,),
        in_specs=[
            pl.BlockSpec((count, features), lambda n: (first, 0)),
            pl.BlockSpec((features, tile), lambda n: (0, n)),
        ],
        out_specs=pl.BlockSpec((count, tile), lambda n: (0, n)),
        out_shape=out,
        compiler_params=params(),
        cost_estimate=cost(2 * count * columns * features, rows, out, weight),
        name="in_product",
    )(rows, weight)


def product(terms, weights, adds, start, count, kind, transposed, window=None, rows=None):
    whole = weights[0].shape[0 if transposed else 1]
    first_column, columns = window or (0, whole)
    tile = 512 if columns % 512 == 0 else 384 if columns % 384 == 0 else 256
    skip = first_column // tile
    specs = [
        pl.BlockSpec(
            (count, value.shape[1]), lambda n, place=(start - row) // count: (place, 0)
        )
        for value, _, _, row in terms
    ]
    for weight in weights:
        if transposed:
            specs.append(pl.BlockSpec((tile, weight.shape[1]), lambda n: (n + skip, 0)))
        else:
            block, size = rows or (0, weight.shape[0])
            specs.append(pl.BlockSpec((size, tile), lambda n, block=block: (block, n + skip)))
    for _, first in adds:
        specs.append(
            pl.BlockSpec((count, tile), lambda n, place=first // count: (place, n + skip))
        )

    def kernel(*refs):
        weight_refs = refs[len(terms) : len(terms) + len(weights)]
        total = None
        for ref, (value, index, offset, _) in zip(refs, terms):
            summed = slice(offset, offset + value.shape[1])
            if transposed:
                part = back_dot(ref[...], weight_refs[index][:, summed])
            else:
                part = dot(ref[...], weight_refs[index][summed, :])
            total = part if total is None else total + part
        for ref in refs[len(terms) + len(weights) : -1]:
            total = total + ref[...].astype(jnp.float32)
        refs[-1][...] = total.astype(kind)

    depth = sum(value.shape[1] for value, *_ in terms)
    out = jax.ShapeDtypeStruct((count, columns), kind)
    return pl.pallas_call(
        kernel,
        grid=(columns // tile,),
        in_specs=specs,
        out_specs=pl.BlockSpec((count, tile), lambda n: (0, n)),
        out_shape=out,
        compiler_params=params(),
        cost_estimate=cost(2 * count * columns * depth, out, *weights),
        name="back_product" if transposed else "out_product",
    )(*(value for value, *_ in terms), *weights, *(add for add, _ in adds))


MLP_CUTS = (512, 256, 768)


def body(layer_input, out_cotangent, w_query, w_key, w_value, w_mlp_in, w_attn_out, w_mlp_out):
    n_gx, n_gz = lax.axis_size("gx"), lax.axis_size("gz")
    own_rows, features = layer_input.shape
    count = own_rows * lax.axis_size("gy")

    def after(value, *earlier):
        return lax.optimization_barrier((value, earlier))[0]

    def others(part):
        if n_gz == 2:
            return trade(part, "gz", 1)
        return half(lax.psum(part.astype(jnp.float32), "gz") - part.astype(jnp.float32))

    def with_x(block):
        return jnp.stack([block, trade(block, "gx", 2)])

    def over_z(pair):
        return [pair, trade(pair, "gy", 1), trade(pair, "gy", 2)]

    def with_core(part):
        return part, trade(part, "gx", 1)

    def swap(packed):
        swapped = lax.all_to_all(packed, "gx", split_axis=0, concat_axis=0, tiled=True)
        return swapped.reshape(n_gx * packed.shape[1], packed.shape[2])

    heads_width = w_query.shape[1] // n_gx
    packed_heads = pack((w_query, w_key, w_value), n_gx, 0, heads_width, heads_width)
    starts = [sum(MLP_CUTS[:cut]) for cut in range(len(MLP_CUTS))]
    packed_mlp = [
        pack((w_mlp_in,), n_gx, start, width, 256) for start, width in zip(starts, MLP_CUTS)
    ]

    cot_pair = with_x(out_cotangent)
    wide = layer_input.astype(jnp.float32)
    total, squares = lax.psum((jnp.sum(wide, axis=1), jnp.sum(wide * wide, axis=1)), "gz")
    center = total / D
    spread = squares / D - center * center
    inverse = lax.rsqrt(spread + EPSILON)
    normed = (wide - center[:, None]) * inverse[:, None]
    normed_pair = with_x(half(normed))

    cot_parts, normed_parts = over_z(cot_pair), over_z(normed_pair)
    cot_parts.append(trade(cot_parts[2], "gy", 1))
    cot_owns, cot_gots = [], []
    for place, part in enumerate(cot_parts):
        own, other = with_core(part)
        if place == 2:
            own = after(own, cot_owns[1], cot_gots[0], normed_parts[1])
        if place == 3:
            own = after(own, cot_gots[1])
        cot_owns.append(cot_product((own, other), w_attn_out, w_mlp_out))
        cot_gots.append(others(cot_owns[-1]))
    normed_parts.append(trade(after(normed_parts[2], *cot_owns[1:4]), "gy", 1))
    normed_parts = [with_core(part) for part in normed_parts]
    normed_parts[0] = after(normed_parts[0], cot_owns[3], cot_gots[2])
    all_in = assemble(normed_parts)

    in_heads = swap(after(packed_heads, normed_pair, cot_owns[0]))
    early = (cot_owns[2], cot_gots[1], cot_parts[3])
    in_mlp = [swap(after(packed_mlp[0], in_heads, *early))]
    in_mlp.append(swap(after(packed_mlp[1], in_mlp[0], all_in)))
    heads_own = in_product(after(all_in, cot_gots[3]), in_heads)
    heads_got = others(heads_own)
    mlp_own = [in_product(after(all_in, heads_own, in_mlp[1]), in_mlp[0])]
    mlp_got = [others(mlp_own[0])]
    in_mlp.append(swap(after(packed_mlp[2], in_mlp[1], heads_own)))
    mlp_own.append(in_product(after(all_in, mlp_own[0]), in_mlp[1]))
    mlp_got.append(others(mlp_own[1]))

    out_grad = add_parts(after(cot_owns, mlp_own[0]), cot_gots)
    late_owns = [in_product(after(all_in, heads_got, out_grad), in_mlp[2], 0)]
    late_gots = [others(late_owns[0])]
    late_owns.append(in_product(after(all_in, late_owns[0]), in_mlp[2], 1))
    late_gots.append(others(late_owns[1]))

    mixed, *head_grads = attend(heads_own, heads_got, out_grad)

    def mlp_terms(cut, first_row, own, got):
        pre = wide_sum(own, got)
        column = heads_width + starts[cut]
        rows = slice(first_row, first_row + own.shape[0])
        grad = gelu_back(pre, out_grad[rows, column : column + own.shape[1]])
        return half(gelu(pre)), grad

    forward_terms = [(after(mixed, late_owns), 0, 0, 0)]
    backward_terms = [
        (grad, 0, index * heads_width, 0) for index, grad in enumerate(head_grads)
    ]
    for cut in range(2):
        act, grad = mlp_terms(cut, 0, after(mlp_own[cut], mixed), mlp_got[cut])
        forward_terms.append((act, 1, starts[cut], 0))
        backward_terms.append((grad, 1 + cut, 0, 0))
    rows = 4 * count
    forward_early = product(
        forward_terms, [w_attn_out, w_mlp_out], [], 0, rows, jnp.bfloat16, False
    )
    backward_early = product(
        backward_terms, [in_heads, *in_mlp[:2]], [], 0, rows, jnp.bfloat16, True
    )
    forward_late, backward_late = [], []

    def add_late(part, *earlier):
        first_row = part * 2 * count
        own = after(late_owns[part], *earlier)
        act, grad = mlp_terms(2, first_row, own, late_gots[part])
        forward_late.append([(act, 0, 0, first_row)])
        backward_late.append([(grad, 0, 0, first_row)])

    late_rows = (starts[2] // MLP_CUTS[2], MLP_CUTS[2])

    def forward_term(start, size, adds, window=None):
        adds, terms = [(forward_early, start), *adds], forward_late[start // (2 * count)]
        return product(
            terms, [w_mlp_out], adds, start, size, jnp.bfloat16, False, window, late_rows
        )

    def backward_term(start, size, adds, window=None):
        adds, terms = [(backward_early, start), *adds], backward_late[start // (2 * count)]
        return product(terms, [in_mlp[2]], adds, start, size, jnp.bfloat16, True, window)

    def wider(value):
        return value.astype(jnp.float32)

    def over_x_z(term, from_core, window):
        from_x = trade(term(2 * count, count, [(from_core, 0)], window), "gx", 2)
        mine = wide_sum(term(3 * count, count, [(from_core, count)], window), from_x)
        mine = mine.reshape(2, 2, own_rows, window[1])
        pair = mine[:, 0] + wider(trade(half(mine[:, 1]), "gy", 1))
        return pair[0] + wider(trade(half(pair[1]), "gy", 2))

    def over_z_x(term, from_core, window):
        both = term(2 * count, 2 * count, [(from_core, 0)], window)
        both = both.reshape(2, 2, 2, own_rows, window[1])
        pair = wide_sum(both[:, :, 0], trade(both[:, :, 1], "gy", 1))
        ends = pair[:, 0] + wider(trade(half(pair[:, 1]), "gy", 2))
        return ends[1] + wider(trade(half(ends[0]), "gx", 2))

    add_late(0, forward_early, backward_early)
    forward_to_core = forward_term(0, 2 * count, [])
    (grad, *where), *_ = backward_late[0]
    backward_late[0] = [(after(grad, late_gots[1]), *where)]
    to_cores = forward_to_core, backward_term(0, 2 * count, [])
    add_late(1, *to_cores)

    def spread_rows(term, to_core, ways):
        width = features // len(ways)
        from_core = trade(to_core, "gx", 1)
        sums = [way(term, from_core, (place * width, width)) for place, way in enumerate(ways)]
        return jnp.concatenate(sums, axis=1)

    normed_grad = spread_rows(backward_term, to_cores[1], (over_x_z, over_z_x))
    layer_out = half(wide + spread_rows(forward_term, to_cores[0], (over_x_z, over_x_z)))
    first, second = lax.psum(
        (jnp.sum(normed_grad, axis=1), jnp.sum(normed_grad * normed, axis=1)), "gz"
    )
    grad_full = out_cotangent.astype(jnp.float32) + inverse[:, None] * (
        normed_grad - (first / D)[:, None] - normed * (second / D)[:, None]
    )
    return (layer_out, half(grad_full))


def solution(mesh):
    in_specs = (
        P(("gx", "gy"), "gz"),
        P(("gx", "gy"), "gz"),
        P(("gz", "gx"), "gy"),
        P(("gz", "gx"), "gy"),
        P(("gz", "gx"), "gy"),
        P(("gz", "gx"), "gy"),
        P(("gy", "gx"), "gz"),
        P(("gy", "gx"), "gz"),
    )
    out_specs = (P(("gx", "gy"), "gz"), P(("gx", "gy"), "gz"))
    return jax.shard_map(body, mesh=mesh, in_specs=in_specs, out_specs=out_specs, check_vma=False)
```

```python
import functools
import math

import jax
import jax.numpy as jnp
from jax import lax
from jax.experimental import pallas as pl
from jax.experimental.pallas import tpu as pltpu
from jax.sharding import PartitionSpec as P

D = 6144
HEAD_DIM = 128
IMG_TOK = 256


EPSILON = 1e-06
ROOT_HALF = 0.7071067811865476
ROOT_TWO_PI_INV = 0.3989422804014327


def attend_kernel(
    q_own, q_got, k_own, k_got, v_own, v_got, g_ref, mixed_ref, dq_ref, dk_ref, dv_ref, *, scale
):
    def total(own, got):
        return own[...].astype(jnp.float32) + got[...].astype(jnp.float32)

    def norm(values):
        center = values - jnp.mean(values, axis=-1, keepdims=True)
        spread = jnp.mean(center * center, axis=-1, keepdims=True)
        inverse = lax.rsqrt(spread + EPSILON)
        return center * inverse, inverse

    def norm_back(grad, normed, inverse):
        slope = inverse * (grad - normed * jnp.mean(grad * normed, axis=-1, keepdims=True))
        return (slope - jnp.mean(slope, axis=-1, keepdims=True)).astype(jnp.bfloat16)

    def contract(left, right, left_dim, right_dim):
        return lax.dot_general(
            left,
            right,
            (((left_dim,), (right_dim,)), ((), ())),
            preferred_element_type=jnp.float32,
        )

    def half(values):
        return values.astype(jnp.bfloat16)

    q_norm, q_inverse = norm(total(q_own, q_got))
    k_norm, k_inverse = norm(total(k_own, k_got))
    q_half, k_half = half(q_norm), half(k_norm)
    v_half = half(total(v_own, v_got))
    grad = g_ref[...]
    weights = jnp.exp(contract(q_half, k_half, 1, 1) * scale)
    probs = weights / jnp.sum(weights, axis=-1, keepdims=True)
    probs_half = half(probs)
    mixed_ref[...] = half(contract(probs_half, v_half, 1, 0))
    dv_ref[...] = half(contract(probs_half, grad, 0, 0))
    probs_grad = half(contract(grad, v_half, 1, 1)).astype(jnp.float32)
    inner = jnp.sum(probs_grad * probs, axis=-1, keepdims=True)
    score_grad = half(probs * (probs_grad - inner) * scale)
    q_grad = half(contract(score_grad, k_half, 1, 0)).astype(jnp.float32)
    k_grad = half(contract(score_grad, q_half, 0, 0)).astype(jnp.float32)
    dq_ref[...] = norm_back(q_grad, q_norm, q_inverse)
    dk_ref[...] = norm_back(k_grad, k_norm, k_inverse)


def attend(own, got, grad):
    rows, width = own.shape[0], own.shape[1] // 3
    heads = width // HEAD_DIM

    def block(part):
        return pl.BlockSpec((IMG_TOK, HEAD_DIM), lambda image, head: (image, part * heads + head))

    half = jax.ShapeDtypeStruct((rows, width), jnp.bfloat16)
    return pl.pallas_call(
        functools.partial(attend_kernel, scale=1.0 / math.sqrt(HEAD_DIM)),
        grid=(rows // IMG_TOK, heads),
        in_specs=[block(0), block(0), block(1), block(1), block(2), block(2), block(0)],
        out_specs=[block(0)] * 4,
        out_shape=[half] * 4,
        compiler_params=pltpu.CompilerParams(vmem_limit_bytes=32 * 1024 * 1024),
        cost_estimate=pl.CostEstimate(
            flops=rows * IMG_TOK * width // 8,
            bytes_accessed=rows * width // 4,
            transcendentals=0,
        ),
        name="attend",
    )(own, got, own, got, own, got, grad)


def gelu(pre):
    return pre * 0.5 * (1.0 + lax.erf(pre * ROOT_HALF))


def gelu_back(pre, grad_half):
    cdf = 0.5 * (1.0 + lax.erf(pre * ROOT_HALF))
    pdf = jnp.exp(-0.5 * pre * pre) * ROOT_TWO_PI_INV
    return (grad_half.astype(jnp.float32) * (cdf + pre * pdf)).astype(jnp.bfloat16)


def dot(left, right):
    return jnp.dot(left, right, preferred_element_type=jnp.float32)


def back_dot(left, right):
    return lax.dot_general(
        left, right, (((1,), (1,)), ((), ())), preferred_element_type=jnp.float32
    )


def half(values):
    return values.astype(jnp.bfloat16)


def wide_sum(own, got):
    return own.astype(jnp.float32) + got.astype(jnp.float32)


def trade(block, axis, bit):
    pairs = [(index, index ^ bit) for index in range(lax.axis_size(axis))]
    return lax.ppermute(block, axis, pairs)


VMEM_LIMIT = 48 * 1024 * 1024


def params():
    return pltpu.CompilerParams(vmem_limit_bytes=VMEM_LIMIT)


def cost(flops, *arrays):
    moved = sum(math.prod(array.shape) * array.dtype.itemsize for array in arrays)
    return pl.CostEstimate(flops=flops // 64, bytes_accessed=moved // 64, transcendentals=0)


def pack_kernel(*refs):
    out_ref, start = refs[-1], 0
    for ref in refs[:-1]:
        out_ref[0, :, start : start + ref.shape[1]] = ref[...]
        start += ref.shape[1]


def pack(weights, owners, start, width, tile):
    rows, columns = weights[0].shape
    first, blocks = start // tile, columns // owners // tile
    out = jax.ShapeDtypeStruct((owners, rows, len(weights) * width), weights[0].dtype)
    spec = pl.BlockSpec((rows, tile), lambda owner, n: (0, owner * blocks + first + n))
    return pl.pallas_call(
        pack_kernel,
        grid=(owners, width // tile),
        in_specs=[spec] * len(weights),
        out_specs=pl.BlockSpec((1, rows, len(weights) * tile), lambda owner, n: (owner, 0, n)),
        out_shape=out,
        compiler_params=params(),
        cost_estimate=cost(0, out, out),
        name="pack",
    )(*weights)


IMAGE_ORDER = ((1, 1), (0, 1), (1, 0), (0, 0))


def assemble_kernel(*refs):
    parts, out_ref = refs[:-1], refs[-1]
    rows = parts[0].shape[1]
    start = 0
    for x_bit, core_bit in IMAGE_ORDER:
        for part in range(len(parts) // 2):
            out_ref[start : start + rows, :] = parts[2 * part + core_bit][x_bit]
            start += rows


def assemble(parts):
    flat = [value for part in parts for value in part]
    _, rows, features = flat[0].shape
    tile = 768
    out = jax.ShapeDtypeStruct((len(flat) * 2 * rows, features), flat[0].dtype)
    return pl.pallas_call(
        assemble_kernel,
        grid=(features // tile,),
        in_specs=[pl.BlockSpec((2, rows, tile), lambda n: (0, 0, n))] * len(flat),
        out_specs=pl.BlockSpec((out.shape[0], tile), lambda n: (0, n)),
        out_shape=out,
        compiler_params=params(),
        cost_estimate=cost(0, out, out),
        name="assemble",
    )(*flat)


def cot_kernel(own_ref, other_ref, attn_ref, mlp_ref, out_ref, rows_ref):
    rows = own_ref.shape[1]
    step = pl.program_id(0)

    @pl.when(step == 0)
    def _():
        for place, (x_bit, core_bit) in enumerate(IMAGE_ORDER):
            part = other_ref if core_bit else own_ref
            rows_ref[place * rows : (place + 1) * rows, :] = part[x_bit]
        out_ref[...] = half(back_dot(rows_ref[...], attn_ref[...]))

    @pl.when(step > 0)
    def _():
        out_ref[...] = half(back_dot(rows_ref[...], mlp_ref[...]))


def cot_product(part, w_attn_out, w_mlp_out):
    own, other = part
    _, rows, features = own.shape
    tile = w_attn_out.shape[0]
    columns = tile + w_mlp_out.shape[0]
    count = len(IMAGE_ORDER) * rows
    out = jax.ShapeDtypeStruct((count, columns), jnp.bfloat16)
    whole = pl.BlockSpec(own.shape, lambda n: (0, 0, 0))
    return pl.pallas_call(
        cot_kernel,
        grid=(columns // tile,),
        in_specs=[
            whole,
            whole,
            pl.BlockSpec((tile, features), lambda n: (0, 0)),
            pl.BlockSpec((tile, features), lambda n: (jnp.maximum(n - 1, 0), 0)),
        ],
        out_specs=pl.BlockSpec((count, tile), lambda n: (0, n)),
        out_shape=out,
        scratch_shapes=[pltpu.VMEM((count, features), jnp.bfloat16)],
        compiler_params=params(),
        cost_estimate=cost(2 * count * columns * features, out, w_attn_out, w_mlp_out),
        name="cot_product",
    )(own, other, w_attn_out, w_mlp_out)


def add_kernel(*refs):
    terms, out_ref = refs[:-1], refs[-1]
    count = len(terms) // 2
    for part in range(count):
        out_ref[0, part] = half(wide_sum(terms[part][0], terms[count + part][0]))


def add_parts(owns, gots):
    images, parts = len(IMAGE_ORDER), len(owns)
    rows, columns = owns[0].shape[0] // images, owns[0].shape[1]
    out = jax.ShapeDtypeStruct((images, parts, rows, columns), jnp.bfloat16)
    terms = [value.reshape(images, rows, columns) for value in (*owns, *gots)]
    added = pl.pallas_call(
        add_kernel,
        grid=(images,),
        in_specs=[pl.BlockSpec((1, rows, columns), lambda image: (image, 0, 0))] * len(terms),
        out_specs=pl.BlockSpec((1, parts, rows, columns), lambda image: (image, 0, 0, 0)),
        out_shape=out,
        compiler_params=params(),
        cost_estimate=cost(0, out, out, out),
        name="add_parts",
    )(*terms)
    return added.reshape(images * parts * rows, columns)


def in_kernel(rows_ref, weight_ref, out_ref):
    out_ref[...] = half(dot(rows_ref[...], weight_ref[...]))


def in_product(rows, weight, half_index=None):
    count, features = rows.shape
    first = half_index or 0
    count = count if half_index is None else count // 2
    columns = weight.shape[1]
    tile = 384 if columns % 384 == 0 else 256
    out = jax.ShapeDtypeStruct((count, columns), jnp.bfloat16)
    return pl.pallas_call(
        in_kernel,
        grid=(columns // tile,),
        in_specs=[
            pl.BlockSpec((count, features), lambda n: (first, 0)),
            pl.BlockSpec((features, tile), lambda n: (0, n)),
        ],
        out_specs=pl.BlockSpec((count, tile), lambda n: (0, n)),
        out_shape=out,
        compiler_params=params(),
        cost_estimate=cost(2 * count * columns * features, rows, out, weight),
        name="in_product",
    )(rows, weight)


def product(terms, weights, adds, start, count, kind, transposed, window=None, rows=None):
    whole = weights[0].shape[0 if transposed else 1]
    first_column, columns = window or (0, whole)
    tile = 512 if columns % 512 == 0 else 384 if columns % 384 == 0 else 256
    skip = first_column // tile
    specs = [
        pl.BlockSpec(
            (count, value.shape[1]), lambda n, place=(start - row) // count: (place, 0)
        )
        for value, _, _, row in terms
    ]
    for weight in weights:
        if transposed:
            specs.append(pl.BlockSpec((tile, weight.shape[1]), lambda n: (n + skip, 0)))
        else:
            block, size = rows or (0, weight.shape[0])
            specs.append(pl.BlockSpec((size, tile), lambda n, block=block: (block, n + skip)))
    for _, first in adds:
        specs.append(
            pl.BlockSpec((count, tile), lambda n, place=first // count: (place, n + skip))
        )

    def kernel(*refs):
        weight_refs = refs[len(terms) : len(terms) + len(weights)]
        total = None
        for ref, (value, index, offset, _) in zip(refs, terms):
            summed = slice(offset, offset + value.shape[1])
            if transposed:
                part = back_dot(ref[...], weight_refs[index][:, summed])
            else:
                part = dot(ref[...], weight_refs[index][summed, :])
            total = part if total is None else total + part
        for ref in refs[len(terms) + len(weights) : -1]:
            total = total + ref[...].astype(jnp.float32)
        refs[-1][...] = total.astype(kind)

    depth = sum(value.shape[1] for value, *_ in terms)
    out = jax.ShapeDtypeStruct((count, columns), kind)
    return pl.pallas_call(
        kernel,
        grid=(columns // tile,),
        in_specs=specs,
        out_specs=pl.BlockSpec((count, tile), lambda n: (0, n)),
        out_shape=out,
        compiler_params=params(),
        cost_estimate=cost(2 * count * columns * depth, out, *weights),
        name="back_product" if transposed else "out_product",
    )(*(value for value, *_ in terms), *weights, *(add for add, _ in adds))


MLP_CUTS = (512, 256, 768)


def body(layer_input, out_cotangent, w_query, w_key, w_value, w_mlp_in, w_attn_out, w_mlp_out):
    n_gx, n_gz = lax.axis_size("gx"), lax.axis_size("gz")
    own_rows, features = layer_input.shape
    count = own_rows * lax.axis_size("gy")

    def after(value, *earlier):
        return lax.optimization_barrier((value, earlier))[0]

    def others(part):
        if n_gz == 2:
            return trade(part, "gz", 1)
        return half(lax.psum(part.astype(jnp.float32), "gz") - part.astype(jnp.float32))

    def with_x(block):
        return jnp.stack([block, trade(block, "gx", 2)])

    def over_z(pair):
        return [pair, trade(pair, "gy", 1), trade(pair, "gy", 2)]

    def with_core(part):
        return part, trade(part, "gx", 1)

    def swap(packed):
        swapped = lax.all_to_all(packed, "gx", split_axis=0, concat_axis=0, tiled=True)
        return swapped.reshape(n_gx * packed.shape[1], packed.shape[2])

    heads_width = w_query.shape[1] // n_gx
    packed_heads = pack((w_query, w_key, w_value), n_gx, 0, heads_width, heads_width)
    starts = [sum(MLP_CUTS[:cut]) for cut in range(len(MLP_CUTS))]
    packed_mlp = [
        pack((w_mlp_in,), n_gx, start, width, 256) for start, width in zip(starts, MLP_CUTS)
    ]

    cot_pair = with_x(out_cotangent)
    wide = layer_input.astype(jnp.float32)
    total, squares = lax.psum((jnp.sum(wide, axis=1), jnp.sum(wide * wide, axis=1)), "gz")
    center = total / D
    spread = squares / D - center * center
    inverse = lax.rsqrt(spread + EPSILON)
    normed = (wide - center[:, None]) * inverse[:, None]
    normed_pair = with_x(half(normed))

    cot_parts, normed_parts = over_z(cot_pair), over_z(normed_pair)
    cot_parts.append(trade(cot_parts[2], "gy", 1))
    cot_owns, cot_gots = [], []
    for place, part in enumerate(cot_parts):
        own, other = with_core(part)
        if place == 2:
            own = after(own, cot_owns[1], cot_gots[0], normed_parts[1])
        if place == 3:
            own = after(own, cot_gots[1])
        cot_owns.append(cot_product((own, other), w_attn_out, w_mlp_out))
        cot_gots.append(others(cot_owns[-1]))
    normed_parts.append(trade(after(normed_parts[2], *cot_owns[1:3]), "gy", 1))
    normed_parts = [with_core(part) for part in normed_parts]
    normed_parts[0] = after(normed_parts[0], cot_owns[3], cot_gots[2])
    all_in = assemble(normed_parts)

    in_heads = swap(after(packed_heads, normed_pair, cot_owns[0]))
    early = (cot_owns[2], cot_gots[1], cot_parts[3])
    in_mlp = [swap(after(packed_mlp[0], in_heads, *early))]
    in_mlp.append(swap(after(packed_mlp[1], in_mlp[0], all_in, cot_gots[3])))
    heads_own = in_product(after(all_in, cot_gots[3]), in_heads)
    heads_got = others(heads_own)
    mlp_own = [in_product(after(all_in, heads_own, in_mlp[1]), in_mlp[0])]
    mlp_got = [others(mlp_own[0])]
    in_mlp.append(swap(after(packed_mlp[2], in_mlp[1], heads_own)))
    mlp_own.append(in_product(after(all_in, mlp_own[0]), in_mlp[1]))
    mlp_got.append(others(mlp_own[1]))

    out_grad = add_parts(after(cot_owns, mlp_own[0]), cot_gots)
    late_owns = [in_product(after(all_in, heads_got, out_grad), in_mlp[2], 0)]
    late_gots = [others(late_owns[0])]
    late_owns.append(in_product(after(all_in, late_owns[0]), in_mlp[2], 1))
    late_gots.append(others(late_owns[1]))

    mixed, *head_grads = attend(heads_own, heads_got, out_grad)

    def mlp_terms(cut, first_row, own, got):
        pre = wide_sum(own, got)
        column = heads_width + starts[cut]
        rows = slice(first_row, first_row + own.shape[0])
        grad = gelu_back(pre, out_grad[rows, column : column + own.shape[1]])
        return half(gelu(pre)), grad

    forward_terms = [(after(mixed, late_owns), 0, 0, 0)]
    backward_terms = [
        (grad, 0, index * heads_width, 0) for index, grad in enumerate(head_grads)
    ]
    for cut in range(2):
        act, grad = mlp_terms(cut, 0, after(mlp_own[cut], mixed), mlp_got[cut])
        forward_terms.append((act, 1, starts[cut], 0))
        backward_terms.append((grad, 1 + cut, 0, 0))
    rows = 4 * count
    forward_early = product(
        forward_terms, [w_attn_out, w_mlp_out], [], 0, rows, jnp.bfloat16, False
    )
    backward_early = product(
        backward_terms, [in_heads, *in_mlp[:2]], [], 0, rows, jnp.bfloat16, True
    )
    forward_late, backward_late = [], []

    def add_late(part, *earlier):
        first_row = part * 2 * count
        own = after(late_owns[part], *earlier)
        act, grad = mlp_terms(2, first_row, own, late_gots[part])
        forward_late.append([(act, 0, 0, first_row)])
        backward_late.append([(grad, 0, 0, first_row)])

    late_rows = (starts[2] // MLP_CUTS[2], MLP_CUTS[2])

    def forward_term(start, size, adds, window=None):
        adds, terms = [(forward_early, start), *adds], forward_late[start // (2 * count)]
        return product(
            terms, [w_mlp_out], adds, start, size, jnp.bfloat16, False, window, late_rows
        )

    def backward_term(start, size, adds, window=None):
        adds, terms = [(backward_early, start), *adds], backward_late[start // (2 * count)]
        return product(terms, [in_mlp[2]], adds, start, size, jnp.bfloat16, True, window)

    def wider(value):
        return value.astype(jnp.float32)

    def over_x_z(term, from_core, window):
        from_x = trade(term(2 * count, count, [(from_core, 0)], window), "gx", 2)
        mine = wide_sum(term(3 * count, count, [(from_core, count)], window), from_x)
        mine = mine.reshape(2, 2, own_rows, window[1])
        pair = mine[:, 0] + wider(trade(half(mine[:, 1]), "gy", 1))
        return pair[0] + wider(trade(half(pair[1]), "gy", 2))

    def over_z_x(term, from_core, window):
        both = term(2 * count, 2 * count, [(from_core, 0)], window)
        both = both.reshape(2, 2, 2, own_rows, window[1])
        pair = wide_sum(both[:, :, 0], trade(both[:, :, 1], "gy", 1))
        ends = pair[:, 0] + wider(trade(half(pair[:, 1]), "gy", 2))
        return ends[1] + wider(trade(half(ends[0]), "gx", 2))

    add_late(0, forward_early, backward_early)
    forward_to_core = forward_term(0, 2 * count, [])
    (grad, *where), *_ = backward_late[0]
    backward_late[0] = [(after(grad, late_gots[1]), *where)]
    to_cores = forward_to_core, backward_term(0, 2 * count, [])
    add_late(1, *to_cores)

    def spread_rows(term, to_core, ways):
        width = features // len(ways)
        from_core = trade(to_core, "gx", 1)
        sums = [way(term, from_core, (place * width, width)) for place, way in enumerate(ways)]
        return jnp.concatenate(sums, axis=1)

    normed_grad = spread_rows(backward_term, to_cores[1], (over_x_z, over_z_x))
    layer_out = half(wide + spread_rows(forward_term, to_cores[0], (over_x_z, over_x_z)))
    first, second = lax.psum(
        (jnp.sum(normed_grad, axis=1), jnp.sum(normed_grad * normed, axis=1)), "gz"
    )
    grad_full = out_cotangent.astype(jnp.float32) + inverse[:, None] * (
        normed_grad - (first / D)[:, None] - normed * (second / D)[:, None]
    )
    return (layer_out, half(grad_full))


def solution(mesh):
    in_specs = (
        P(("gx", "gy"), "gz"),
        P(("gx", "gy"), "gz"),
        P(("gz", "gx"), "gy"),
        P(("gz", "gx"), "gy"),
        P(("gz", "gx"), "gy"),
        P(("gz", "gx"), "gy"),
        P(("gy", "gx"), "gz"),
        P(("gy", "gx"), "gz"),
    )
    out_specs = (P(("gx", "gy"), "gz"), P(("gx", "gy"), "gz"))
    return jax.shard_map(body, mesh=mesh, in_specs=in_specs, out_specs=out_specs, check_vma=False)
```

```python
import functools
import math

import jax
import jax.numpy as jnp
from jax import lax
from jax.experimental import pallas as pl
from jax.experimental.pallas import tpu as pltpu
from jax.sharding import PartitionSpec as P

D = 6144
HEAD_DIM = 128
IMG_TOK = 256


EPSILON = 1e-06
ROOT_HALF = 0.7071067811865476
ROOT_TWO_PI_INV = 0.3989422804014327


def attend_kernel(
    q_own, q_got, k_own, k_got, v_own, v_got, g_ref, mixed_ref, dq_ref, dk_ref, dv_ref, *, scale
):
    def total(own, got):
        return own[...].astype(jnp.float32) + got[...].astype(jnp.float32)

    def norm(values):
        center = values - jnp.mean(values, axis=-1, keepdims=True)
        spread = jnp.mean(center * center, axis=-1, keepdims=True)
        inverse = lax.rsqrt(spread + EPSILON)
        return center * inverse, inverse

    def norm_back(grad, normed, inverse):
        slope = inverse * (grad - normed * jnp.mean(grad * normed, axis=-1, keepdims=True))
        return (slope - jnp.mean(slope, axis=-1, keepdims=True)).astype(jnp.bfloat16)

    def contract(left, right, left_dim, right_dim):
        return lax.dot_general(
            left,
            right,
            (((left_dim,), (right_dim,)), ((), ())),
            preferred_element_type=jnp.float32,
        )

    def half(values):
        return values.astype(jnp.bfloat16)

    q_norm, q_inverse = norm(total(q_own, q_got))
    k_norm, k_inverse = norm(total(k_own, k_got))
    q_half, k_half = half(q_norm), half(k_norm)
    v_half = half(total(v_own, v_got))
    grad = g_ref[...]
    weights = jnp.exp(contract(q_half, k_half, 1, 1) * scale)
    probs = weights / jnp.sum(weights, axis=-1, keepdims=True)
    probs_half = half(probs)
    mixed_ref[...] = half(contract(probs_half, v_half, 1, 0))
    dv_ref[...] = half(contract(probs_half, grad, 0, 0))
    probs_grad = half(contract(grad, v_half, 1, 1)).astype(jnp.float32)
    inner = jnp.sum(probs_grad * probs, axis=-1, keepdims=True)
    score_grad = half(probs * (probs_grad - inner) * scale)
    q_grad = half(contract(score_grad, k_half, 1, 0)).astype(jnp.float32)
    k_grad = half(contract(score_grad, q_half, 0, 0)).astype(jnp.float32)
    dq_ref[...] = norm_back(q_grad, q_norm, q_inverse)
    dk_ref[...] = norm_back(k_grad, k_norm, k_inverse)


def attend(own, got, grad):
    rows, width = own.shape[0], own.shape[1] // 3
    heads = width // HEAD_DIM

    def block(part):
        return pl.BlockSpec((IMG_TOK, HEAD_DIM), lambda image, head: (image, part * heads + head))

    half = jax.ShapeDtypeStruct((rows, width), jnp.bfloat16)
    return pl.pallas_call(
        functools.partial(attend_kernel, scale=1.0 / math.sqrt(HEAD_DIM)),
        grid=(rows // IMG_TOK, heads),
        in_specs=[block(0), block(0), block(1), block(1), block(2), block(2), block(0)],
        out_specs=[block(0)] * 4,
        out_shape=[half] * 4,
        compiler_params=pltpu.CompilerParams(vmem_limit_bytes=32 * 1024 * 1024),
        cost_estimate=pl.CostEstimate(
            flops=rows * IMG_TOK * width // 8,
            bytes_accessed=rows * width // 4,
            transcendentals=0,
        ),
        name="attend",
    )(own, got, own, got, own, got, grad)


def gelu(pre):
    return pre * 0.5 * (1.0 + lax.erf(pre * ROOT_HALF))


def gelu_back(pre, grad_half):
    cdf = 0.5 * (1.0 + lax.erf(pre * ROOT_HALF))
    pdf = jnp.exp(-0.5 * pre * pre) * ROOT_TWO_PI_INV
    return (grad_half.astype(jnp.float32) * (cdf + pre * pdf)).astype(jnp.bfloat16)


def dot(left, right):
    return jnp.dot(left, right, preferred_element_type=jnp.float32)


def back_dot(left, right):
    return lax.dot_general(
        left, right, (((1,), (1,)), ((), ())), preferred_element_type=jnp.float32
    )


def half(values):
    return values.astype(jnp.bfloat16)


def wide_sum(own, got):
    return own.astype(jnp.float32) + got.astype(jnp.float32)


def trade(block, axis, bit):
    pairs = [(index, index ^ bit) for index in range(lax.axis_size(axis))]
    return lax.ppermute(block, axis, pairs)


VMEM_LIMIT = 48 * 1024 * 1024


def params():
    return pltpu.CompilerParams(vmem_limit_bytes=VMEM_LIMIT)


def cost(flops, *arrays):
    moved = sum(math.prod(array.shape) * array.dtype.itemsize for array in arrays)
    return pl.CostEstimate(flops=flops // 64, bytes_accessed=moved // 64, transcendentals=0)


def pack_kernel(*refs):
    out_ref, start = refs[-1], 0
    for ref in refs[:-1]:
        out_ref[0, :, start : start + ref.shape[1]] = ref[...]
        start += ref.shape[1]


def pack(weights, owners, start, width, tile):
    rows, columns = weights[0].shape
    first, blocks = start // tile, columns // owners // tile
    out = jax.ShapeDtypeStruct((owners, rows, len(weights) * width), weights[0].dtype)
    spec = pl.BlockSpec((rows, tile), lambda owner, n: (0, owner * blocks + first + n))
    return pl.pallas_call(
        pack_kernel,
        grid=(owners, width // tile),
        in_specs=[spec] * len(weights),
        out_specs=pl.BlockSpec((1, rows, len(weights) * tile), lambda owner, n: (owner, 0, n)),
        out_shape=out,
        compiler_params=params(),
        cost_estimate=cost(0, out, out),
        name="pack",
    )(*weights)


IMAGE_ORDER = ((1, 1), (0, 1), (1, 0), (0, 0))


def assemble_kernel(*refs):
    parts, out_ref = refs[:-1], refs[-1]
    rows = parts[0].shape[1]
    start = 0
    for x_bit, core_bit in IMAGE_ORDER:
        for part in range(len(parts) // 2):
            out_ref[start : start + rows, :] = parts[2 * part + core_bit][x_bit]
            start += rows


def assemble(parts):
    flat = [value for part in parts for value in part]
    _, rows, features = flat[0].shape
    tile = 768
    out = jax.ShapeDtypeStruct((len(flat) * 2 * rows, features), flat[0].dtype)
    return pl.pallas_call(
        assemble_kernel,
        grid=(features // tile,),
        in_specs=[pl.BlockSpec((2, rows, tile), lambda n: (0, 0, n))] * len(flat),
        out_specs=pl.BlockSpec((out.shape[0], tile), lambda n: (0, n)),
        out_shape=out,
        compiler_params=params(),
        cost_estimate=cost(0, out, out),
        name="assemble",
    )(*flat)


def cot_kernel(own_ref, other_ref, attn_ref, mlp_ref, out_ref, rows_ref):
    rows = own_ref.shape[1]
    step = pl.program_id(0)

    @pl.when(step == 0)
    def _():
        for place, (x_bit, core_bit) in enumerate(IMAGE_ORDER):
            part = other_ref if core_bit else own_ref
            rows_ref[place * rows : (place + 1) * rows, :] = part[x_bit]
        out_ref[...] = half(back_dot(rows_ref[...], attn_ref[...]))

    @pl.when(step > 0)
    def _():
        out_ref[...] = half(back_dot(rows_ref[...], mlp_ref[...]))


def cot_product(part, w_attn_out, w_mlp_out):
    own, other = part
    _, rows, features = own.shape
    tile = w_attn_out.shape[0]
    columns = tile + w_mlp_out.shape[0]
    count = len(IMAGE_ORDER) * rows
    out = jax.ShapeDtypeStruct((count, columns), jnp.bfloat16)
    whole = pl.BlockSpec(own.shape, lambda n: (0, 0, 0))
    return pl.pallas_call(
        cot_kernel,
        grid=(columns // tile,),
        in_specs=[
            whole,
            whole,
            pl.BlockSpec((tile, features), lambda n: (0, 0)),
            pl.BlockSpec((tile, features), lambda n: (jnp.maximum(n - 1, 0), 0)),
        ],
        out_specs=pl.BlockSpec((count, tile), lambda n: (0, n)),
        out_shape=out,
        scratch_shapes=[pltpu.VMEM((count, features), jnp.bfloat16)],
        compiler_params=params(),
        cost_estimate=cost(2 * count * columns * features, out, w_attn_out, w_mlp_out),
        name="cot_product",
    )(own, other, w_attn_out, w_mlp_out)


def add_kernel(*refs):
    terms, out_ref = refs[:-1], refs[-1]
    count = len(terms) // 2
    for part in range(count):
        out_ref[0, part] = half(wide_sum(terms[part][0], terms[count + part][0]))


def add_parts(owns, gots):
    images, parts = len(IMAGE_ORDER), len(owns)
    rows, columns = owns[0].shape[0] // images, owns[0].shape[1]
    out = jax.ShapeDtypeStruct((images, parts, rows, columns), jnp.bfloat16)
    terms = [value.reshape(images, rows, columns) for value in (*owns, *gots)]
    added = pl.pallas_call(
        add_kernel,
        grid=(images,),
        in_specs=[pl.BlockSpec((1, rows, columns), lambda image: (image, 0, 0))] * len(terms),
        out_specs=pl.BlockSpec((1, parts, rows, columns), lambda image: (image, 0, 0, 0)),
        out_shape=out,
        compiler_params=params(),
        cost_estimate=cost(0, out, out, out),
        name="add_parts",
    )(*terms)
    return added.reshape(images * parts * rows, columns)


def in_kernel(rows_ref, weight_ref, out_ref):
    out_ref[...] = half(dot(rows_ref[...], weight_ref[...]))


def in_product(rows, weight, half_index=None):
    count, features = rows.shape
    first = half_index or 0
    count = count if half_index is None else count // 2
    columns = weight.shape[1]
    tile = 384 if columns % 384 == 0 else 256
    out = jax.ShapeDtypeStruct((count, columns), jnp.bfloat16)
    return pl.pallas_call(
        in_kernel,
        grid=(columns // tile,),
        in_specs=[
            pl.BlockSpec((count, features), lambda n: (first, 0)),
            pl.BlockSpec((features, tile), lambda n: (0, n)),
        ],
        out_specs=pl.BlockSpec((count, tile), lambda n: (0, n)),
        out_shape=out,
        compiler_params=params(),
        cost_estimate=cost(2 * count * columns * features, rows, out, weight),
        name="in_product",
    )(rows, weight)


def product(terms, weights, adds, start, count, kind, transposed, window=None, rows=None):
    whole = weights[0].shape[0 if transposed else 1]
    first_column, columns = window or (0, whole)
    tile = 512 if columns % 512 == 0 else 384 if columns % 384 == 0 else 256
    skip = first_column // tile
    specs = [
        pl.BlockSpec(
            (count, value.shape[1]), lambda n, place=(start - row) // count: (place, 0)
        )
        for value, _, _, row in terms
    ]
    for weight in weights:
        if transposed:
            specs.append(pl.BlockSpec((tile, weight.shape[1]), lambda n: (n + skip, 0)))
        else:
            block, size = rows or (0, weight.shape[0])
            specs.append(pl.BlockSpec((size, tile), lambda n, block=block: (block, n + skip)))
    for _, first in adds:
        specs.append(
            pl.BlockSpec((count, tile), lambda n, place=first // count: (place, n + skip))
        )

    def kernel(*refs):
        weight_refs = refs[len(terms) : len(terms) + len(weights)]
        total = None
        for ref, (value, index, offset, _) in zip(refs, terms):
            summed = slice(offset, offset + value.shape[1])
            if transposed:
                part = back_dot(ref[...], weight_refs[index][:, summed])
            else:
                part = dot(ref[...], weight_refs[index][summed, :])
            total = part if total is None else total + part
        for ref in refs[len(terms) + len(weights) : -1]:
            total = total + ref[...].astype(jnp.float32)
        refs[-1][...] = total.astype(kind)

    depth = sum(value.shape[1] for value, *_ in terms)
    out = jax.ShapeDtypeStruct((count, columns), kind)
    return pl.pallas_call(
        kernel,
        grid=(columns // tile,),
        in_specs=specs,
        out_specs=pl.BlockSpec((count, tile), lambda n: (0, n)),
        out_shape=out,
        compiler_params=params(),
        cost_estimate=cost(2 * count * columns * depth, out, *weights),
        name="back_product" if transposed else "out_product",
    )(*(value for value, *_ in terms), *weights, *(add for add, _ in adds))


MLP_CUTS = (512, 256, 768)


def body(layer_input, out_cotangent, w_query, w_key, w_value, w_mlp_in, w_attn_out, w_mlp_out):
    n_gx, n_gz = lax.axis_size("gx"), lax.axis_size("gz")
    own_rows, features = layer_input.shape
    count = own_rows * lax.axis_size("gy")

    def after(value, *earlier):
        return lax.optimization_barrier((value, earlier))[0]

    def others(part):
        if n_gz == 2:
            return trade(part, "gz", 1)
        return half(lax.psum(part.astype(jnp.float32), "gz") - part.astype(jnp.float32))

    def with_x(block):
        return jnp.stack([block, trade(block, "gx", 2)])

    def over_z(pair):
        return [pair, trade(pair, "gy", 1), trade(pair, "gy", 2)]

    def with_core(part):
        return part, trade(part, "gx", 1)

    def swap(packed):
        swapped = lax.all_to_all(packed, "gx", split_axis=0, concat_axis=0, tiled=True)
        return swapped.reshape(n_gx * packed.shape[1], packed.shape[2])

    heads_width = w_query.shape[1] // n_gx
    packed_heads = pack((w_query, w_key, w_value), n_gx, 0, heads_width, heads_width)
    starts = [sum(MLP_CUTS[:cut]) for cut in range(len(MLP_CUTS))]
    packed_mlp = [
        pack((w_mlp_in,), n_gx, start, width, 256) for start, width in zip(starts, MLP_CUTS)
    ]

    cot_pair = with_x(out_cotangent)
    wide = layer_input.astype(jnp.float32)
    total, squares = lax.psum((jnp.sum(wide, axis=1), jnp.sum(wide * wide, axis=1)), "gz")
    center = total / D
    spread = squares / D - center * center
    inverse = lax.rsqrt(spread + EPSILON)
    normed = (wide - center[:, None]) * inverse[:, None]
    normed_pair = with_x(half(normed))

    cot_parts, normed_parts = over_z(cot_pair), over_z(normed_pair)
    cot_parts.append(trade(cot_parts[2], "gy", 1))
    cot_owns, cot_gots = [], []
    for place, part in enumerate(cot_parts):
        own, other = with_core(part)
        if place == 2:
            own = after(own, cot_owns[1], cot_gots[0], normed_parts[1], *packed_mlp[1:])
        if place == 3:
            own = after(own, cot_gots[1])
        cot_owns.append(cot_product((own, other), w_attn_out, w_mlp_out))
        cot_gots.append(others(cot_owns[-1]))
    normed_parts.append(trade(after(normed_parts[2], *cot_owns[1:3]), "gy", 1))
    normed_parts = [with_core(part) for part in normed_parts]
    normed_parts[0] = after(normed_parts[0], cot_owns[3], cot_gots[2])
    all_in = assemble(normed_parts)

    in_heads = swap(after(packed_heads, normed_pair, cot_owns[0]))
    early = (cot_owns[2], cot_gots[1], cot_parts[3])
    in_mlp = [swap(after(packed_mlp[0], in_heads, *early))]
    in_mlp.append(swap(after(packed_mlp[1], in_mlp[0], all_in, cot_gots[3])))
    heads_own = in_product(after(all_in, cot_gots[3]), in_heads)
    heads_got = others(heads_own)
    mlp_own = [in_product(after(all_in, heads_own, in_mlp[1]), in_mlp[0])]
    mlp_got = [others(mlp_own[0])]
    in_mlp.append(swap(after(packed_mlp[2], in_mlp[1], heads_own)))
    mlp_own.append(in_product(after(all_in, mlp_own[0]), in_mlp[1]))
    mlp_got.append(others(mlp_own[1]))

    out_grad = add_parts(after(cot_owns, mlp_own[0]), cot_gots)
    late_owns = [in_product(after(all_in, heads_got, out_grad), in_mlp[2], 0)]
    late_gots = [others(late_owns[0])]
    late_owns.append(in_product(after(all_in, late_owns[0]), in_mlp[2], 1))
    late_gots.append(others(late_owns[1]))

    mixed, *head_grads = attend(heads_own, heads_got, out_grad)

    def mlp_terms(cut, first_row, own, got):
        pre = wide_sum(own, got)
        column = heads_width + starts[cut]
        rows = slice(first_row, first_row + own.shape[0])
        grad = gelu_back(pre, out_grad[rows, column : column + own.shape[1]])
        return half(gelu(pre)), grad

    forward_terms = [(after(mixed, late_owns), 0, 0, 0)]
    backward_terms = [
        (grad, 0, index * heads_width, 0) for index, grad in enumerate(head_grads)
    ]
    for cut in range(2):
        act, grad = mlp_terms(cut, 0, after(mlp_own[cut], mixed), mlp_got[cut])
        forward_terms.append((act, 1, starts[cut], 0))
        backward_terms.append((grad, 1 + cut, 0, 0))
    rows = 4 * count
    forward_early = product(
        forward_terms, [w_attn_out, w_mlp_out], [], 0, rows, jnp.bfloat16, False
    )
    backward_early = product(
        backward_terms, [in_heads, *in_mlp[:2]], [], 0, rows, jnp.bfloat16, True
    )
    forward_late, backward_late = [], []

    def add_late(part, *earlier):
        first_row = part * 2 * count
        own = after(late_owns[part], *earlier)
        act, grad = mlp_terms(2, first_row, own, late_gots[part])
        forward_late.append([(act, 0, 0, first_row)])
        backward_late.append([(grad, 0, 0, first_row)])

    late_rows = (starts[2] // MLP_CUTS[2], MLP_CUTS[2])

    def forward_term(start, size, adds, window=None):
        adds, terms = [(forward_early, start), *adds], forward_late[start // (2 * count)]
        return product(
            terms, [w_mlp_out], adds, start, size, jnp.bfloat16, False, window, late_rows
        )

    def backward_term(start, size, adds, window=None):
        adds, terms = [(backward_early, start), *adds], backward_late[start // (2 * count)]
        return product(terms, [in_mlp[2]], adds, start, size, jnp.bfloat16, True, window)

    def wider(value):
        return value.astype(jnp.float32)

    def over_x_z(term, from_core, window):
        from_x = trade(term(2 * count, count, [(from_core, 0)], window), "gx", 2)
        mine = wide_sum(term(3 * count, count, [(from_core, count)], window), from_x)
        mine = mine.reshape(2, 2, own_rows, window[1])
        pair = mine[:, 0] + wider(trade(half(mine[:, 1]), "gy", 1))
        return pair[0] + wider(trade(half(pair[1]), "gy", 2))

    def over_z_x(term, from_core, window):
        both = term(2 * count, 2 * count, [(from_core, 0)], window)
        both = both.reshape(2, 2, 2, own_rows, window[1])
        pair = wide_sum(both[:, :, 0], trade(both[:, :, 1], "gy", 1))
        ends = pair[:, 0] + wider(trade(half(pair[:, 1]), "gy", 2))
        return ends[1] + wider(trade(half(ends[0]), "gx", 2))

    add_late(0, forward_early, backward_early)
    forward_to_core = forward_term(0, 2 * count, [])
    (grad, *where), *_ = backward_late[0]
    backward_late[0] = [(after(grad, late_gots[1]), *where)]
    to_cores = forward_to_core, backward_term(0, 2 * count, [])
    add_late(1, *to_cores)

    def spread_rows(term, to_core, ways):
        width = features // len(ways)
        from_core = trade(to_core, "gx", 1)
        sums = [way(term, from_core, (place * width, width)) for place, way in enumerate(ways)]
        return jnp.concatenate(sums, axis=1)

    normed_grad = spread_rows(backward_term, to_cores[1], (over_x_z, over_z_x))
    layer_out = half(wide + spread_rows(forward_term, to_cores[0], (over_x_z, over_x_z)))
    first, second = lax.psum(
        (jnp.sum(normed_grad, axis=1), jnp.sum(normed_grad * normed, axis=1)), "gz"
    )
    grad_full = out_cotangent.astype(jnp.float32) + inverse[:, None] * (
        normed_grad - (first / D)[:, None] - normed * (second / D)[:, None]
    )
    return (layer_out, half(grad_full))


def solution(mesh):
    in_specs = (
        P(("gx", "gy"), "gz"),
        P(("gx", "gy"), "gz"),
        P(("gz", "gx"), "gy"),
        P(("gz", "gx"), "gy"),
        P(("gz", "gx"), "gy"),
        P(("gz", "gx"), "gy"),
        P(("gy", "gx"), "gz"),
        P(("gy", "gx"), "gz"),
    )
    out_specs = (P(("gx", "gy"), "gz"), P(("gx", "gy"), "gz"))
    return jax.shard_map(body, mesh=mesh, in_specs=in_specs, out_specs=out_specs, check_vma=False)
```

```python
import functools
import math

import jax
import jax.numpy as jnp
from jax import lax
from jax.experimental import pallas as pl
from jax.experimental.pallas import tpu as pltpu
from jax.sharding import PartitionSpec as P

D = 6144
HEAD_DIM = 128
IMG_TOK = 256


EPSILON = 1e-06
ROOT_HALF = 0.7071067811865476
ROOT_TWO_PI_INV = 0.3989422804014327


def attend_kernel(
    q_own, q_got, k_own, k_got, v_own, v_got, g_ref, mixed_ref, dq_ref, dk_ref, dv_ref, *, scale
):
    def total(own, got):
        return own[...].astype(jnp.float32) + got[...].astype(jnp.float32)

    def norm(values):
        center = values - jnp.mean(values, axis=-1, keepdims=True)
        spread = jnp.mean(center * center, axis=-1, keepdims=True)
        inverse = lax.rsqrt(spread + EPSILON)
        return center * inverse, inverse

    def norm_back(grad, normed, inverse):
        slope = inverse * (grad - normed * jnp.mean(grad * normed, axis=-1, keepdims=True))
        return (slope - jnp.mean(slope, axis=-1, keepdims=True)).astype(jnp.bfloat16)

    def contract(left, right, left_dim, right_dim):
        return lax.dot_general(
            left,
            right,
            (((left_dim,), (right_dim,)), ((), ())),
            preferred_element_type=jnp.float32,
        )

    def half(values):
        return values.astype(jnp.bfloat16)

    q_norm, q_inverse = norm(total(q_own, q_got))
    k_norm, k_inverse = norm(total(k_own, k_got))
    q_half, k_half = half(q_norm), half(k_norm)
    v_half = half(total(v_own, v_got))
    grad = g_ref[...]
    weights = jnp.exp(contract(q_half, k_half, 1, 1) * scale)
    probs = weights / jnp.sum(weights, axis=-1, keepdims=True)
    probs_half = half(probs)
    mixed_ref[...] = half(contract(probs_half, v_half, 1, 0))
    dv_ref[...] = half(contract(probs_half, grad, 0, 0))
    probs_grad = half(contract(grad, v_half, 1, 1)).astype(jnp.float32)
    inner = jnp.sum(probs_grad * probs, axis=-1, keepdims=True)
    score_grad = half(probs * (probs_grad - inner) * scale)
    q_grad = half(contract(score_grad, k_half, 1, 0)).astype(jnp.float32)
    k_grad = half(contract(score_grad, q_half, 0, 0)).astype(jnp.float32)
    dq_ref[...] = norm_back(q_grad, q_norm, q_inverse)
    dk_ref[...] = norm_back(k_grad, k_norm, k_inverse)


def attend(own, got, grad):
    rows, width = own.shape[0], own.shape[1] // 3
    heads = width // HEAD_DIM

    def block(part):
        return pl.BlockSpec((IMG_TOK, HEAD_DIM), lambda image, head: (image, part * heads + head))

    half = jax.ShapeDtypeStruct((rows, width), jnp.bfloat16)
    return pl.pallas_call(
        functools.partial(attend_kernel, scale=1.0 / math.sqrt(HEAD_DIM)),
        grid=(rows // IMG_TOK, heads),
        in_specs=[block(0), block(0), block(1), block(1), block(2), block(2), block(0)],
        out_specs=[block(0)] * 4,
        out_shape=[half] * 4,
        compiler_params=pltpu.CompilerParams(vmem_limit_bytes=32 * 1024 * 1024),
        cost_estimate=pl.CostEstimate(
            flops=rows * IMG_TOK * width // 8,
            bytes_accessed=rows * width // 4,
            transcendentals=0,
        ),
        name="attend",
    )(own, got, own, got, own, got, grad)


def gelu(pre):
    return pre * 0.5 * (1.0 + lax.erf(pre * ROOT_HALF))


def gelu_back(pre, grad_half):
    cdf = 0.5 * (1.0 + lax.erf(pre * ROOT_HALF))
    pdf = jnp.exp(-0.5 * pre * pre) * ROOT_TWO_PI_INV
    return (grad_half.astype(jnp.float32) * (cdf + pre * pdf)).astype(jnp.bfloat16)


def dot(left, right):
    return jnp.dot(left, right, preferred_element_type=jnp.float32)


def back_dot(left, right):
    return lax.dot_general(
        left, right, (((1,), (1,)), ((), ())), preferred_element_type=jnp.float32
    )


def half(values):
    return values.astype(jnp.bfloat16)


def wide_sum(own, got):
    return own.astype(jnp.float32) + got.astype(jnp.float32)


def trade(block, axis, bit):
    pairs = [(index, index ^ bit) for index in range(lax.axis_size(axis))]
    return lax.ppermute(block, axis, pairs)


VMEM_LIMIT = 48 * 1024 * 1024


def params():
    return pltpu.CompilerParams(vmem_limit_bytes=VMEM_LIMIT)


def cost(flops, *arrays):
    moved = sum(math.prod(array.shape) * array.dtype.itemsize for array in arrays)
    return pl.CostEstimate(flops=flops // 64, bytes_accessed=moved // 64, transcendentals=0)


def pack_kernel(*refs):
    out_ref, start = refs[-1], 0
    for ref in refs[:-1]:
        out_ref[0, :, start : start + ref.shape[1]] = ref[...]
        start += ref.shape[1]


def pack(weights, owners, start, width, tile):
    rows, columns = weights[0].shape
    first, blocks = start // tile, columns // owners // tile
    out = jax.ShapeDtypeStruct((owners, rows, len(weights) * width), weights[0].dtype)
    spec = pl.BlockSpec((rows, tile), lambda owner, n: (0, owner * blocks + first + n))
    return pl.pallas_call(
        pack_kernel,
        grid=(owners, width // tile),
        in_specs=[spec] * len(weights),
        out_specs=pl.BlockSpec((1, rows, len(weights) * tile), lambda owner, n: (owner, 0, n)),
        out_shape=out,
        compiler_params=params(),
        cost_estimate=cost(0, out, out),
        name="pack",
    )(*weights)


IMAGE_ORDER = ((1, 1), (0, 1), (1, 0), (0, 0))


def assemble_kernel(*refs):
    parts, out_ref = refs[:-1], refs[-1]
    rows = parts[0].shape[1]
    start = 0
    for x_bit, core_bit in IMAGE_ORDER:
        for part in range(len(parts) // 2):
            out_ref[start : start + rows, :] = parts[2 * part + core_bit][x_bit]
            start += rows


def assemble(parts):
    flat = [value for part in parts for value in part]
    _, rows, features = flat[0].shape
    tile = 768
    out = jax.ShapeDtypeStruct((len(flat) * 2 * rows, features), flat[0].dtype)
    return pl.pallas_call(
        assemble_kernel,
        grid=(features // tile,),
        in_specs=[pl.BlockSpec((2, rows, tile), lambda n: (0, 0, n))] * len(flat),
        out_specs=pl.BlockSpec((out.shape[0], tile), lambda n: (0, n)),
        out_shape=out,
        compiler_params=params(),
        cost_estimate=cost(0, out, out),
        name="assemble",
    )(*flat)


def cot_kernel(own_ref, other_ref, attn_ref, mlp_ref, out_ref, rows_ref):
    rows = own_ref.shape[1]
    step = pl.program_id(0)

    @pl.when(step == 0)
    def _():
        for place, (x_bit, core_bit) in enumerate(IMAGE_ORDER):
            part = other_ref if core_bit else own_ref
            rows_ref[place * rows : (place + 1) * rows, :] = part[x_bit]
        out_ref[...] = half(back_dot(rows_ref[...], attn_ref[...]))

    @pl.when(step > 0)
    def _():
        out_ref[...] = half(back_dot(rows_ref[...], mlp_ref[...]))


def cot_product(part, w_attn_out, w_mlp_out):
    own, other = part
    _, rows, features = own.shape
    tile = w_attn_out.shape[0]
    columns = tile + w_mlp_out.shape[0]
    count = len(IMAGE_ORDER) * rows
    out = jax.ShapeDtypeStruct((count, columns), jnp.bfloat16)
    whole = pl.BlockSpec(own.shape, lambda n: (0, 0, 0))
    return pl.pallas_call(
        cot_kernel,
        grid=(columns // tile,),
        in_specs=[
            whole,
            whole,
            pl.BlockSpec((tile, features), lambda n: (0, 0)),
            pl.BlockSpec((tile, features), lambda n: (jnp.maximum(n - 1, 0), 0)),
        ],
        out_specs=pl.BlockSpec((count, tile), lambda n: (0, n)),
        out_shape=out,
        scratch_shapes=[pltpu.VMEM((count, features), jnp.bfloat16)],
        compiler_params=params(),
        cost_estimate=cost(2 * count * columns * features, out, w_attn_out, w_mlp_out),
        name="cot_product",
    )(own, other, w_attn_out, w_mlp_out)


def add_kernel(*refs):
    terms, out_ref = refs[:-1], refs[-1]
    count = len(terms) // 2
    for part in range(count):
        out_ref[0, part] = half(wide_sum(terms[part][0], terms[count + part][0]))


def add_parts(owns, gots):
    images, parts = len(IMAGE_ORDER), len(owns)
    rows, columns = owns[0].shape[0] // images, owns[0].shape[1]
    out = jax.ShapeDtypeStruct((images, parts, rows, columns), jnp.bfloat16)
    terms = [value.reshape(images, rows, columns) for value in (*owns, *gots)]
    added = pl.pallas_call(
        add_kernel,
        grid=(images,),
        in_specs=[pl.BlockSpec((1, rows, columns), lambda image: (image, 0, 0))] * len(terms),
        out_specs=pl.BlockSpec((1, parts, rows, columns), lambda image: (image, 0, 0, 0)),
        out_shape=out,
        compiler_params=params(),
        cost_estimate=cost(0, out, out, out),
        name="add_parts",
    )(*terms)
    return added.reshape(images * parts * rows, columns)


def in_kernel(rows_ref, weight_ref, out_ref):
    out_ref[...] = half(dot(rows_ref[...], weight_ref[...]))


def in_product(rows, weight, half_index=None):
    count, features = rows.shape
    first = half_index or 0
    count = count if half_index is None else count // 2
    columns = weight.shape[1]
    tile = 384 if columns % 384 == 0 else 256
    out = jax.ShapeDtypeStruct((count, columns), jnp.bfloat16)
    return pl.pallas_call(
        in_kernel,
        grid=(columns // tile,),
        in_specs=[
            pl.BlockSpec((count, features), lambda n: (first, 0)),
            pl.BlockSpec((features, tile), lambda n: (0, n)),
        ],
        out_specs=pl.BlockSpec((count, tile), lambda n: (0, n)),
        out_shape=out,
        compiler_params=params(),
        cost_estimate=cost(2 * count * columns * features, rows, out, weight),
        name="in_product",
    )(rows, weight)


def product(terms, weights, adds, start, count, kind, transposed, window=None, rows=None):
    whole = weights[0].shape[0 if transposed else 1]
    first_column, columns = window or (0, whole)
    tile = 512 if columns % 512 == 0 else 384 if columns % 384 == 0 else 256
    skip = first_column // tile
    specs = [
        pl.BlockSpec(
            (count, value.shape[1]), lambda n, place=(start - row) // count: (place, 0)
        )
        for value, _, _, row in terms
    ]
    for weight in weights:
        if transposed:
            specs.append(pl.BlockSpec((tile, weight.shape[1]), lambda n: (n + skip, 0)))
        else:
            block, size = rows or (0, weight.shape[0])
            specs.append(pl.BlockSpec((size, tile), lambda n, block=block: (block, n + skip)))
    for _, first in adds:
        specs.append(
            pl.BlockSpec((count, tile), lambda n, place=first // count: (place, n + skip))
        )

    def kernel(*refs):
        weight_refs = refs[len(terms) : len(terms) + len(weights)]
        total = None
        for ref, (value, index, offset, _) in zip(refs, terms):
            summed = slice(offset, offset + value.shape[1])
            if transposed:
                part = back_dot(ref[...], weight_refs[index][:, summed])
            else:
                part = dot(ref[...], weight_refs[index][summed, :])
            total = part if total is None else total + part
        for ref in refs[len(terms) + len(weights) : -1]:
            total = total + ref[...].astype(jnp.float32)
        refs[-1][...] = total.astype(kind)

    depth = sum(value.shape[1] for value, *_ in terms)
    out = jax.ShapeDtypeStruct((count, columns), kind)
    return pl.pallas_call(
        kernel,
        grid=(columns // tile,),
        in_specs=specs,
        out_specs=pl.BlockSpec((count, tile), lambda n: (0, n)),
        out_shape=out,
        compiler_params=params(),
        cost_estimate=cost(2 * count * columns * depth, out, *weights),
        name="back_product" if transposed else "out_product",
    )(*(value for value, *_ in terms), *weights, *(add for add, _ in adds))


MLP_CUTS = (512, 256, 768)


def body(layer_input, out_cotangent, w_query, w_key, w_value, w_mlp_in, w_attn_out, w_mlp_out):
    n_gx, n_gz = lax.axis_size("gx"), lax.axis_size("gz")
    own_rows, features = layer_input.shape
    count = own_rows * lax.axis_size("gy")

    def after(value, *earlier):
        return lax.optimization_barrier((value, earlier))[0]

    def others(part):
        if n_gz == 2:
            return trade(part, "gz", 1)
        return half(lax.psum(part.astype(jnp.float32), "gz") - part.astype(jnp.float32))

    def with_x(block):
        return jnp.stack([block, trade(block, "gx", 2)])

    def over_z(pair):
        return [pair, trade(pair, "gy", 1), trade(pair, "gy", 2)]

    def with_core(part):
        return part, trade(part, "gx", 1)

    def swap(packed):
        swapped = lax.all_to_all(packed, "gx", split_axis=0, concat_axis=0, tiled=True)
        return swapped.reshape(n_gx * packed.shape[1], packed.shape[2])

    heads_width = w_query.shape[1] // n_gx
    packed_heads = pack((w_query, w_key, w_value), n_gx, 0, heads_width, heads_width)
    starts = [sum(MLP_CUTS[:cut]) for cut in range(len(MLP_CUTS))]
    packed_mlp = [
        pack((w_mlp_in,), n_gx, start, width, 256) for start, width in zip(starts[:2], MLP_CUTS)
    ]

    cot_pair = with_x(out_cotangent)
    wide = layer_input.astype(jnp.float32)
    total, squares = lax.psum((jnp.sum(wide, axis=1), jnp.sum(wide * wide, axis=1)), "gz")
    center = total / D
    spread = squares / D - center * center
    inverse = lax.rsqrt(spread + EPSILON)
    normed = (wide - center[:, None]) * inverse[:, None]
    normed_pair = with_x(half(normed))

    cot_parts, normed_parts = over_z(cot_pair), over_z(normed_pair)
    cot_parts.append(trade(cot_parts[2], "gy", 1))
    cot_owns, cot_gots = [], []
    for place, part in enumerate(cot_parts):
        own, other = with_core(part)
        if place == 2:
            own = after(own, cot_owns[1], cot_gots[0], normed_parts[1])
        if place == 3:
            own = after(own, cot_gots[1])
        cot_owns.append(cot_product((own, other), w_attn_out, w_mlp_out))
        cot_gots.append(others(cot_owns[-1]))
    normed_parts.append(trade(after(normed_parts[2], *cot_owns[1:3]), "gy", 1))
    normed_parts = [with_core(part) for part in normed_parts]
    normed_parts[0] = after(normed_parts[0], cot_owns[3], cot_gots[2])
    all_in = assemble(normed_parts)

    in_heads = swap(after(packed_heads, normed_pair, cot_owns[0]))
    early = (cot_owns[2], cot_gots[1], cot_parts[3])
    in_mlp = [swap(after(packed_mlp[0], in_heads, *early))]
    in_mlp.append(swap(after(packed_mlp[1], in_mlp[0], all_in, cot_gots[3])))
    heads_own = in_product(after(all_in, cot_gots[3]), in_heads)
    heads_got = others(heads_own)
    last_weight = after(w_mlp_in, heads_own)
    packed_last = pack((last_weight,), n_gx, starts[2], MLP_CUTS[2], 256)
    mlp_own = [in_product(after(all_in, heads_own, packed_last, in_mlp[1]), in_mlp[0])]
    mlp_got = [others(mlp_own[0])]
    in_mlp.append(swap(after(packed_last, in_mlp[1])))
    mlp_own.append(in_product(after(all_in, mlp_own[0]), in_mlp[1]))
    mlp_got.append(others(mlp_own[1]))

    out_grad = add_parts(after(cot_owns, mlp_own[0]), cot_gots)
    late_owns = [in_product(after(all_in, heads_got, out_grad), in_mlp[2], 0)]
    late_gots = [others(late_owns[0])]
    late_owns.append(in_product(after(all_in, late_owns[0]), in_mlp[2], 1))
    late_gots.append(others(late_owns[1]))

    mixed, *head_grads = attend(heads_own, heads_got, out_grad)

    def mlp_terms(cut, first_row, own, got):
        pre = wide_sum(own, got)
        column = heads_width + starts[cut]
        rows = slice(first_row, first_row + own.shape[0])
        grad = gelu_back(pre, out_grad[rows, column : column + own.shape[1]])
        return half(gelu(pre)), grad

    forward_terms = [(after(mixed, late_owns), 0, 0, 0)]
    backward_terms = [
        (grad, 0, index * heads_width, 0) for index, grad in enumerate(head_grads)
    ]
    for cut in range(2):
        act, grad = mlp_terms(cut, 0, after(mlp_own[cut], mixed), mlp_got[cut])
        forward_terms.append((act, 1, starts[cut], 0))
        backward_terms.append((grad, 1 + cut, 0, 0))
    rows = 4 * count
    forward_early = product(
        forward_terms, [w_attn_out, w_mlp_out], [], 0, rows, jnp.bfloat16, False
    )
    backward_early = product(
        backward_terms, [in_heads, *in_mlp[:2]], [], 0, rows, jnp.bfloat16, True
    )
    forward_late, backward_late = [], []

    def add_late(part, *earlier):
        first_row = part * 2 * count
        own = after(late_owns[part], *earlier)
        act, grad = mlp_terms(2, first_row, own, late_gots[part])
        forward_late.append([(act, 0, 0, first_row)])
        backward_late.append([(grad, 0, 0, first_row)])

    late_rows = (starts[2] // MLP_CUTS[2], MLP_CUTS[2])

    def forward_term(start, size, adds, window=None):
        adds, terms = [(forward_early, start), *adds], forward_late[start // (2 * count)]
        return product(
            terms, [w_mlp_out], adds, start, size, jnp.bfloat16, False, window, late_rows
        )

    def backward_term(start, size, adds, window=None):
        adds, terms = [(backward_early, start), *adds], backward_late[start // (2 * count)]
        return product(terms, [in_mlp[2]], adds, start, size, jnp.bfloat16, True, window)

    def wider(value):
        return value.astype(jnp.float32)

    def over_x_z(term, from_core, window):
        from_x = trade(term(2 * count, count, [(from_core, 0)], window), "gx", 2)
        mine = wide_sum(term(3 * count, count, [(from_core, count)], window), from_x)
        mine = mine.reshape(2, 2, own_rows, window[1])
        pair = mine[:, 0] + wider(trade(half(mine[:, 1]), "gy", 1))
        return pair[0] + wider(trade(half(pair[1]), "gy", 2))

    def over_z_x(term, from_core, window):
        both = term(2 * count, 2 * count, [(from_core, 0)], window)
        both = both.reshape(2, 2, 2, own_rows, window[1])
        pair = wide_sum(both[:, :, 0], trade(both[:, :, 1], "gy", 1))
        ends = pair[:, 0] + wider(trade(half(pair[:, 1]), "gy", 2))
        return ends[1] + wider(trade(half(ends[0]), "gx", 2))

    add_late(0, forward_early, backward_early)
    forward_to_core = forward_term(0, 2 * count, [])
    (grad, *where), *_ = backward_late[0]
    backward_late[0] = [(after(grad, late_gots[1]), *where)]
    to_cores = forward_to_core, backward_term(0, 2 * count, [])
    add_late(1, *to_cores)

    def spread_rows(term, to_core, ways):
        width = features // len(ways)
        from_core = trade(to_core, "gx", 1)
        sums = [way(term, from_core, (place * width, width)) for place, way in enumerate(ways)]
        return jnp.concatenate(sums, axis=1)

    normed_grad = spread_rows(backward_term, to_cores[1], (over_x_z, over_z_x))
    layer_out = half(wide + spread_rows(forward_term, to_cores[0], (over_x_z, over_x_z)))
    first, second = lax.psum(
        (jnp.sum(normed_grad, axis=1), jnp.sum(normed_grad * normed, axis=1)), "gz"
    )
    grad_full = out_cotangent.astype(jnp.float32) + inverse[:, None] * (
        normed_grad - (first / D)[:, None] - normed * (second / D)[:, None]
    )
    return (layer_out, half(grad_full))


def solution(mesh):
    in_specs = (
        P(("gx", "gy"), "gz"),
        P(("gx", "gy"), "gz"),
        P(("gz", "gx"), "gy"),
        P(("gz", "gx"), "gy"),
        P(("gz", "gx"), "gy"),
        P(("gz", "gx"), "gy"),
        P(("gy", "gx"), "gz"),
        P(("gy", "gx"), "gz"),
    )
    out_specs = (P(("gx", "gy"), "gz"), P(("gx", "gy"), "gz"))
    return jax.shard_map(body, mesh=mesh, in_specs=in_specs, out_specs=out_specs, check_vma=False)
```
